32 devices in a mesh: px: 8 (over z, x), py: 4 (over y, core).
Axes of the slice: x: 2, y: 2, z: 4, core: 2. Of those that a mesh axis runs over, the one named last changes fastest.
Arguments:
- coords: float32 [3, 65536], P(None, ('px', 'py')), may hold values from -6 to 6
- displacement: float32 [3, 65536], P(None, ('px', 'py')), may hold values from -3 to 3
- velocity: float32 [3, 65536], P(None, ('px', 'py')), may hold values from -6 to 6
- inv_mass: float32 [65536], P(('px', 'py')), may hold values from 0.5 to 2
- ext_force: float32 [3, 65536], P(None, ('px', 'py')), may hold values from -6 to 6
- thickness: float32 [65536], P(('px', 'py')), may hold values from 0.5 to 2
- stiffness: float32 [12, 12], replicated, may hold values from -12 to 12
- elem_nodes: int32 [4, 65536], P(None, ('px', 'py')), may hold values from 0 to 4095
- block_class: int32 [512], P(('px', 'py')), may hold values from 0 to 1
- halo_lists: int32 [4, 16384], P(None, ('px', 'py')), may hold values from 0 to 2047
- contact_nodes: int32 [65536], P(('px', 'py')), may hold values from 0 to 2047
- contact_bucket: int32 [65536, 1], P(('px', 'py')), may hold values from 0 to 31; in each aligned block of 2048 rows (0 to 2047, 2048 to 4095, ...) at most 128 rows name the same one
- tile_pairs: int32 [2, 512], P(None, ('px', 'py')), may hold values from 0 to 31
Outputs:
- disp_out: float32 [3, 65536], P(None, ('px', 'py'))
- vel_out: float32 [3, 65536], P(None, ('px', 'py'))
The draws below stay inside these ranges and needn't reach their ends.
Inputs may be any that keep to these rules, and one draw needn't show every extreme that they name: `elem_nodes`: indices into the device's extended list: 2048 own nodes, then four blocks of 512 received nodes. `halo_lists`: row 0 is sent to the neighbour one lower along px, row 1 one higher along px, row 2 one lower along py, row 3 one higher along py; entries are own node indices. `block_class`: class of each block of 128 consecutive elements. `contact_nodes`: own node indices of the device. `contact_bucket`: among the 2048 rows of one device no bucket is named more than 128 times, and in every draw some device names some bucket exactly 128 times. `tile_pairs`: tile numbers within the device's own bucket.
All inputs are finite; a program needn't handle non-finite values.
Results may differ from the reference program's by a relative error of at most 0.0003.
Values sent between devices are 32-bit elements; how exact they have to be, the bound alone decides.
No kernel may reach another device: no remote copies, remote signals or barrier semaphores. Data moves between devices by JAX's collectives and lax.ppermute only.
A program may use at most 64 MiB of HBM per device.

```python
import math
import jax
import jax.numpy as jnp
import numpy as np
from jax import lax

ELEM_DEV = 2048
HALO = 512
CN_DEV = 2048
PAIRS = 16
TILE = 128
EBLK = 128
STEPS = 2
SUBS = 2
NODE_DEV = 2048
CAP = 128
TILES = 32
NODES = 65536
ELEMS = 65536
N_PX = 8
N_PY = 4


def place_ends(values, stream_key, smallest, top_value):
    shape = values.shape
    spot = [jax.random.randint(jax.random.fold_in(stream_key, axis), (), 0, shape[axis]) for axis in range(len(shape))]
    values = values.at[tuple(spot)].set(smallest)
    longest = shape.index(max(shape))
    spot[longest] = (spot[longest] + 1) % shape[longest]
    return values.at[tuple(spot)].set(top_value)


def block_scale(rng, shape, pieces, low, high):
    loudness, own = 1.0, jax.random.fold_in(rng, 6)
    for dim, shards_of in pieces:
        steps = jnp.exp(jax.random.uniform(jax.random.fold_in(own, dim), (shards_of,), jnp.float32, low / len(pieces), high / len(pieces)))
        loudness = loudness * jnp.repeat(steps, shape[dim] // shards_of).reshape([-1 if axis == dim else 1 for axis in range(len(shape))])
    return loudness


def deal_out(key, own, number, rows, number_of, top, most, skew):
    ranking = jax.random.permutation(key, number_of)
    crowded, ordinary = shares(number_of, rows * top, most, skew, True), shares(number_of, rows * top, most, skew, False)
    places = jnp.arange(number_of)

    def named(sizes, offset_by):
        used = int((sizes > 0).sum())
        fixed = max(1, used // 4)
        moved = fixed + (places - fixed + offset_by * (used - fixed)) % max(1, number_of - fixed)
        return jnp.zeros((number_of,), jnp.int32).at[ranking[jnp.where(places < fixed, places, moved)]].set(jnp.asarray(sizes, jnp.int32))

    sizes = jnp.where(number % 4 == 0, named(crowded, number // 4), named(ordinary, number - number // 4 - 1))
    mixed = jax.random.permutation(jax.random.fold_in(own, 3), number_of)
    donor, sink = mixed[0:number_of // 2 * 2:2], mixed[1:number_of // 2 * 2:2]
    margin = jnp.minimum(sizes[donor] - 1, most - sizes[sink]) // 2
    margin = jnp.where((donor == ranking[0]) | (sink == ranking[0]) | (sizes[sink] == 0), 0, jnp.maximum(margin, 0))
    moved = jax.random.randint(jax.random.fold_in(own, 4), (number_of // 2,), 0, 1 << 20) % (margin + 1)
    sizes = sizes.at[donor].add(-moved).at[sink].add(moved)
    items = jnp.searchsorted(jnp.cumsum(sizes), jnp.arange(rows * top), side="right").astype(jnp.int32)
    table = items.reshape(top, rows).T
    table = table[jax.random.permutation(jax.random.fold_in(own, 1), rows)]
    offset_by = jax.random.randint(jax.random.fold_in(own, 2), (rows, 1), 0, top)
    return jnp.take_along_axis(table, (jnp.arange(top)[None, :] + offset_by) % top, axis=1)


def shares(amount, total, bound, skew, full):
    portions = [(1 << 20) // math.isqrt(grade ** skew) + 1 for grade in range(1, amount + 1)]
    largest = bound if full else min(bound, max(-(-total // amount), total * portions[0] // sum(portions)))
    least = 1 if total - largest >= amount - 1 else 0
    holding, surplus = [largest] + [least] * (amount - 1), total - largest - least * (amount - 1)
    while surplus > 0:
        candidates = [i for i in range(1, amount) if holding[i] < largest] or [i for i in range(1, amount) if holding[i] < bound]
        pool, left = sum([portions[i] for i in candidates]), surplus
        for i in candidates:
            more = min(bound - holding[i], max(1, left * portions[i] // pool), surplus)
            holding[i] = holding[i] + more
            surplus = surplus - more
    return np.array(holding)


def gaussian(own_key, extent, scale, most, shards=(), kind=jnp.bfloat16):
    drawn = scale * jax.random.normal(own_key, extent, jnp.float32)
    if shards:
        drawn = drawn * block_scale(own_key, extent, shards, -0.22, 0.18)
    return jnp.clip(drawn, -most, most).astype(kind)


def setup_inputs(seed: int = 0) -> dict:
    key_list = jax.random.split(jax.random.key(seed), 14)
    coords = gaussian(key_list[0], (3, NODES), 1.0, 6.0, ((1, 32),), jnp.float32)
    displacement = gaussian(key_list[1], (3, NODES), 0.5, 3.0, ((1, 32),), jnp.float32)
    velocity = gaussian(key_list[2], (3, NODES), 1.0, 6.0, ((1, 32),), jnp.float32)
    inv_mass = jnp.clip(jnp.exp(math.log(2.0) - 1.3862944 * jax.random.uniform(key_list[3], (NODES,), jnp.float32) ** block_scale(key_list[3], (NODES,), ((0, 32),), -0.2, 0.2)), 0.5, 2.0)
    ext_force = gaussian(key_list[4], (3, NODES), 1.0, 6.0, ((1, 32),), jnp.float32)
    thickness = jnp.clip(jnp.exp(math.log(2.0) - 1.3862944 * jax.random.uniform(key_list[5], (ELEMS,), jnp.float32) ** block_scale(key_list[5], (ELEMS,), ((0, 32),), -0.2, 0.2)), 0.5, 2.0)
    stiffness = gaussian(key_list[6], (12, 12), 3.0, 12.0, (), jnp.float32)
    elem_nodes = place_ends(jax.random.randint(key_list[7], (4, ELEMS), 0, NODE_DEV + 4 * HALO), jax.random.fold_in(key_list[7], 1), 0, (NODE_DEV + 4 * HALO) - 1).astype(jnp.int32)
    block_class = place_ends(jax.random.randint(key_list[8], (ELEMS // EBLK,), 0, 2), jax.random.fold_in(key_list[8], 1), 0, 1).astype(jnp.int32)
    halo_lists = place_ends(jax.random.randint(key_list[9], (4, HALO * N_PX * N_PY), 0, NODE_DEV), jax.random.fold_in(key_list[9], 1), 0, NODE_DEV - 1).astype(jnp.int32)
    contact_nodes = place_ends(jax.random.randint(key_list[10], (CN_DEV * N_PX * N_PY,), 0, NODE_DEV), jax.random.fold_in(key_list[10], 1), 0, NODE_DEV - 1).astype(jnp.int32)
    contact_bucket_keys = jax.random.split(jax.random.fold_in(key_list[11], 1), (CN_DEV * N_PX * N_PY) // CN_DEV)
    contact_bucket_turns = jax.random.permutation(jax.random.fold_in(key_list[11], 3), (CN_DEV * N_PX * N_PY) // CN_DEV)
    contact_bucket = jax.vmap(lambda own, number: deal_out(jax.random.fold_in(key_list[11], 2), own, number, CN_DEV, N_PX * N_PY, 1, CAP, 2))(contact_bucket_keys, contact_bucket_turns).reshape((CN_DEV * N_PX * N_PY, 1))
    tile_pairs = place_ends(jax.random.randint(key_list[12], (2, PAIRS * N_PX * N_PY), 0, TILES), jax.random.fold_in(key_list[12], 1), 0, TILES - 1).astype(jnp.int32)
    return dict(coords=coords, displacement=displacement, velocity=velocity, inv_mass=inv_mass, ext_force=ext_force, thickness=thickness, stiffness=stiffness, elem_nodes=elem_nodes, block_class=block_class, halo_lists=halo_lists, contact_nodes=contact_nodes, contact_bucket=contact_bucket, tile_pairs=tile_pairs)


FAR = 1.0e4
DT = 0.05
PENALTY = 0.5
REACH = 4.0


def split_dev(array_in, width):
    lead = array_in.shape[:-1]
    blocks = array_in.reshape(lead + (N_PX * N_PY, width))
    return jnp.moveaxis(blocks, -2, 0)


def join_dev(blocks):
    moved = jnp.moveaxis(blocks, 0, -2)
    return moved.reshape(moved.shape[:-2] + (moved.shape[-2] * moved.shape[-1],))


def grid_shift(blocks, axis_no, offset):
    length = blocks.shape[axis_no]
    zero_part = jnp.zeros_like(lax.slice_in_dim(blocks, 0, 1, axis=axis_no))
    if offset == 1:
        return jnp.concatenate([zero_part, lax.slice_in_dim(blocks, 0, length - 1, axis=axis_no)], axis_no)
    return jnp.concatenate([lax.slice_in_dim(blocks, 1, length, axis=axis_no), zero_part], axis_no)


def halo_extend(values, lists):
    picked = jax.vmap(lambda field_in, rows_in: field_in[:, rows_in])(values, lists)
    grid = picked.reshape(N_PX, N_PY, 3, 4, HALO)
    from_low_x = grid_shift(grid[:, :, :, 1], 0, 1)
    from_high_x = grid_shift(grid[:, :, :, 0], 0, -1)
    from_low_y = grid_shift(grid[:, :, :, 3], 1, 1)
    from_high_y = grid_shift(grid[:, :, :, 2], 1, -1)
    parts = [blk.reshape(N_PX * N_PY, 3, HALO) for blk in (from_low_x, from_high_x, from_low_y, from_high_y)]
    return jnp.concatenate([values] + parts, axis=2)


def halo_return(force_ext, lists):
    owned_count = NODE_DEV
    blocks = [force_ext[:, :, owned_count + number * HALO: owned_count + (number + 1) * HALO].reshape(N_PX, N_PY, 3, HALO) for number in range(4)]
    back_zero = grid_shift(blocks[1], 0, 1)
    back_one = grid_shift(blocks[0], 0, -1)
    back_two = grid_shift(blocks[3], 1, 1)
    back_three = grid_shift(blocks[2], 1, -1)
    returned = jnp.stack([back_zero, back_one, back_two, back_three], axis=3).reshape(N_PX * N_PY, 3, 4 * HALO)

    def add_back(own_part, ret_part, rows_in):
        return own_part + jnp.zeros((3, owned_count), jnp.float32).at[:, rows_in.reshape(-1)].add(ret_part)

    return jax.vmap(add_back)(force_ext[:, :, :owned_count], returned, lists)


def element_forces(ext_values, elem_nodes, thickness, stiffness):
    corners = ext_values[:, elem_nodes]
    local = corners.reshape(12, elem_nodes.shape[1])
    return thickness[None, :] * jnp.dot(stiffness, local, precision=lax.Precision.HIGHEST)


def assemble(forces, elem_nodes, extended):
    return jnp.zeros((3, extended), jnp.float32).at[:, elem_nodes.reshape(-1)].add(forces.reshape(3, -1))


def contact_slots(bucket, devices, capacity):
    onehot = (bucket[:, None] == jnp.arange(devices, dtype=jnp.int32)[None, :]).astype(jnp.int32)
    before = jnp.cumsum(onehot, axis=0) - onehot
    ranks = jnp.sum(before * onehot, axis=1).astype(jnp.int32)
    return (bucket * capacity + ranks).astype(jnp.int32)


def tile_forces(arrived, tile_pairs):
    tiles = arrived.reshape(3, -1, TILE)

    def one_pair(total, pair):
        first = pair[0]
        second = pair[1]
        pos_a = lax.dynamic_index_in_dim(tiles, first, 1, keepdims=False)
        pos_b = lax.dynamic_index_in_dim(tiles, second, 1, keepdims=False)
        gap = pos_a[:, :, None] - pos_b[:, None, :]
        dist = jnp.sum(gap * gap, axis=0)
        weight = PENALTY * jnp.exp(-dist / REACH)
        push = jnp.sum(weight[None, :, :] * gap, axis=2)
        current = lax.dynamic_index_in_dim(total, first, 1, keepdims=False)
        return lax.dynamic_update_index_in_dim(total, current + push, first, 1), None

    start = jnp.zeros(tiles.shape, jnp.float32)
    total, unused = lax.scan(one_pair, start, tile_pairs.T)
    return total.reshape(3, -1)


def relayout(blocks, devices, capacity):
    grid = blocks.reshape(devices, 3, devices, capacity)
    return jnp.transpose(grid, (2, 1, 0, 3)).reshape(devices, 3, devices * capacity)


def reference(coords, displacement, velocity, inv_mass, ext_force, thickness, stiffness, elem_nodes, block_class, halo_lists, contact_nodes, contact_bucket, tile_pairs):
    devices = N_PX * N_PY
    capacity = 2 * CN_DEV // devices
    width = devices * capacity
    extended = NODE_DEV + 4 * HALO
    base = split_dev(coords, NODE_DEV)
    disp = split_dev(displacement, NODE_DEV)
    vel = split_dev(velocity, NODE_DEV)
    inv_m = split_dev(inv_mass, NODE_DEV)
    f_ext = split_dev(ext_force, NODE_DEV)
    thick = split_dev(thickness, ELEM_DEV)
    enodes = split_dev(elem_nodes, ELEM_DEV)
    slow_elems = jnp.repeat(split_dev(block_class, ELEM_DEV // EBLK), EBLK, axis=1) == 1
    lists = split_dev(halo_lists, HALO)
    cnodes = split_dev(contact_nodes, CN_DEV)
    buckets = contact_bucket[:, 0].reshape(devices, CN_DEV)
    pairs = split_dev(tile_pairs, PAIRS)
    slots = jax.vmap(lambda bucket_row: contact_slots(bucket_row, devices, capacity))(buckets)

    def fill_slots(points, node_ids, slot_ids):
        return jnp.full((3, width), FAR, jnp.float32).at[:, slot_ids].set(points[:, node_ids])

    def take_back(force_in, node_ids, slot_ids):
        return jnp.zeros((3, NODE_DEV), jnp.float32).at[:, node_ids].add(force_in[:, slot_ids])

    for step_no in range(STEPS):
        outgoing = jax.vmap(fill_slots)(base + disp, cnodes, slots)
        arrived = relayout(outgoing, devices, capacity)
        pushes = jax.vmap(tile_forces)(arrived, pairs)
        returned = relayout(pushes, devices, capacity)
        contact = jax.vmap(take_back)(returned, cnodes, slots)
        held_forces = None
        for sub_no in range(SUBS):
            ext_disp = halo_extend(disp, lists)
            forces = jax.vmap(lambda ev, en, th: element_forces(ev, en, th, stiffness))(ext_disp, enodes, thick)
            if sub_no == 0:
                held_forces = forces
            else:
                forces = jnp.where(slow_elems[:, None, :], held_forces, forces)
            summed = jax.vmap(lambda fo, en: assemble(fo, en, extended))(forces, enodes)
            internal = halo_return(summed, lists)
            accel = inv_m[:, None, :] * (f_ext - internal + contact)
            vel = vel + DT * accel
            disp = disp + DT * vel
    return join_dev(disp), join_dev(vel)
```

```python
import functools

import jax
import jax.numpy as jnp
from jax import lax
from jax.experimental import pallas as pl
from jax.experimental.pallas import tpu as pltpu
from jax.sharding import PartitionSpec as P

LANES = 128
EBLK = 128
STEPS = 2
SUBS = 2

FAR = 10000.0
DT = 0.05
PENALTY = 0.5
REACH = 4.0

F32 = jnp.float32
BF16 = jnp.bfloat16
I32 = jnp.int32

VMEM_BYTES = 40 * 1024 * 1024


def lookup(table_row, rows, index):
    hi = index >> 7
    lo = index & (LANES - 1)
    found = [jnp.zeros(index.shape, F32) for _ in range(3)]
    for h in range(rows):
        here = hi == h
        for c in range(3):
            row = jnp.broadcast_to(table_row(c, h), index.shape)
            got = jnp.take_along_axis(row, lo, axis=1, mode="promise_in_bounds")
            found[c] = jnp.where(here, got, found[c])
    return found


def halves(values):
    top = values.astype(BF16).astype(F32)
    return [top, values - top]


def scatter_dot(hi_rows, lo_rows, value_rows, rows):
    row_no = lax.broadcasted_iota(I32, (rows, LANES), 0)
    lane_no = lax.broadcasted_iota(I32, (LANES, LANES), 0)
    total = None
    group = 2
    for start in range(0, len(hi_rows), group):
        lefts, rights = [], []
        for r in range(start, start + group):
            here = row_no == hi_rows[r]
            lefts.append(
                jnp.concatenate(
                    [
                        jnp.where(here, jnp.broadcast_to(vals[r], (rows, LANES)), 0.0)
                        for vals in value_rows
                    ],
                    axis=0,
                ).astype(BF16)
            )
            rights.append((lane_no == lo_rows[r]).astype(F32).astype(BF16))
        part = lax.dot_general(
            jnp.concatenate(lefts, axis=1),
            jnp.concatenate(rights, axis=1),
            (((1,), (1,)), ((), ())),
            preferred_element_type=F32,
        )
        total = part if total is None else total + part
    return total


def scatter_add(index_row, value_row, count, rows):
    hi_rows, lo_rows = [], []
    value_rows = [[] for _ in range(6)]
    for r in range(count):
        idx = index_row(r)
        hi_rows.append(idx >> 7)
        lo_rows.append(idx & (LANES - 1))
        for c in range(3):
            for part, vals in enumerate(halves(value_row(c, r))):
                value_rows[2 * c + part].append(vals)
    total = scatter_dot(hi_rows, lo_rows, value_rows, rows)
    return [
        total[2 * c * rows : (2 * c + 1) * rows] + total[(2 * c + 1) * rows : (2 * c + 2) * rows]
        for c in range(3)
    ]


def spread_rows(source, target, groups):
    rows = source.shape[1] // LANES
    for g in range(groups):
        for h in range(rows):
            target[g * rows + h : g * rows + h + 1, :] = source[
                g : g + 1, h * LANES : (h + 1) * LANES
            ]


def gather_halo(disp, rows, lists, sends):
    found = lookup(lambda c, h: disp[c * rows + h : c * rows + h + 1, :], rows, lists[...])
    quarter = lists.shape[0] // 4
    for b in range(4):
        for c in range(3):
            sends[b][c * quarter : (c + 1) * quarter, :] = found[c][b * quarter : (b + 1) * quarter]


def gather_slots(coords, disp, rows, inverse, outgoing):
    slot_node = inverse[...]
    used = slot_node >= 0
    found = lookup(
        lambda c, h: coords[c * rows + h : c * rows + h + 1, :]
        + disp[c * rows + h : c * rows + h + 1, :],
        rows,
        jnp.maximum(slot_node, 0),
    )
    for c in range(3):
        outgoing[:, c, :] = jnp.where(used, found[c], FAR)


def setup_kernel(
    devices,
    capacity,
    coords_in,
    disp_in,
    vel_in,
    ext_in,
    nodes_in,
    lists_in,
    bucket,
    contact_nodes,
    coords,
    disp,
    vel,
    ext,
    nodes,
    lists,
    inverse,
    outgoing,
    send0,
    send1,
    send2,
    send3,
):
    rows = coords_in.shape[1] // LANES
    spread_rows(disp_in, disp, 3)
    spread_rows(lists_in, lists, 4)
    gather_halo(disp, rows, lists, (send0, send1, send2, send3))
    spread_rows(coords_in, coords, 3)
    count = bucket.shape[0]
    slot_rows = inverse.shape[0]
    dev_no = lax.broadcasted_iota(I32, (devices, LANES), 0)
    first = lax.broadcasted_iota(I32, (LANES, 2 * LANES), 0)
    second = lax.broadcasted_iota(I32, (LANES, 2 * LANES), 1)
    before = ((first < second) | (second >= LANES)).astype(F32).astype(BF16)
    base = jnp.zeros((devices, LANES), F32)
    hi_rows, lo_rows, digits = [], [], [[], []]
    for r in range(count):
        b = bucket[r : r + 1, :]
        onehot = (dev_no == b).astype(F32)
        counts = jnp.dot(onehot.astype(BF16), before, preferred_element_type=F32)
        rank = jnp.sum(onehot * (counts[:, :LANES] + base), axis=0, keepdims=True)
        base = base + counts[:, LANES:]
        slot = b * capacity + rank.astype(I32)
        hi_rows.append(slot >> 7)
        lo_rows.append(slot & (LANES - 1))
        value = contact_nodes[r : r + 1, :] + 1
        digits[0].append((value >> 6).astype(F32))
        digits[1].append((value & 63).astype(F32))
    total = scatter_dot(hi_rows, lo_rows, digits, slot_rows)
    inverse[...] = (total[:slot_rows] * 64.0 + total[slot_rows:]).astype(I32) - 1
    gather_slots(coords, disp, rows, inverse, outgoing)
    spread_rows(nodes_in, nodes, 4)
    spread_rows(vel_in, vel, 3)
    spread_rows(ext_in, ext, 3)


def element_kernel(later, *refs):
    if later:
        (disp, recv0, recv1, recv2, recv3, nodes, thick, stiff, held, slow) = refs[:10]
        (own, out0, out1, out2, out3) = refs[10:]
    else:
        (disp, recv0, recv1, recv2, recv3, nodes, thick, stiff) = refs[:8]
        (own, out0, out1, out2, out3, held) = refs[8:]
    rows = disp.shape[0] // 3
    quarter = recv0.shape[0] // 3
    recvs = (recv0, recv1, recv2, recv3)
    outs = (out0, out1, out2, out3)
    elem_rows = thick.shape[0]

    def table_row(c, h):
        if h < rows:
            return disp[c * rows + h : c * rows + h + 1, :]
        b, q = divmod(h - rows, quarter)
        return recvs[b][c * quarter + q : c * quarter + q + 1, :]

    extended = rows + 4 * quarter
    corners = []
    for k in range(4):
        corners.append(
            lookup(table_row, extended, nodes[k * elem_rows : (k + 1) * elem_rows, :])
        )
    factor = thick[...]
    forces = []
    for i in range(12):
        total = None
        for j in range(12):
            term = stiff[i, j] * corners[j % 4][j // 4]
            total = term if total is None else total + term
        total = factor * total
        span = slice(i * elem_rows, (i + 1) * elem_rows)
        if later:
            total = jnp.where(slow[...] == 1, held[span, :], total)
        else:
            held[span, :] = total
        forces.append(total)

    def value_row(c, r):
        k, h = divmod(r, elem_rows)
        return forces[c * 4 + k][h : h + 1, :]

    sums = scatter_add(lambda r: nodes[r : r + 1, :], value_row, 4 * elem_rows, extended)
    for c in range(3):
        own[c * rows : (c + 1) * rows, :] = sums[c][:rows]
        for b in range(4):
            start = rows + b * quarter
            outs[b][c * quarter : (c + 1) * quarter, :] = sums[c][start : start + quarter]


def contact_kernel(pairs, arrived, pushes, turned):
    tiles = arrived.shape[0]
    pushes[...] = jnp.zeros(pushes.shape, F32)
    for t in range(tiles):
        block = jnp.concatenate([arrived[t], jnp.zeros((5, LANES), F32)], axis=0)
        turned[t] = jnp.transpose(block)
    for p in range(pairs.shape[1]):
        a = pairs[0, p]
        b = pairs[1, p]
        pos_a = arrived[a]
        pos_b = turned[b]
        gaps = [
            jnp.broadcast_to(pos_a[c : c + 1, :], (LANES, LANES))
            - jnp.broadcast_to(pos_b[:, c : c + 1], (LANES, LANES))
            for c in range(3)
        ]
        dist = gaps[0] * gaps[0] + gaps[1] * gaps[1] + gaps[2] * gaps[2]
        weight = PENALTY * jnp.exp(dist * (-1.0 / REACH))
        push = jnp.concatenate(
            [jnp.sum(weight * gaps[c], axis=0, keepdims=True) for c in range(3)], axis=0
        )
        pushes[a] = pushes[a] + push


def update_kernel(first, last, final, *refs):
    refs = list(refs)
    own, back0, back1, back2, back3, lists, ext, inv_mass, vel, disp = refs[:10]
    refs = refs[10:]
    if first:
        returned, inverse = refs[:2]
        refs = refs[2:]
    else:
        contact_in = refs.pop(0)
    if last and not final:
        coords, inverse = refs[:2]
        refs = refs[2:]
    backs = (back0, back1, back2, back3)
    rows = disp.shape[0] // 3
    quarter = back0.shape[0] // 3
    new_vel, new_disp = refs[:2]
    refs = refs[2:]

    def back_row(c, r):
        b, q = divmod(r, quarter)
        return backs[b][c * quarter + q : c * quarter + q + 1, :]

    halo = scatter_add(lambda r: lists[r : r + 1, :], back_row, 4 * quarter, rows)
    if first:
        contact_out = refs.pop(0)
        contact = scatter_add(
            lambda r: inverse[r : r + 1, :],
            lambda c, r: returned[r, c : c + 1, :],
            inverse.shape[0],
            rows,
        )
        for c in range(3):
            contact_out[c * rows : (c + 1) * rows, :] = contact[c]
    else:
        contact = [contact_in[c * rows : (c + 1) * rows, :] for c in range(3)]
    for c in range(3):
        span = slice(c * rows, (c + 1) * rows)
        internal = own[span, :] + halo[c]
        accel = inv_mass[...] * (ext[span, :] - internal + contact[c])
        vel_c = vel[span, :] + DT * accel
        disp_c = disp[span, :] + DT * vel_c
        if final:
            for h in range(rows):
                new_vel[c : c + 1, h * LANES : (h + 1) * LANES] = vel_c[h : h + 1, :]
                new_disp[c : c + 1, h * LANES : (h + 1) * LANES] = disp_c[h : h + 1, :]
        else:
            new_vel[span, :] = vel_c
            new_disp[span, :] = disp_c
    if not final:
        gather_halo(new_disp, rows, lists, refs[:4])
        if last:
            gather_slots(coords, new_disp, rows, inverse, refs[4])


def vmem(count):
    return [pl.BlockSpec(memory_space=pltpu.VMEM)] * count


def shape(*dims):
    return jax.ShapeDtypeStruct(dims, F32)


def call(kernel, inputs, outputs, name, smem=(), scratch=()):
    specs = [
        pl.BlockSpec(memory_space=pltpu.SMEM if i in smem else pltpu.VMEM)
        for i in range(len(inputs))
    ]
    return pl.pallas_call(
        kernel,
        out_shape=tuple(outputs),
        in_specs=specs,
        out_specs=tuple(vmem(len(outputs))),
        scratch_shapes=list(scratch),
        compiler_params=pltpu.CompilerParams(vmem_limit_bytes=VMEM_BYTES),
        name=name,
    )(*inputs)


def shift(block, axis, step):
    count = lax.axis_size(axis)
    pairs = [(i, i + step) for i in range(count) if 0 <= i + step < count]
    return lax.ppermute(block, axis, pairs)


def exchange(to_low_x, to_high_x, to_low_y, to_high_y):
    return (
        shift(to_high_x, "px", 1),
        shift(to_low_x, "px", -1),
        shift(to_high_y, "py", 1),
        shift(to_low_y, "py", -1),
    )


def swap(slots, devices, capacity):
    axes = ("px", "py")
    if capacity == LANES:
        return lax.all_to_all(slots, axes, 0, 0, tiled=True)
    ratio = LANES // capacity
    parts = jnp.transpose(slots.reshape(-1, 3, ratio, capacity), (0, 2, 1, 3)).reshape(
        devices, 3, capacity
    )
    moved = lax.all_to_all(parts, axes, 0, 0, tiled=True)
    return jnp.transpose(moved.reshape(-1, ratio, 3, capacity), (0, 2, 1, 3)).reshape(
        -1, 3, LANES
    )


def body(
    coords,
    displacement,
    velocity,
    inv_mass,
    ext_force,
    thickness,
    stiffness,
    elem_nodes,
    block_class,
    halo_lists,
    contact_nodes,
    contact_bucket,
    tile_pairs,
):
    rows = coords.shape[1] // LANES
    quarter = halo_lists.shape[1] // LANES
    elem_rows = elem_nodes.shape[1] // LANES
    devices = lax.axis_size("px") * lax.axis_size("py")
    capacity = 2 * contact_nodes.shape[0] // devices
    slot_rows = devices * capacity // LANES
    inv_mass = inv_mass.reshape(rows, LANES)
    thickness = thickness.reshape(elem_rows, LANES)
    slow = jnp.broadcast_to(block_class[:, None], (elem_rows, LANES))
    nodal = shape(3 * rows, LANES)
    sent = [shape(3 * quarter, LANES)] * 4
    slots = shape(slot_rows, 3, LANES)

    coords, disp, vel, ext, nodes, lists, inverse, outgoing, *sends = call(
        functools.partial(setup_kernel, devices, capacity),
        [
            coords,
            displacement,
            velocity,
            ext_force,
            elem_nodes,
            halo_lists,
            contact_bucket.reshape(-1, LANES),
            contact_nodes.reshape(-1, LANES),
        ],
        [nodal] * 4
        + [
            jax.ShapeDtypeStruct((4 * elem_rows, LANES), I32),
            jax.ShapeDtypeStruct((4 * quarter, LANES), I32),
            jax.ShapeDtypeStruct((slot_rows, LANES), I32),
            slots,
        ]
        + sent,
        "setup",
    )
    for step_no in range(STEPS):
        for sub_no in range(SUBS):
            first = sub_no == 0
            last = sub_no == SUBS - 1
            final = last and step_no == STEPS - 1
            recvs = exchange(*sends)
            if first:
                arrived = swap(outgoing, devices, capacity)
                own, *rest = call(
                    functools.partial(element_kernel, False),
                    [disp, *recvs, nodes, thickness, stiffness],
                    [nodal] + sent + [shape(12 * elem_rows, LANES)],
                    "elements",
                    smem=(7,),
                )
                held = rest[4]
                backs = exchange(*rest[:4])
                (pushes,) = call(
                    contact_kernel,
                    [tile_pairs, arrived],
                    [slots],
                    "contact",
                    smem=(0,),
                    scratch=[pltpu.VMEM((slot_rows, LANES, 8), F32)],
                )
                returned = swap(pushes, devices, capacity)
            else:
                own, *rest = call(
                    functools.partial(element_kernel, True),
                    [disp, *recvs, nodes, thickness, stiffness, held, slow],
                    [nodal] + sent,
                    "elements_later",
                    smem=(7,),
                )
                backs = exchange(*rest[:4])
            inputs = [own, *backs]
            inputs += [lists, ext, inv_mass, vel, disp]
            inputs += [returned, inverse] if first else [contact]
            outputs = [shape(3, rows * LANES)] * 2 if final else [nodal] * 2
            if first:
                outputs.append(nodal)
            if last and not final:
                inputs += [coords, inverse]
            if not final:
                outputs += sent
                if last:
                    outputs.append(slots)
            vel, disp, *rest = call(
                functools.partial(update_kernel, first, last, final), inputs, outputs, "update"
            )
            if first:
                contact = rest.pop(0)
            if not final:
                sends = rest[:4]
                if last:
                    outgoing = rest[4]
    return (disp, vel)


def solution(mesh):
    placed = (
        P(None, ("px", "py")),
        P(None, ("px", "py")),
        P(None, ("px", "py")),
        P(("px", "py")),
        P(None, ("px", "py")),
        P(("px", "py")),
        P(),
        P(None, ("px", "py")),
        P(("px", "py")),
        P(None, ("px", "py")),
        P(("px", "py")),
        P(("px", "py"), None),
        P(None, ("px", "py")),
    )
    return jax.shard_map(
        body,
        mesh=mesh,
        in_specs=placed,
        out_specs=(P(None, ("px", "py")), P(None, ("px", "py"))),
        check_vma=False,
    )
```

```python
import functools

import jax
import jax.numpy as jnp
from jax import lax
from jax.experimental import pallas as pl
from jax.experimental.pallas import tpu as pltpu
from jax.sharding import PartitionSpec as P

LANES = 128
EBLK = 128
STEPS = 2
SUBS = 2

FAR = 10000.0
DT = 0.05
PENALTY = 0.5
REACH = 4.0

F32 = jnp.float32
BF16 = jnp.bfloat16
I32 = jnp.int32

VMEM_BYTES = 40 * 1024 * 1024


def lookup(table_row, rows, index):
    hi = index >> 7
    lo = index & (LANES - 1)
    found = [jnp.zeros(index.shape, F32) for _ in range(3)]
    for h in range(rows):
        here = hi == h
        for c in range(3):
            row = jnp.broadcast_to(table_row(c, h), index.shape)
            got = jnp.take_along_axis(row, lo, axis=1, mode="promise_in_bounds")
            found[c] = jnp.where(here, got, found[c])
    return found


def halves(values):
    top = values.astype(BF16).astype(F32)
    return [top, values - top]


def scatter_dot(hi_rows, lo_rows, value_rows, rows):
    row_no = lax.broadcasted_iota(I32, (rows, LANES), 0)
    lane_no = lax.broadcasted_iota(I32, (LANES, LANES), 0)
    total = None
    group = 2
    for start in range(0, len(hi_rows), group):
        lefts, rights = [], []
        for r in range(start, start + group):
            here = row_no == hi_rows[r]
            lefts.append(
                jnp.concatenate(
                    [
                        jnp.where(here, jnp.broadcast_to(vals[r], (rows, LANES)), 0.0)
                        for vals in value_rows
                    ],
                    axis=0,
                ).astype(BF16)
            )
            rights.append((lane_no == lo_rows[r]).astype(F32).astype(BF16))
        part = lax.dot_general(
            jnp.concatenate(lefts, axis=1),
            jnp.concatenate(rights, axis=1),
            (((1,), (1,)), ((), ())),
            preferred_element_type=F32,
        )
        total = part if total is None else total + part
    return total


def scatter_add(index_row, value_row, count, rows):
    hi_rows, lo_rows = [], []
    value_rows = [[] for _ in range(6)]
    for r in range(count):
        idx = index_row(r)
        hi_rows.append(idx >> 7)
        lo_rows.append(idx & (LANES - 1))
        for c in range(3):
            for part, vals in enumerate(halves(value_row(c, r))):
                value_rows[2 * c + part].append(vals)
    total = scatter_dot(hi_rows, lo_rows, value_rows, rows)
    return [
        total[2 * c * rows : (2 * c + 1) * rows] + total[(2 * c + 1) * rows : (2 * c + 2) * rows]
        for c in range(3)
    ]


def spread_rows(source, target, groups):
    rows = source.shape[1] // LANES
    for g in range(groups):
        for h in range(rows):
            target[g * rows + h : g * rows + h + 1, :] = source[
                g : g + 1, h * LANES : (h + 1) * LANES
            ]


def gather_halo(disp, rows, lists, sends):
    found = lookup(lambda c, h: disp[c * rows + h : c * rows + h + 1, :], rows, lists[...])
    quarter = lists.shape[0] // 4
    for b in range(4):
        for c in range(3):
            sends[b][c * quarter : (c + 1) * quarter, :] = found[c][b * quarter : (b + 1) * quarter]


def gather_slots(coords, disp, rows, inverse, outgoing):
    slot_node = inverse[...]
    used = slot_node >= 0
    found = lookup(
        lambda c, h: coords[c * rows + h : c * rows + h + 1, :]
        + disp[c * rows + h : c * rows + h + 1, :],
        rows,
        jnp.maximum(slot_node, 0),
    )
    for c in range(3):
        outgoing[:, c, :] = jnp.where(used, found[c], FAR)


def block_remap(index, own_count, width, px_no, py_no, px_count, py_count):
    block = (index - own_count) >> (width.bit_length() - 1)
    along_x = block < 2
    place = jnp.where(along_x, px_no, py_no)
    ends = jnp.where(along_x, px_count - 1, py_count - 1)
    edge = jnp.where((block & 1) == 0, 0, ends)
    moved = index ^ ((1 - (place & 1)) * width)
    moved = jnp.where(place == edge, -1, moved)
    return jnp.where(index < own_count, index, moved)


def setup_kernel(devices, capacity, counts, *refs):
    places = refs[0]
    sources = refs[1:9]
    (coords, disp, vel, ext, nodes, lists, inverse, outgoing) = refs[9:17]
    sends = refs[17:21]
    buffers = refs[21:29]
    sems = refs[29]
    (coords_in, disp_in, vel_in, ext_in, nodes_in, lists_in, bucket, contact_nodes) = buffers
    copies = [
        pltpu.make_async_copy(source, target, sems.at[n])
        for n, (source, target) in enumerate(zip(sources, buffers))
    ]
    for copy in copies:
        copy.start()
    for copy in copies:
        copy.wait()
    px_no = places[0]
    py_no = places[1]
    own_count = coords_in.shape[1]
    rows = own_count // LANES
    spread_rows(disp_in, disp, 3)
    width = lists_in.shape[1]
    quarter = width // LANES
    for b in range(4):
        place = px_no if b < 2 else py_no
        count = counts[b // 2]
        to_high = (place & 1) ^ (1 - b % 2)
        row = (b // 2) * 2
        missing = (place == to_high * (count - 1)).astype(I32)
        for q in range(quarter):
            span = slice(q * LANES, (q + 1) * LANES)
            chosen = jnp.where(
                jnp.full((1, LANES), to_high) == 1,
                lists_in[row + 1 : row + 2, span],
                lists_in[row : row + 1, span],
            )
            lists[b * quarter + q : b * quarter + q + 1, :] = jnp.where(
                jnp.full((1, LANES), missing) == 1, -1, chosen
            )
    gather_halo(disp, rows, lists, sends)
    spread_rows(coords_in, coords, 3)
    count = bucket.shape[0]
    slot_rows = inverse.shape[0]
    dev_no = lax.broadcasted_iota(I32, (devices, LANES), 0)
    first = lax.broadcasted_iota(I32, (LANES, 2 * LANES), 0)
    second = lax.broadcasted_iota(I32, (LANES, 2 * LANES), 1)
    before = ((first < second) | (second >= LANES)).astype(F32).astype(BF16)
    base = jnp.zeros((devices, LANES), F32)
    hi_rows, lo_rows, digits = [], [], [[], []]
    for r in range(count):
        b = bucket[r : r + 1, :]
        onehot = (dev_no == b).astype(F32)
        sums = jnp.dot(onehot.astype(BF16), before, preferred_element_type=F32)
        rank = jnp.sum(onehot * (sums[:, :LANES] + base), axis=0, keepdims=True)
        base = base + sums[:, LANES:]
        slot = b * capacity + rank.astype(I32)
        hi_rows.append(slot >> 7)
        lo_rows.append(slot & (LANES - 1))
        value = contact_nodes[r : r + 1, :] + 1
        digits[0].append((value >> 6).astype(F32))
        digits[1].append((value & 63).astype(F32))
    total = scatter_dot(hi_rows, lo_rows, digits, slot_rows)
    inverse[...] = (total[:slot_rows] * 64.0 + total[slot_rows:]).astype(I32) - 1
    gather_slots(coords, disp, rows, inverse, outgoing)
    spread_rows(nodes_in, nodes, 4)
    nodes[...] = block_remap(nodes[...], own_count, width, px_no, py_no, *counts)
    spread_rows(vel_in, vel, 3)
    spread_rows(ext_in, ext, 3)


def element_kernel(later, *refs):
    if later:
        (disp, recv0, recv1, recv2, recv3, nodes, thick, stiff, held, slow) = refs[:10]
        (own, out0, out1, out2, out3) = refs[10:]
    else:
        (disp, recv0, recv1, recv2, recv3, nodes, thick, stiff, pairs, arrived) = refs[:10]
        (own, out0, out1, out2, out3, held, pushes) = refs[10:]
        contact_tiles(pairs, arrived, pushes)
    rows = disp.shape[0] // 3
    quarter = recv0.shape[0] // 3
    recvs = (recv0, recv1, recv2, recv3)
    outs = (out0, out1, out2, out3)
    elem_rows = thick.shape[0]

    def table_row(c, h):
        if h < rows:
            return disp[c * rows + h : c * rows + h + 1, :]
        b, q = divmod(h - rows, quarter)
        return recvs[b][c * quarter + q : c * quarter + q + 1, :]

    extended = rows + 4 * quarter
    corners = []
    for k in range(4):
        corners.append(
            lookup(table_row, extended, nodes[k * elem_rows : (k + 1) * elem_rows, :])
        )
    factor = thick[...]
    forces = []
    for i in range(12):
        total = None
        for j in range(12):
            term = stiff[i, j] * corners[j % 4][j // 4]
            total = term if total is None else total + term
        total = factor * total
        span = slice(i * elem_rows, (i + 1) * elem_rows)
        if later:
            total = jnp.where(slow[...] == 1, held[span, :], total)
        else:
            held[span, :] = total
        forces.append(total)

    def value_row(c, r):
        k, h = divmod(r, elem_rows)
        return forces[c * 4 + k][h : h + 1, :]

    sums = scatter_add(lambda r: nodes[r : r + 1, :], value_row, 4 * elem_rows, extended)
    for c in range(3):
        own[c * rows : (c + 1) * rows, :] = sums[c][:rows]
        for b in range(4):
            start = rows + b * quarter
            outs[b][c * quarter : (c + 1) * quarter, :] = sums[c][start : start + quarter]


def contact_tiles(pairs, arrived, pushes):
    pushes[...] = jnp.zeros(pushes.shape, F32)
    empty = jnp.zeros((5, LANES), F32)
    for start in range(0, pairs.shape[1], LANES // 8):
        stop = min(start + LANES // 8, pairs.shape[1])
        others = []
        for p in range(start, stop):
            others += [arrived[pairs[1, p]], empty]
        if stop - start < LANES // 8:
            others.append(jnp.zeros((LANES - 8 * (stop - start), LANES), F32))
        turned = jnp.transpose(jnp.concatenate(others, axis=0))
        for p in range(start, stop):
            a = pairs[0, p]
            pos_a = arrived[a]
            column = 8 * (p - start)
            gaps = [
                jnp.broadcast_to(pos_a[c : c + 1, :], (LANES, LANES))
                - jnp.broadcast_to(turned[:, column + c : column + c + 1], (LANES, LANES))
                for c in range(3)
            ]
            dist = gaps[0] * gaps[0] + gaps[1] * gaps[1] + gaps[2] * gaps[2]
            weight = jnp.exp(dist * (-1.0 / REACH))
            push = jnp.concatenate(
                [jnp.sum(weight * gaps[c], axis=0, keepdims=True) for c in range(3)], axis=0
            )
            pushes[a] = pushes[a] + PENALTY * push


def update_kernel(first, last, final, *refs):
    refs = list(refs)
    own, back0, back1, back2, back3, lists, ext, inv_mass, vel, disp = refs[:10]
    refs = refs[10:]
    if first:
        returned, inverse = refs[:2]
        refs = refs[2:]
    else:
        contact_in = refs.pop(0)
    if last and not final:
        coords, inverse = refs[:2]
        refs = refs[2:]
    backs = (back0, back1, back2, back3)
    rows = disp.shape[0] // 3
    quarter = back0.shape[0] // 3
    new_vel, new_disp = refs[:2]
    refs = refs[2:]

    def back_row(c, r):
        b, q = divmod(r, quarter)
        return backs[b][c * quarter + q : c * quarter + q + 1, :]

    halo = scatter_add(lambda r: lists[r : r + 1, :], back_row, 4 * quarter, rows)
    if first:
        contact_out = refs.pop(0)
        contact = scatter_add(
            lambda r: inverse[r : r + 1, :],
            lambda c, r: returned[r, c : c + 1, :],
            inverse.shape[0],
            rows,
        )
        for c in range(3):
            contact_out[c * rows : (c + 1) * rows, :] = contact[c]
    else:
        contact = [contact_in[c * rows : (c + 1) * rows, :] for c in range(3)]
    for c in range(3):
        span = slice(c * rows, (c + 1) * rows)
        internal = own[span, :] + halo[c]
        accel = inv_mass[...] * (ext[span, :] - internal + contact[c])
        vel_c = vel[span, :] + DT * accel
        disp_c = disp[span, :] + DT * vel_c
        if final:
            for h in range(rows):
                new_vel[c : c + 1, h * LANES : (h + 1) * LANES] = vel_c[h : h + 1, :]
                new_disp[c : c + 1, h * LANES : (h + 1) * LANES] = disp_c[h : h + 1, :]
        else:
            new_vel[span, :] = vel_c
            new_disp[span, :] = disp_c
    if not final:
        gather_halo(new_disp, rows, lists, refs[:4])
        if last:
            gather_slots(coords, new_disp, rows, inverse, refs[4])


def vmem(count):
    return [pl.BlockSpec(memory_space=pltpu.VMEM)] * count


def shape(*dims):
    return jax.ShapeDtypeStruct(dims, F32)


def call(kernel, inputs, outputs, name, smem=(), far=(), scratch=()):
    specs = [
        pl.BlockSpec(
            memory_space=pltpu.SMEM if i in smem else pltpu.HBM if i in far else pltpu.VMEM
        )
        for i in range(len(inputs))
    ]
    return pl.pallas_call(
        kernel,
        out_shape=tuple(outputs),
        in_specs=specs,
        out_specs=tuple(vmem(len(outputs))),
        scratch_shapes=list(scratch),
        compiler_params=pltpu.CompilerParams(vmem_limit_bytes=VMEM_BYTES),
        name=name,
    )(*inputs)


def partners():
    px, py = lax.axis_size("px"), lax.axis_size("py")
    number = lambda i, j: i * py + j
    swaps = [[] for _ in range(4)]
    for i in range(px):
        for j in range(py):
            me = number(i, j)
            swaps[0].append((me, number(i ^ 1, j)))
            other = i - 1 if i % 2 == 0 else i + 1
            swaps[1].append((me, number(other, j) if 0 <= other < px else number(i, j ^ 1)))
            swaps[2].append((me, number(i, j ^ 1)))
            other = j - 1 if j % 2 == 0 else j + 1
            swaps[3].append((me, number(i, other % py)))
    return swaps


def exchange(blocks):
    return [lax.ppermute(block, ("px", "py"), pairs) for block, pairs in zip(blocks, partners())]


def swap(slots, devices, capacity):
    axes = ("px", "py")
    if capacity == LANES:
        return lax.all_to_all(slots, axes, 0, 0, tiled=True)
    ratio = LANES // capacity
    parts = jnp.transpose(slots.reshape(-1, 3, ratio, capacity), (0, 2, 1, 3)).reshape(
        devices, 3, capacity
    )
    moved = lax.all_to_all(parts, axes, 0, 0, tiled=True)
    return jnp.transpose(moved.reshape(-1, ratio, 3, capacity), (0, 2, 1, 3)).reshape(
        -1, 3, LANES
    )


def body(
    coords,
    displacement,
    velocity,
    inv_mass,
    ext_force,
    thickness,
    stiffness,
    elem_nodes,
    block_class,
    halo_lists,
    contact_nodes,
    contact_bucket,
    tile_pairs,
):
    rows = coords.shape[1] // LANES
    quarter = halo_lists.shape[1] // LANES
    elem_rows = elem_nodes.shape[1] // LANES
    devices = lax.axis_size("px") * lax.axis_size("py")
    capacity = 2 * contact_nodes.shape[0] // devices
    slot_rows = devices * capacity // LANES
    inv_mass = inv_mass.reshape(rows, LANES)
    thickness = thickness.reshape(elem_rows, LANES)
    slow = jnp.broadcast_to(block_class[:, None], (elem_rows, LANES))
    nodal = shape(3 * rows, LANES)
    sent = [shape(3 * quarter, LANES)] * 4
    slots = shape(slot_rows, 3, LANES)

    places = jnp.stack([lax.axis_index("px"), lax.axis_index("py")]).astype(I32)
    sources = [
        coords,
        displacement,
        velocity,
        ext_force,
        elem_nodes,
        halo_lists,
        contact_bucket.reshape(-1, LANES),
        contact_nodes.reshape(-1, LANES),
    ]
    coords, disp, vel, ext, nodes, lists, inverse, outgoing, *sends = call(
        functools.partial(
            setup_kernel, devices, capacity, (lax.axis_size("px"), lax.axis_size("py"))
        ),
        [places] + sources,
        [nodal] * 4
        + [
            jax.ShapeDtypeStruct((4 * elem_rows, LANES), I32),
            jax.ShapeDtypeStruct((4 * quarter, LANES), I32),
            jax.ShapeDtypeStruct((slot_rows, LANES), I32),
            slots,
        ]
        + sent,
        "setup",
        smem=(0,),
        far=range(1, 9),
        scratch=[pltpu.VMEM(source.shape, source.dtype) for source in sources]
        + [pltpu.SemaphoreType.DMA((len(sources),))],
    )
    for step_no in range(STEPS):
        for sub_no in range(SUBS):
            first = sub_no == 0
            last = sub_no == SUBS - 1
            final = last and step_no == STEPS - 1
            if first:
                arrived = swap(outgoing, devices, capacity)
            recvs = exchange(sends)
            if first:
                own, *rest = call(
                    functools.partial(element_kernel, False),
                    [disp, *recvs, nodes, thickness, stiffness, tile_pairs, arrived],
                    [nodal] + sent + [shape(12 * elem_rows, LANES), slots],
                    "elements",
                    smem=(7, 8),
                )
                held, pushes = rest[4:]
                returned = swap(pushes, devices, capacity)
            else:
                own, *rest = call(
                    functools.partial(element_kernel, True),
                    [disp, *recvs, nodes, thickness, stiffness, held, slow],
                    [nodal] + sent,
                    "elements_later",
                    smem=(7,),
                )
            backs = exchange(rest[:4])
            inputs = [own, *backs]
            inputs += [lists, ext, inv_mass, vel, disp]
            inputs += [returned, inverse] if first else [contact]
            outputs = [shape(3, rows * LANES)] * 2 if final else [nodal] * 2
            if first:
                outputs.append(nodal)
            if last and not final:
                inputs += [coords, inverse]
            if not final:
                outputs += sent
                if last:
                    outputs.append(slots)
            vel, disp, *rest = call(
                functools.partial(update_kernel, first, last, final), inputs, outputs, "update"
            )
            if first:
                contact = rest.pop(0)
            if not final:
                sends = rest[:4]
                if last:
                    outgoing = rest[4]
    return (disp, vel)


def solution(mesh):
    placed = (
        P(None, ("px", "py")),
        P(None, ("px", "py")),
        P(None, ("px", "py")),
        P(("px", "py")),
        P(None, ("px", "py")),
        P(("px", "py")),
        P(),
        P(None, ("px", "py")),
        P(("px", "py")),
        P(None, ("px", "py")),
        P(("px", "py")),
        P(("px", "py"), None),
        P(None, ("px", "py")),
    )
    return jax.shard_map(
        body,
        mesh=mesh,
        in_specs=placed,
        out_specs=(P(None, ("px", "py")), P(None, ("px", "py"))),
        check_vma=False,
    )
```

```python
import functools

import jax
import jax.numpy as jnp
from jax import lax
from jax.experimental import pallas as pl
from jax.experimental.pallas import tpu as pltpu
from jax.sharding import PartitionSpec as P

LANES = 128
EBLK = 128
STEPS = 2
SUBS = 2

FAR = 10000.0
DT = 0.05
PENALTY = 0.5
REACH = 4.0

F32 = jnp.float32
BF16 = jnp.bfloat16
I32 = jnp.int32

VMEM_BYTES = 32 * 1024 * 1024
WHOLE_VMEM = 64 * 1024 * 1024


def lookup(table_row, rows, index):
    parts = []
    for start in range(0, index.shape[0], 8):
        block = index[start : start + 8]
        hi = block >> 7
        lo = block & (LANES - 1)
        found = [jnp.zeros(block.shape, F32) for _ in range(3)]
        for h in range(rows):
            here = hi == h
            for c in range(3):
                row = jnp.broadcast_to(table_row(c, h), block.shape)
                got = jnp.take_along_axis(row, lo, axis=1, mode="promise_in_bounds")
                found[c] = jnp.where(here, got, found[c])
        parts.append(found)
    return [jnp.concatenate([part[c] for part in parts], axis=0) for c in range(3)]


def halves(values):
    top = values.astype(BF16).astype(F32)
    return [top, values - top]


def scatter_dot(hi_rows, lo_rows, value_rows, rows):
    row_no = lax.broadcasted_iota(I32, (rows, LANES), 0)
    lane_no = lax.broadcasted_iota(I32, (LANES, LANES), 0)
    total = None
    group = 2
    for start in range(0, len(hi_rows), group):
        lefts, rights = [], []
        for r in range(start, start + group):
            here = row_no == hi_rows[r]
            lefts.append(
                jnp.concatenate(
                    [
                        jnp.where(here, jnp.broadcast_to(vals[r], (rows, LANES)), 0.0)
                        for vals in value_rows
                    ],
                    axis=0,
                ).astype(BF16)
            )
            rights.append((lane_no == lo_rows[r]).astype(F32).astype(BF16))
        part = lax.dot_general(
            jnp.concatenate(lefts, axis=1),
            jnp.concatenate(rights, axis=1),
            (((1,), (1,)), ((), ())),
            preferred_element_type=F32,
        )
        total = part if total is None else total + part
    return total


def scatter_add(index_row, value_row, count, rows):
    hi_rows, lo_rows = [], []
    value_rows = [[] for _ in range(6)]
    for r in range(count):
        idx = index_row(r)
        hi_rows.append(idx >> 7)
        lo_rows.append(idx & (LANES - 1))
        for c in range(3):
            for part, vals in enumerate(halves(value_row(c, r))):
                value_rows[2 * c + part].append(vals)
    total = scatter_dot(hi_rows, lo_rows, value_rows, rows)
    return [
        total[2 * c * rows : (2 * c + 1) * rows] + total[(2 * c + 1) * rows : (2 * c + 2) * rows]
        for c in range(3)
    ]


def spread_rows(source, target, groups):
    rows = source.shape[1] // LANES
    for g in range(groups):
        for h in range(rows):
            target[g * rows + h : g * rows + h + 1, :] = source[
                g : g + 1, h * LANES : (h + 1) * LANES
            ]


def gather_halo(disp, rows, lists, sends):
    found = lookup(lambda c, h: disp[c * rows + h : c * rows + h + 1, :], rows, lists[...])
    quarter = lists.shape[0] // 4
    for b in range(4):
        for c in range(3):
            sends[b][c * quarter : (c + 1) * quarter, :] = found[c][b * quarter : (b + 1) * quarter]


def gather_slots(coords, disp, rows, inverse, outgoing):
    slot_node = inverse[...]
    used = slot_node >= 0
    found = lookup(
        lambda c, h: coords[c * rows + h : c * rows + h + 1, :]
        + disp[c * rows + h : c * rows + h + 1, :],
        rows,
        jnp.maximum(slot_node, 0),
    )
    for c in range(3):
        outgoing[:, c, :] = jnp.where(used, found[c], FAR)


def block_remap(index, own_count, width, px_no, py_no, px_count, py_count):
    block = (index - own_count) >> (width.bit_length() - 1)
    along_x = block < 2
    place = jnp.where(along_x, px_no, py_no)
    ends = jnp.where(along_x, px_count - 1, py_count - 1)
    edge = jnp.where((block & 1) == 0, 0, ends)
    moved = index ^ ((1 - (place & 1)) * width)
    moved = jnp.where(place == edge, -1, moved)
    return jnp.where(index < own_count, index, moved)


def setup_kernel(devices, capacity, counts, *refs):
    sources = refs[:11]
    (coords, disp, vel, ext, nodes, lists, inverse, outgoing, splat, slow, select) = refs[11:22]
    sends = refs[22:26]
    buffers = refs[26:37]
    sems = refs[37]
    (coords_in, disp_in, vel_in, ext_in, nodes_in, lists_in, bucket, contact_nodes) = buffers[:8]
    (stiff, classes, pairs) = buffers[8:]
    copies = [
        pltpu.make_async_copy(source, target, sems.at[n])
        for n, (source, target) in enumerate(zip(sources, buffers))
    ]
    for copy in copies:
        copy.start()
    for copy in copies:
        copy.wait()
    px_no = lax.axis_index("px")
    py_no = lax.axis_index("py")
    own_count = coords_in.shape[1]
    rows = own_count // LANES
    spread_rows(disp_in, disp, 3)
    width = lists_in.shape[1]
    quarter = width // LANES
    for b in range(4):
        place = px_no if b < 2 else py_no
        count = counts[b // 2]
        to_high = (place & 1) ^ (1 - b % 2)
        row = (b // 2) * 2
        missing = (place == to_high * (count - 1)).astype(I32)
        for q in range(quarter):
            span = slice(q * LANES, (q + 1) * LANES)
            chosen = jnp.where(
                jnp.full((1, LANES), to_high) == 1,
                lists_in[row + 1 : row + 2, span],
                lists_in[row : row + 1, span],
            )
            lists[b * quarter + q : b * quarter + q + 1, :] = jnp.where(
                jnp.full((1, LANES), missing) == 1, -1, chosen
            )
    gather_halo(disp, rows, lists, sends)
    spread_rows(coords_in, coords, 3)
    count = bucket.shape[0]
    slot_rows = inverse.shape[0]
    dev_no = lax.broadcasted_iota(I32, (devices, LANES), 0)
    first = lax.broadcasted_iota(I32, (LANES, 2 * LANES), 0)
    second = lax.broadcasted_iota(I32, (LANES, 2 * LANES), 1)
    before = ((first < second) | (second >= LANES)).astype(F32).astype(BF16)
    base = jnp.zeros((devices, LANES), F32)
    hi_rows, lo_rows, digits = [], [], [[], []]
    for r in range(count):
        b = bucket[r : r + 1, :]
        onehot = (dev_no == b).astype(F32)
        sums = jnp.dot(onehot.astype(BF16), before, preferred_element_type=F32)
        rank = jnp.sum(onehot * (sums[:, :LANES] + base), axis=0, keepdims=True)
        base = base + sums[:, LANES:]
        slot = b * capacity + rank.astype(I32)
        hi_rows.append(slot >> 7)
        lo_rows.append(slot & (LANES - 1))
        value = contact_nodes[r : r + 1, :] + 1
        digits[0].append((value >> 6).astype(F32))
        digits[1].append((value & 63).astype(F32))
    total = scatter_dot(hi_rows, lo_rows, digits, slot_rows)
    inverse[...] = (total[:slot_rows] * 64.0 + total[slot_rows:]).astype(I32) - 1
    gather_slots(coords, disp, rows, inverse, outgoing)
    spread_rows(nodes_in, nodes, 4)
    nodes[...] = block_remap(nodes[...], own_count, width, px_no, py_no, *counts)
    spread_rows(vel_in, vel, 3)
    spread_rows(ext_in, ext, 3)
    size = stiff.shape[0]
    for j in range(size):
        splat[j * size : (j + 1) * size, :] = jnp.broadcast_to(stiff[:, j : j + 1], (size, LANES))
    for h in range(slow.shape[0]):
        slow[h : h + 1, :] = jnp.full((1, LANES), classes[h])
    tile_no = lax.broadcasted_iota(I32, (slot_rows, LANES), 0)
    short = LANES - pairs.shape[1]
    onehots = []
    for side in range(2):
        row = pairs[side : side + 1, :]
        if short:
            row = jnp.concatenate([row, jnp.full((1, short), -1)], axis=1)
        onehots.append((tile_no == row).astype(F32))
    onehots.append(jnp.zeros((LANES - 2 * slot_rows, LANES), F32))
    onehots = jnp.concatenate(onehots, axis=0)
    select[0] = onehots
    select[1] = jnp.transpose(onehots)


def corner_forces(disp, recvs, nodes, thick, splat):
    rows = disp.shape[0] // 3
    quarter = recvs[0].shape[0] // 3
    elem_rows = thick.shape[0]

    def table_row(c, h):
        if h < rows:
            return disp[c * rows + h : c * rows + h + 1, :]
        b, q = divmod(h - rows, quarter)
        return recvs[b][c * quarter + q : c * quarter + q + 1, :]

    corners = [
        lookup(table_row, rows + 4 * quarter, nodes[k * elem_rows : (k + 1) * elem_rows, :])
        for k in range(4)
    ]
    factor = thick[...]
    forces = []
    for i in range(12):
        total = None
        for j in range(12):
            term = splat[j * 12 + i : j * 12 + i + 1, :] * corners[j % 4][j // 4]
            total = term if total is None else total + term
        forces.append(factor * total)
    return forces


def assemble(force_row, nodes, own, outs):
    rows = own.shape[0] // 3
    quarter = outs[0].shape[0] // 3
    sums = scatter_add(
        lambda r: nodes[r : r + 1, :], force_row, nodes.shape[0], rows + 4 * quarter
    )
    for c in range(3):
        own[c * rows : (c + 1) * rows, :] = sums[c][:rows]
        for b in range(4):
            start = rows + b * quarter
            outs[b][c * quarter : (c + 1) * quarter, :] = sums[c][start : start + quarter]


def force_kernel(disp, recv0, recv1, recv2, recv3, nodes, thick, splat, held):
    elem_rows = thick.shape[0]
    forces = corner_forces(disp, (recv0, recv1, recv2, recv3), nodes, thick, splat)
    for i in range(12):
        held[i * elem_rows : (i + 1) * elem_rows, :] = forces[i]


def assemble_kernel(held, nodes, after, own, out0, out1, out2, out3):
    count = nodes.shape[0]
    assemble(
        lambda c, r: held[c * count + r : c * count + r + 1, :], nodes, own, (out0, out1, out2, out3)
    )


def later_kernel(
    disp,
    recv0,
    recv1,
    recv2,
    recv3,
    nodes,
    thick,
    splat,
    held,
    slow,
    own,
    out0,
    out1,
    out2,
    out3,
):
    elem_rows = thick.shape[0]
    forces = corner_forces(disp, (recv0, recv1, recv2, recv3), nodes, thick, splat)
    kept = slow[...] == 1
    forces = [
        jnp.where(kept, held[i * elem_rows : (i + 1) * elem_rows, :], forces[i])
        for i in range(12)
    ]

    def force_row(c, r):
        k, h = divmod(r, elem_rows)
        return forces[c * 4 + k][h : h + 1, :]

    assemble(force_row, nodes, own, (out0, out1, out2, out3))


def contact_kernel(pair_count, select, arrived, after, pushes):
    tiles = arrived.shape[0]
    points = jnp.concatenate([arrived[:, c, :] for c in range(3)], axis=1)
    picked = []
    for side in range(2):
        onehot = select[1, :pair_count, side * tiles : (side + 1) * tiles]
        picked.append(
            jnp.dot(onehot, points, preferred_element_type=F32, precision=lax.Precision.HIGHEST)
        )
    first, second = picked
    group = LANES // 4
    pushed = []
    for start in range(0, pair_count, group):
        stop = min(start + group, pair_count)
        block = jnp.concatenate(
            [second[start:stop, c * LANES : (c + 1) * LANES] for c in range(3)]
            + [jnp.zeros((LANES - 3 * (stop - start), LANES), F32)],
            axis=0,
        )
        turned = jnp.transpose(block)
        for p in range(start, stop):
            gaps = []
            for c in range(3):
                column = c * (stop - start) + p - start
                gaps.append(
                    jnp.broadcast_to(
                        first[p : p + 1, c * LANES : (c + 1) * LANES], (LANES, LANES)
                    )
                    - jnp.broadcast_to(turned[:, column : column + 1], (LANES, LANES))
                )
            dist = gaps[0] * gaps[0] + gaps[1] * gaps[1] + gaps[2] * gaps[2]
            weight = jnp.exp(dist * (-1.0 / REACH))
            pushed.append(
                jnp.concatenate(
                    [jnp.sum(weight * gaps[c], axis=0, keepdims=True) for c in range(3)], axis=1
                )
            )
    total = PENALTY * jnp.dot(
        select[0, :tiles, :pair_count],
        jnp.concatenate(pushed, axis=0),
        preferred_element_type=F32,
        precision=lax.Precision.HIGHEST,
    )
    for c in range(3):
        pushes[:, c, :] = total[:, c * LANES : (c + 1) * LANES]


def update_kernel(first, last, final, *refs):
    refs = list(refs)
    own, back0, back1, back2, back3, lists, ext, inv_mass, vel, disp = refs[:10]
    refs = refs[10:]
    if first:
        returned, inverse = refs[:2]
        refs = refs[2:]
    else:
        contact_in = refs.pop(0)
    if last and not final:
        coords, inverse = refs[:2]
        refs = refs[2:]
    backs = (back0, back1, back2, back3)
    rows = disp.shape[0] // 3
    quarter = back0.shape[0] // 3
    new_vel, new_disp = refs[:2]
    refs = refs[2:]

    def back_row(c, r):
        b, q = divmod(r, quarter)
        return backs[b][c * quarter + q : c * quarter + q + 1, :]

    halo = scatter_add(lambda r: lists[r : r + 1, :], back_row, 4 * quarter, rows)
    if first:
        contact_out = refs.pop(0)
        contact = scatter_add(
            lambda r: inverse[r : r + 1, :],
            lambda c, r: returned[r, c : c + 1, :],
            inverse.shape[0],
            rows,
        )
        for c in range(3):
            contact_out[c * rows : (c + 1) * rows, :] = contact[c]
    else:
        contact = [contact_in[c * rows : (c + 1) * rows, :] for c in range(3)]
    for c in range(3):
        span = slice(c * rows, (c + 1) * rows)
        internal = own[span, :] + halo[c]
        accel = inv_mass[...] * (ext[span, :] - internal + contact[c])
        vel_c = vel[span, :] + DT * accel
        disp_c = disp[span, :] + DT * vel_c
        if final:
            for h in range(rows):
                new_vel[c : c + 1, h * LANES : (h + 1) * LANES] = vel_c[h : h + 1, :]
                new_disp[c : c + 1, h * LANES : (h + 1) * LANES] = disp_c[h : h + 1, :]
        else:
            new_vel[span, :] = vel_c
            new_disp[span, :] = disp_c
    if not final:
        gather_halo(new_disp, rows, lists, refs[:4])
        if last:
            gather_slots(coords, new_disp, rows, inverse, refs[4])


def vmem(count):
    return [pl.BlockSpec(memory_space=pltpu.VMEM)] * count


def shape(*dims):
    return jax.ShapeDtypeStruct(dims, F32)


def call(kernel, inputs, outputs, name, smem=(), far=(), scratch=(), vmem_bytes=VMEM_BYTES):
    specs = [
        pl.BlockSpec(
            memory_space=pltpu.SMEM if i in smem else pl.ANY if i in far else pltpu.VMEM
        )
        for i in range(len(inputs))
    ]
    return pl.pallas_call(
        kernel,
        out_shape=tuple(outputs),
        in_specs=specs,
        out_specs=tuple(vmem(len(outputs))),
        scratch_shapes=list(scratch),
        compiler_params=pltpu.CompilerParams(vmem_limit_bytes=vmem_bytes),
        name=name,
    )(*inputs)


def partners():
    px, py = lax.axis_size("px"), lax.axis_size("py")
    number = lambda i, j: i * py + j
    swaps = [[] for _ in range(4)]
    for i in range(px):
        for j in range(py):
            me = number(i, j)
            swaps[0].append((me, number(i ^ 1, j)))
            other = i - 1 if i % 2 == 0 else i + 1
            swaps[1].append((me, number(other, j) if 0 <= other < px else number(i, j ^ 1)))
            swaps[2].append((me, number(i, j ^ 1)))
            other = j - 1 if j % 2 == 0 else j + 1
            swaps[3].append((me, number(i, other % py)))
    return swaps


def exchange(blocks):
    return [lax.ppermute(block, ("px", "py"), pairs) for block, pairs in zip(blocks, partners())]


def swap(slots, devices, capacity):
    axes = ("px", "py")
    if capacity == LANES:
        return lax.all_to_all(slots, axes, 0, 0, tiled=True)
    ratio = LANES // capacity
    parts = jnp.transpose(slots.reshape(-1, 3, ratio, capacity), (0, 2, 1, 3)).reshape(
        devices, 3, capacity
    )
    moved = lax.all_to_all(parts, axes, 0, 0, tiled=True)
    return jnp.transpose(moved.reshape(-1, ratio, 3, capacity), (0, 2, 1, 3)).reshape(
        -1, 3, LANES
    )


def body(
    coords,
    displacement,
    velocity,
    inv_mass,
    ext_force,
    thickness,
    stiffness,
    elem_nodes,
    block_class,
    halo_lists,
    contact_nodes,
    contact_bucket,
    tile_pairs,
):
    rows = coords.shape[1] // LANES
    quarter = halo_lists.shape[1] // LANES
    elem_rows = elem_nodes.shape[1] // LANES
    devices = lax.axis_size("px") * lax.axis_size("py")
    capacity = 2 * contact_nodes.shape[0] // devices
    slot_rows = devices * capacity // LANES
    inv_mass = inv_mass.reshape(rows, LANES)
    thickness = thickness.reshape(elem_rows, LANES)
    nodal = shape(3 * rows, LANES)
    sent = [shape(3 * quarter, LANES)] * 4
    slots = shape(slot_rows, 3, LANES)

    sources = [
        coords,
        displacement,
        velocity,
        ext_force,
        elem_nodes,
        halo_lists,
        contact_bucket.reshape(-1, LANES),
        contact_nodes.reshape(-1, LANES),
        stiffness,
        block_class,
        tile_pairs,
    ]
    memories = [pltpu.SMEM if source is block_class else pltpu.VMEM for source in sources]
    coords, disp, vel, ext, nodes, lists, inverse, outgoing, splat, slow, select, *sends = call(
        functools.partial(
            setup_kernel, devices, capacity, (lax.axis_size("px"), lax.axis_size("py"))
        ),
        sources,
        [nodal] * 4
        + [
            jax.ShapeDtypeStruct((4 * elem_rows, LANES), I32),
            jax.ShapeDtypeStruct((4 * quarter, LANES), I32),
            jax.ShapeDtypeStruct((slot_rows, LANES), I32),
            slots,
            shape(144, LANES),
            jax.ShapeDtypeStruct((elem_rows, LANES), I32),
            shape(2, LANES, LANES),
        ]
        + sent,
        "setup",
        far=range(len(sources)),
        scratch=[
            memory(source.shape, source.dtype) for memory, source in zip(memories, sources)
        ]
        + [pltpu.SemaphoreType.DMA((len(sources),))],
        vmem_bytes=WHOLE_VMEM,
    )
    for step_no in range(STEPS):
        for sub_no in range(SUBS):
            first = sub_no == 0
            last = sub_no == SUBS - 1
            final = last and step_no == STEPS - 1
            if first:
                arrived = swap(outgoing, devices, capacity)
            recvs = exchange(sends)
            field = [disp, *recvs, nodes, thickness, splat]
            if first:
                (held,) = call(
                    force_kernel, field, [shape(12 * elem_rows, LANES)], "forces"
                )
                (pushes,) = call(
                    functools.partial(contact_kernel, tile_pairs.shape[1]),
                    [select, arrived, held],
                    [slots],
                    "contact",
                    far=(2,),
                )
                returned = swap(pushes, devices, capacity)
                own, *rest = call(
                    assemble_kernel, [held, nodes, pushes], [nodal] + sent, "assemble", far=(2,)
                )
            else:
                own, *rest = call(
                    later_kernel, field + [held, slow], [nodal] + sent, "forces_assemble"
                )
            backs = exchange(rest[:4])
            inputs = [own, *backs]
            inputs += [lists, ext, inv_mass, vel, disp]
            inputs += [returned, inverse] if first else [contact]
            outputs = [shape(3, rows * LANES)] * 2 if final else [nodal] * 2
            if first:
                outputs.append(nodal)
            if last and not final:
                inputs += [coords, inverse]
            if not final:
                outputs += sent
                if last:
                    outputs.append(slots)
            vel, disp, *rest = call(
                functools.partial(update_kernel, first, last, final), inputs, outputs, "update"
            )
            if first:
                contact = rest.pop(0)
            if not final:
                sends = rest[:4]
                if last:
                    outgoing = rest[4]
    return (disp, vel)


def solution(mesh):
    placed = (
        P(None, ("px", "py")),
        P(None, ("px", "py")),
        P(None, ("px", "py")),
        P(("px", "py")),
        P(None, ("px", "py")),
        P(("px", "py")),
        P(),
        P(None, ("px", "py")),
        P(("px", "py")),
        P(None, ("px", "py")),
        P(("px", "py")),
        P(("px", "py"), None),
        P(None, ("px", "py")),
    )
    return jax.shard_map(
        body,
        mesh=mesh,
        in_specs=placed,
        out_specs=(P(None, ("px", "py")), P(None, ("px", "py"))),
        check_vma=False,
    )
```

```python
import functools

import jax
import jax.numpy as jnp
from jax import lax
from jax.experimental import pallas as pl
from jax.experimental.pallas import tpu as pltpu
from jax.sharding import PartitionSpec as P

LANES = 128
EBLK = 128
STEPS = 2
SUBS = 2

FAR = 10000.0
DT = 0.05
PENALTY = 0.5
REACH = 4.0

F32 = jnp.float32
BF16 = jnp.bfloat16
I32 = jnp.int32

VMEM_BYTES = 32 * 1024 * 1024
WHOLE_VMEM = 64 * 1024 * 1024


def lookup(table_row, rows, index):
    parts = []
    for start in range(0, index.shape[0], 8):
        block = index[start : start + 8]
        hi = block >> 7
        lo = block & (LANES - 1)
        found = [jnp.zeros(block.shape, F32) for _ in range(3)]
        for h in range(rows):
            here = hi == h
            for c in range(3):
                row = jnp.broadcast_to(table_row(c, h), block.shape)
                got = jnp.take_along_axis(row, lo, axis=1, mode="promise_in_bounds")
                found[c] = jnp.where(here, got, found[c])
        parts.append(found)
    return [jnp.concatenate([part[c] for part in parts], axis=0) for c in range(3)]


def halves(values):
    top = values.astype(BF16).astype(F32)
    return [top, values - top]


def scatter_dot(hi_rows, lo_rows, value_rows, rows, total=None):
    row_no = lax.broadcasted_iota(I32, (rows, LANES), 0)
    lane_no = lax.broadcasted_iota(I32, (LANES, LANES), 0)
    group = 2
    for start in range(0, len(hi_rows), group):
        lefts, rights = [], []
        for r in range(start, start + group):
            here = row_no == hi_rows[r]
            lefts.append(
                jnp.concatenate(
                    [
                        jnp.where(here, jnp.broadcast_to(vals[r], (rows, LANES)), 0.0)
                        for vals in value_rows
                    ],
                    axis=0,
                ).astype(BF16)
            )
            rights.append((lane_no == lo_rows[r]).astype(F32).astype(BF16))
        part = lax.dot_general(
            jnp.concatenate(lefts, axis=1),
            jnp.concatenate(rights, axis=1),
            (((1,), (1,)), ((), ())),
            preferred_element_type=F32,
        )
        total = part if total is None else total + part
    return total


def scatter_some(index_row, value_row, numbers, rows, total=None):
    hi_rows, lo_rows = [], []
    value_rows = [[] for _ in range(6)]
    for r in numbers:
        idx = index_row(r)
        hi_rows.append(idx >> 7)
        lo_rows.append(idx & (LANES - 1))
        for c in range(3):
            for part, vals in enumerate(halves(value_row(c, r))):
                value_rows[2 * c + part].append(vals)
    return scatter_dot(hi_rows, lo_rows, value_rows, rows, total)


def add_halves(total, rows):
    return [
        total[2 * c * rows : (2 * c + 1) * rows] + total[(2 * c + 1) * rows : (2 * c + 2) * rows]
        for c in range(3)
    ]


def scatter_add(index_row, value_row, count, rows):
    return add_halves(scatter_some(index_row, value_row, range(count), rows), rows)


def spread_rows(source, target, groups):
    rows = source.shape[1] // LANES
    for g in range(groups):
        for h in range(rows):
            target[g * rows + h : g * rows + h + 1, :] = source[
                g : g + 1, h * LANES : (h + 1) * LANES
            ]


def gather_halo(disp, rows, lists, sends):
    found = lookup(lambda c, h: disp[c * rows + h : c * rows + h + 1, :], rows, lists[...])
    quarter = lists.shape[0] // 4
    for b in range(4):
        for c in range(3):
            sends[b][c * quarter : (c + 1) * quarter, :] = found[c][b * quarter : (b + 1) * quarter]


def gather_slots(coords, disp, rows, inverse, outgoing):
    slot_node = inverse[...]
    used = slot_node >= 0
    found = lookup(
        lambda c, h: coords[c * rows + h : c * rows + h + 1, :]
        + disp[c * rows + h : c * rows + h + 1, :],
        rows,
        jnp.maximum(slot_node, 0),
    )
    for c in range(3):
        outgoing[:, c, :] = jnp.where(used, found[c], FAR)


def block_remap(index, own_count, width, px_no, py_no, px_count, py_count):
    block = (index - own_count) >> (width.bit_length() - 1)
    along_x = block < 2
    place = jnp.where(along_x, px_no, py_no)
    ends = jnp.where(along_x, px_count - 1, py_count - 1)
    edge = jnp.where((block & 1) == 0, 0, ends)
    moved = index ^ ((1 - (place & 1)) * width)
    moved = jnp.where(place == edge, -1, moved)
    return jnp.where(index < own_count, index, moved)


def setup_kernel(devices, capacity, counts, *refs):
    sources = refs[:11]
    (coords, disp, vel, ext, nodes, lists, inverse, outgoing, splat, slow, select) = refs[11:22]
    sends = refs[22:26]
    buffers = refs[26:37]
    sems = refs[37]
    (coords_in, disp_in, vel_in, ext_in, nodes_in, lists_in, bucket, contact_nodes) = buffers[:8]
    (stiff, classes, pairs) = buffers[8:]
    copies = [
        pltpu.make_async_copy(source, target, sems.at[n])
        for n, (source, target) in enumerate(zip(sources, buffers))
    ]
    for copy in copies:
        copy.start()
    copies[1].wait()
    copies[5].wait()
    px_no = lax.axis_index("px")
    py_no = lax.axis_index("py")
    own_count = coords_in.shape[1]
    rows = own_count // LANES
    spread_rows(disp_in, disp, 3)
    width = lists_in.shape[1]
    quarter = width // LANES
    for b in range(4):
        place = px_no if b < 2 else py_no
        count = counts[b // 2]
        to_high = (place & 1) ^ (1 - b % 2)
        row = (b // 2) * 2
        missing = (place == to_high * (count - 1)).astype(I32)
        for q in range(quarter):
            span = slice(q * LANES, (q + 1) * LANES)
            chosen = jnp.where(
                jnp.full((1, LANES), to_high) == 1,
                lists_in[row + 1 : row + 2, span],
                lists_in[row : row + 1, span],
            )
            lists[b * quarter + q : b * quarter + q + 1, :] = jnp.where(
                jnp.full((1, LANES), missing) == 1, -1, chosen
            )
    gather_halo(disp, rows, lists, sends)
    for n in (0, 6, 7):
        copies[n].wait()
    spread_rows(coords_in, coords, 3)
    count = bucket.shape[0]
    slot_rows = inverse.shape[0]
    dev_no = lax.broadcasted_iota(I32, (devices, LANES), 0)
    first = lax.broadcasted_iota(I32, (LANES, 2 * LANES), 0)
    second = lax.broadcasted_iota(I32, (LANES, 2 * LANES), 1)
    before = ((first < second) | (second >= LANES)).astype(F32).astype(BF16)
    base = jnp.zeros((devices, LANES), F32)
    hi_rows, lo_rows, digits = [], [], [[], []]
    for r in range(count):
        b = bucket[r : r + 1, :]
        onehot = (dev_no == b).astype(F32)
        sums = jnp.dot(onehot.astype(BF16), before, preferred_element_type=F32)
        rank = jnp.sum(onehot * (sums[:, :LANES] + base), axis=0, keepdims=True)
        base = base + sums[:, LANES:]
        slot = b * capacity + rank.astype(I32)
        hi_rows.append(slot >> 7)
        lo_rows.append(slot & (LANES - 1))
        value = contact_nodes[r : r + 1, :] + 1
        digits[0].append((value >> 6).astype(F32))
        digits[1].append((value & 63).astype(F32))
    total = scatter_dot(hi_rows, lo_rows, digits, slot_rows)
    inverse[...] = (total[:slot_rows] * 64.0 + total[slot_rows:]).astype(I32) - 1
    gather_slots(coords, disp, rows, inverse, outgoing)
    for n in (2, 3, 4, 8, 9, 10):
        copies[n].wait()
    spread_rows(nodes_in, nodes, 4)
    nodes[...] = block_remap(nodes[...], own_count, width, px_no, py_no, *counts)
    spread_rows(vel_in, vel, 3)
    spread_rows(ext_in, ext, 3)
    size = stiff.shape[0]
    for j in range(size):
        splat[j * size : (j + 1) * size, :] = jnp.broadcast_to(stiff[:, j : j + 1], (size, LANES))
    for h in range(slow.shape[0]):
        slow[h : h + 1, :] = jnp.full((1, LANES), classes[h])
    ends = [pairs[0:1, :], pairs[1:2, :]]
    short = LANES - 2 * pairs.shape[1]
    if short:
        ends.append(jnp.full((1, short), -1))
    tile_no = lax.broadcasted_iota(I32, (LANES, LANES), 0)
    onehot = (tile_no == jnp.concatenate(ends, axis=1)).astype(F32)
    select[0] = onehot
    select[1] = jnp.transpose(onehot)


BLOCK = 8


def corner_forces(disp, recvs, nodes, factor, splat, elem_rows, start):
    rows = disp.shape[0] // 3
    quarter = recvs[0].shape[0] // 3

    def table_row(c, h):
        if h < rows:
            return disp[c * rows + h : c * rows + h + 1, :]
        b, q = divmod(h - rows, quarter)
        return recvs[b][c * quarter + q : c * quarter + q + 1, :]

    corners = []
    for k in range(4):
        first = k * elem_rows + start
        corners.append(lookup(table_row, rows + 4 * quarter, nodes[first : first + BLOCK, :]))
    forces = []
    for i in range(12):
        total = None
        for j in range(12):
            term = splat[j * 12 + i : j * 12 + i + 1, :] * corners[j % 4][j // 4]
            total = term if total is None else total + term
        forces.append(factor * total)
    return forces


def store_sums(sums, own, outs):
    rows = own.shape[0] // 3
    quarter = outs[0].shape[0] // 3
    for c in range(3):
        own[c * rows : (c + 1) * rows, :] = sums[c][:rows]
        for b in range(4):
            start = rows + b * quarter
            outs[b][c * quarter : (c + 1) * quarter, :] = sums[c][start : start + quarter]


def force_kernel(disp, recv0, recv1, recv2, recv3, nodes, thick, splat, held):
    elem_rows = thick.shape[0]
    recvs = (recv0, recv1, recv2, recv3)
    for start in range(0, elem_rows, BLOCK):
        factor = thick[start : start + BLOCK, :]
        forces = corner_forces(disp, recvs, nodes, factor, splat, elem_rows, start)
        for i in range(12):
            first = i * elem_rows + start
            held[first : first + BLOCK, :] = forces[i]


def assemble_kernel(held, nodes, after, own, out0, out1, out2, out3):
    count = nodes.shape[0]
    outs = (out0, out1, out2, out3)
    sums = scatter_add(
        lambda r: nodes[r : r + 1, :],
        lambda c, r: held[c * count + r : c * count + r + 1, :],
        count,
        (own.shape[0] + sum(out.shape[0] for out in outs)) // 3,
    )
    store_sums(sums, own, outs)


def later_kernel(
    disp,
    recv0,
    recv1,
    recv2,
    recv3,
    nodes,
    thick,
    splat,
    held,
    slow,
    own,
    out0,
    out1,
    out2,
    out3,
):
    elem_rows = thick.shape[0]
    recvs = (recv0, recv1, recv2, recv3)
    outs = (out0, out1, out2, out3)
    extended = (own.shape[0] + sum(out.shape[0] for out in outs)) // 3
    total = None
    for start in range(0, elem_rows, BLOCK):
        factor = thick[start : start + BLOCK, :]
        forces = corner_forces(disp, recvs, nodes, factor, splat, elem_rows, start)
        kept = slow[start : start + BLOCK, :] == 1
        for i in range(12):
            first = i * elem_rows + start
            forces[i] = jnp.where(kept, held[first : first + BLOCK, :], forces[i])
        total = scatter_some(
            lambda r: nodes[r : r + 1, :],
            lambda c, r: forces[c * 4 + r // elem_rows][
                r % elem_rows - start : r % elem_rows - start + 1, :
            ],
            [k * elem_rows + h for k in range(4) for h in range(start, start + BLOCK)],
            extended,
            total,
        )
    store_sums(add_halves(total, extended), own, outs)


def thirds(values):
    parts = []
    for _ in range(3):
        top = values.astype(BF16)
        parts.append(top)
        values = values - top.astype(F32)
    return jnp.concatenate(parts, axis=1)


def dot_thirds(onehot, values):
    width = values.shape[1]
    sums = jnp.dot(onehot.astype(BF16), thirds(values), preferred_element_type=F32)
    return sums[:, :width] + sums[:, width : 2 * width] + sums[:, 2 * width :]


def contact_kernel(pair_count, select, arrived, after, pushes):
    tiles = arrived.shape[0]
    points = jnp.concatenate([arrived[:, c, :] for c in range(3)], axis=1)
    picked = dot_thirds(select[1, : 2 * pair_count, :tiles], points)
    first, second = picked[:pair_count], picked[pair_count:]
    group = LANES // 4
    pushed = []
    for start in range(0, pair_count, group):
        stop = min(start + group, pair_count)
        block = jnp.concatenate(
            [second[start:stop, c * LANES : (c + 1) * LANES] for c in range(3)]
            + [jnp.zeros((LANES - 3 * (stop - start), LANES), F32)],
            axis=0,
        )
        turned = jnp.transpose(block)
        for p in range(start, stop):
            gaps = []
            for c in range(3):
                column = c * (stop - start) + p - start
                gaps.append(
                    jnp.broadcast_to(
                        first[p : p + 1, c * LANES : (c + 1) * LANES], (LANES, LANES)
                    )
                    - jnp.broadcast_to(turned[:, column : column + 1], (LANES, LANES))
                )
            dist = gaps[0] * gaps[0] + gaps[1] * gaps[1] + gaps[2] * gaps[2]
            weight = jnp.exp(dist * (-1.0 / REACH))
            pushed.append(
                jnp.concatenate(
                    [jnp.sum(weight * gaps[c], axis=0, keepdims=True) for c in range(3)], axis=1
                )
            )
    total = PENALTY * dot_thirds(select[0, :tiles, :pair_count], jnp.concatenate(pushed, axis=0))
    for c in range(3):
        pushes[:, c, :] = total[:, c * LANES : (c + 1) * LANES]


def update_kernel(first, last, final, *refs):
    refs = list(refs)
    own, back0, back1, back2, back3, lists, ext, inv_mass, vel, disp = refs[:10]
    refs = refs[10:]
    if first:
        returned, inverse = refs[:2]
        refs = refs[2:]
    else:
        contact_in = refs.pop(0)
    if last and not final:
        coords, inverse = refs[:2]
        refs = refs[2:]
    backs = (back0, back1, back2, back3)
    rows = disp.shape[0] // 3
    quarter = back0.shape[0] // 3
    new_vel, new_disp = refs[:2]
    refs = refs[2:]

    def back_row(c, r):
        b, q = divmod(r, quarter)
        return backs[b][c * quarter + q : c * quarter + q + 1, :]

    halo = scatter_add(lambda r: lists[r : r + 1, :], back_row, 4 * quarter, rows)
    if first:
        contact_out = refs.pop(0)
        contact = scatter_add(
            lambda r: inverse[r : r + 1, :],
            lambda c, r: returned[r, c : c + 1, :],
            inverse.shape[0],
            rows,
        )
        for c in range(3):
            contact_out[c * rows : (c + 1) * rows, :] = contact[c]
    else:
        contact = [contact_in[c * rows : (c + 1) * rows, :] for c in range(3)]
    for c in range(3):
        span = slice(c * rows, (c + 1) * rows)
        internal = own[span, :] + halo[c]
        accel = inv_mass[...] * (ext[span, :] - internal + contact[c])
        vel_c = vel[span, :] + DT * accel
        disp_c = disp[span, :] + DT * vel_c
        if final:
            for h in range(rows):
                new_vel[c : c + 1, h * LANES : (h + 1) * LANES] = vel_c[h : h + 1, :]
                new_disp[c : c + 1, h * LANES : (h + 1) * LANES] = disp_c[h : h + 1, :]
        else:
            new_vel[span, :] = vel_c
            new_disp[span, :] = disp_c
    if not final:
        gather_halo(new_disp, rows, lists, refs[:4])
        if last:
            gather_slots(coords, new_disp, rows, inverse, refs[4])


def vmem(count):
    return [pl.BlockSpec(memory_space=pltpu.VMEM)] * count


def shape(*dims):
    return jax.ShapeDtypeStruct(dims, F32)


def call(kernel, inputs, outputs, name, smem=(), far=(), scratch=(), vmem_bytes=VMEM_BYTES):
    specs = [
        pl.BlockSpec(
            memory_space=pltpu.SMEM if i in smem else pl.ANY if i in far else pltpu.VMEM
        )
        for i in range(len(inputs))
    ]
    return pl.pallas_call(
        kernel,
        out_shape=tuple(outputs),
        in_specs=specs,
        out_specs=tuple(vmem(len(outputs))),
        scratch_shapes=list(scratch),
        compiler_params=pltpu.CompilerParams(vmem_limit_bytes=vmem_bytes),
        name=name,
    )(*inputs)


def partners():
    px, py = lax.axis_size("px"), lax.axis_size("py")
    number = lambda i, j: i * py + j
    swaps = [[] for _ in range(4)]
    for i in range(px):
        for j in range(py):
            me = number(i, j)
            swaps[0].append((me, number(i ^ 1, j)))
            other = i - 1 if i % 2 == 0 else i + 1
            swaps[1].append((me, number(other, j) if 0 <= other < px else number(i, j ^ 1)))
            swaps[2].append((me, number(i, j ^ 1)))
            other = j - 1 if j % 2 == 0 else j + 1
            swaps[3].append((me, number(i, other % py)))
    return swaps


def exchange(blocks):
    swaps = partners()
    arrived = [None] * 4
    for n in (1, 3, 0, 2):
        arrived[n] = lax.ppermute(blocks[n], ("px", "py"), swaps[n])
    return arrived


def swap(slots, devices, capacity):
    axes = ("px", "py")
    if capacity == LANES:
        return lax.all_to_all(slots, axes, 0, 0, tiled=True)
    ratio = LANES // capacity
    parts = jnp.transpose(slots.reshape(-1, 3, ratio, capacity), (0, 2, 1, 3)).reshape(
        devices, 3, capacity
    )
    moved = lax.all_to_all(parts, axes, 0, 0, tiled=True)
    return jnp.transpose(moved.reshape(-1, ratio, 3, capacity), (0, 2, 1, 3)).reshape(
        -1, 3, LANES
    )


def body(
    coords,
    displacement,
    velocity,
    inv_mass,
    ext_force,
    thickness,
    stiffness,
    elem_nodes,
    block_class,
    halo_lists,
    contact_nodes,
    contact_bucket,
    tile_pairs,
):
    rows = coords.shape[1] // LANES
    quarter = halo_lists.shape[1] // LANES
    elem_rows = elem_nodes.shape[1] // LANES
    devices = lax.axis_size("px") * lax.axis_size("py")
    capacity = 2 * contact_nodes.shape[0] // devices
    slot_rows = devices * capacity // LANES
    inv_mass = inv_mass.reshape(rows, LANES)
    thickness = thickness.reshape(elem_rows, LANES)
    nodal = shape(3 * rows, LANES)
    sent = [shape(3 * quarter, LANES)] * 4
    slots = shape(slot_rows, 3, LANES)

    sources = [
        coords,
        displacement,
        velocity,
        ext_force,
        elem_nodes,
        halo_lists,
        contact_bucket.reshape(-1, LANES),
        contact_nodes.reshape(-1, LANES),
        stiffness,
        block_class,
        tile_pairs,
    ]
    memories = [pltpu.SMEM if source is block_class else pltpu.VMEM for source in sources]
    coords, disp, vel, ext, nodes, lists, inverse, outgoing, splat, slow, select, *sends = call(
        functools.partial(
            setup_kernel, devices, capacity, (lax.axis_size("px"), lax.axis_size("py"))
        ),
        sources,
        [nodal] * 4
        + [
            jax.ShapeDtypeStruct((4 * elem_rows, LANES), I32),
            jax.ShapeDtypeStruct((4 * quarter, LANES), I32),
            jax.ShapeDtypeStruct((slot_rows, LANES), I32),
            slots,
            shape(144, LANES),
            jax.ShapeDtypeStruct((elem_rows, LANES), I32),
            shape(2, LANES, LANES),
        ]
        + sent,
        "setup",
        far=range(len(sources)),
        scratch=[
            memory(source.shape, source.dtype) for memory, source in zip(memories, sources)
        ]
        + [pltpu.SemaphoreType.DMA((len(sources),))],
        vmem_bytes=WHOLE_VMEM,
    )
    for step_no in range(STEPS):
        for sub_no in range(SUBS):
            first = sub_no == 0
            last = sub_no == SUBS - 1
            final = last and step_no == STEPS - 1
            if first:
                arrived = swap(outgoing, devices, capacity)
            recvs = exchange(sends)
            field = [disp, *recvs, nodes, thickness, splat]
            if first:
                (held,) = call(
                    force_kernel, field, [shape(12 * elem_rows, LANES)], "forces"
                )
                (pushes,) = call(
                    functools.partial(contact_kernel, tile_pairs.shape[1]),
                    [select, arrived, held],
                    [slots],
                    "contact",
                    far=(2,),
                )
                returned = swap(pushes, devices, capacity)
                own, *rest = call(
                    assemble_kernel, [held, nodes, pushes], [nodal] + sent, "assemble", far=(2,)
                )
            else:
                own, *rest = call(
                    later_kernel, field + [held, slow], [nodal] + sent, "forces_assemble"
                )
            backs = exchange(rest[:4])
            inputs = [own, *backs]
            inputs += [lists, ext, inv_mass, vel, disp]
            inputs += [returned, inverse] if first else [contact]
            outputs = [shape(3, rows * LANES)] * 2 if final else [nodal] * 2
            if first:
                outputs.append(nodal)
            if last and not final:
                inputs += [coords, inverse]
            if not final:
                outputs += sent
                if last:
                    outputs.append(slots)
            vel, disp, *rest = call(
                functools.partial(update_kernel, first, last, final), inputs, outputs, "update"
            )
            if first:
                contact = rest.pop(0)
            if not final:
                sends = rest[:4]
                if last:
                    outgoing = rest[4]
    return (disp, vel)


def solution(mesh):
    placed = (
        P(None, ("px", "py")),
        P(None, ("px", "py")),
        P(None, ("px", "py")),
        P(("px", "py")),
        P(None, ("px", "py")),
        P(("px", "py")),
        P(),
        P(None, ("px", "py")),
        P(("px", "py")),
        P(None, ("px", "py")),
        P(("px", "py")),
        P(("px", "py"), None),
        P(None, ("px", "py")),
    )
    return jax.shard_map(
        body,
        mesh=mesh,
        in_specs=placed,
        out_specs=(P(None, ("px", "py")), P(None, ("px", "py"))),
        check_vma=False,
    )
```

```python
import functools

import jax
import jax.numpy as jnp
from jax import lax
from jax.experimental import pallas as pl
from jax.experimental.pallas import tpu as pltpu
from jax.sharding import PartitionSpec as P

LANES = 128
EBLK = 128
STEPS = 2
SUBS = 2

FAR = 10000.0
DT = 0.05
PENALTY = 0.5
REACH = 4.0

F32 = jnp.float32
BF16 = jnp.bfloat16
I32 = jnp.int32

VMEM_BYTES = 32 * 1024 * 1024
WHOLE_VMEM = 64 * 1024 * 1024


def lookup(table_row, rows, index):
    parts = []
    for start in range(0, index.shape[0], 8):
        block = index[start : start + 8]
        hi = block >> 7
        lo = block & (LANES - 1)
        found = [jnp.zeros(block.shape, F32) for _ in range(3)]
        for h in range(rows):
            here = hi == h
            for c in range(3):
                row = jnp.broadcast_to(table_row(c, h), block.shape)
                got = jnp.take_along_axis(row, lo, axis=1, mode="promise_in_bounds")
                found[c] = jnp.where(here, got, found[c])
        parts.append(found)
    return [jnp.concatenate([part[c] for part in parts], axis=0) for c in range(3)]


def halves(values):
    top = values.astype(BF16).astype(F32)
    return [top, values - top]


def scatter_dot(hi_rows, lo_rows, value_rows, rows, total=None):
    row_no = lax.broadcasted_iota(I32, (rows, LANES), 0)
    lane_no = lax.broadcasted_iota(I32, (LANES, LANES), 0)
    group = 2
    for start in range(0, len(hi_rows), group):
        lefts, rights = [], []
        for r in range(start, start + group):
            here = row_no == hi_rows[r]
            lefts.append(
                jnp.concatenate(
                    [
                        jnp.where(here, jnp.broadcast_to(vals[r], (rows, LANES)), 0.0)
                        for vals in value_rows
                    ],
                    axis=0,
                ).astype(BF16)
            )
            rights.append((lane_no == lo_rows[r]).astype(F32).astype(BF16))
        part = lax.dot_general(
            jnp.concatenate(lefts, axis=1),
            jnp.concatenate(rights, axis=1),
            (((1,), (1,)), ((), ())),
            preferred_element_type=F32,
        )
        total = part if total is None else total + part
    return total


def scatter_some(index_row, value_row, numbers, rows, total=None):
    hi_rows, lo_rows = [], []
    value_rows = [[] for _ in range(6)]
    for r in numbers:
        idx = index_row(r)
        hi_rows.append(idx >> 7)
        lo_rows.append(idx & (LANES - 1))
        for c in range(3):
            for part, vals in enumerate(halves(value_row(c, r))):
                value_rows[2 * c + part].append(vals)
    return scatter_dot(hi_rows, lo_rows, value_rows, rows, total)


def add_halves(total, rows):
    return [
        total[2 * c * rows : (2 * c + 1) * rows] + total[(2 * c + 1) * rows : (2 * c + 2) * rows]
        for c in range(3)
    ]


def scatter_add(index_row, value_row, count, rows):
    return add_halves(scatter_some(index_row, value_row, range(count), rows), rows)


def spread_rows(source, target, groups):
    rows = source.shape[1] // LANES
    for g in range(groups):
        for h in range(rows):
            target[g * rows + h : g * rows + h + 1, :] = source[
                g : g + 1, h * LANES : (h + 1) * LANES
            ]


def gather_halo(disp, rows, lists, sends):
    found = lookup(lambda c, h: disp[c * rows + h : c * rows + h + 1, :], rows, lists[...])
    quarter = lists.shape[0] // 4
    for b in range(4):
        for c in range(3):
            sends[b][c * quarter : (c + 1) * quarter, :] = found[c][b * quarter : (b + 1) * quarter]


def gather_slots(coords, disp, rows, inverse, outgoing):
    slot_node = inverse[...]
    used = slot_node >= 0
    found = lookup(
        lambda c, h: coords[c * rows + h : c * rows + h + 1, :]
        + disp[c * rows + h : c * rows + h + 1, :],
        rows,
        jnp.maximum(slot_node, 0),
    )
    for c in range(3):
        outgoing[:, c, :] = jnp.where(used, found[c], FAR)


def block_remap(index, own_count, width, px_no, py_no, px_count, py_count):
    block = (index - own_count) >> (width.bit_length() - 1)
    along_x = block < 2
    place = jnp.where(along_x, px_no, py_no)
    ends = jnp.where(along_x, px_count - 1, py_count - 1)
    edge = jnp.where((block & 1) == 0, 0, ends)
    moved = index ^ ((1 - (place & 1)) * width)
    moved = jnp.where(place == edge, -1, moved)
    return jnp.where(index < own_count, index, moved)


def setup_kernel(devices, capacity, counts, *refs):
    sources = refs[:11]
    (coords, disp, vel, ext, nodes, lists, inverse, outgoing, splat, slow, select) = refs[11:22]
    sends = refs[22:26]
    buffers = refs[26:37]
    sems = refs[37]
    (coords_in, disp_in, vel_in, ext_in, nodes_in, lists_in, bucket, contact_nodes) = buffers[:8]
    (stiff, classes, pairs) = buffers[8:]
    copies = [
        pltpu.make_async_copy(source, target, sems.at[n])
        for n, (source, target) in enumerate(zip(sources, buffers))
    ]
    for copy in copies:
        copy.start()
    copies[1].wait()
    copies[5].wait()
    px_no = lax.axis_index("px")
    py_no = lax.axis_index("py")
    own_count = coords_in.shape[1]
    rows = own_count // LANES
    spread_rows(disp_in, disp, 3)
    width = lists_in.shape[1]
    quarter = width // LANES
    for b in range(4):
        place = px_no if b < 2 else py_no
        count = counts[b // 2]
        to_high = (place & 1) ^ (1 - b % 2)
        row = (b // 2) * 2
        missing = (place == to_high * (count - 1)).astype(I32)
        for q in range(quarter):
            span = slice(q * LANES, (q + 1) * LANES)
            chosen = jnp.where(
                jnp.full((1, LANES), to_high) == 1,
                lists_in[row + 1 : row + 2, span],
                lists_in[row : row + 1, span],
            )
            lists[b * quarter + q : b * quarter + q + 1, :] = jnp.where(
                jnp.full((1, LANES), missing) == 1, -1, chosen
            )
    gather_halo(disp, rows, lists, sends)
    for n in (0, 6, 7):
        copies[n].wait()
    spread_rows(coords_in, coords, 3)
    count = bucket.shape[0]
    slot_rows = inverse.shape[0]
    dev_no = lax.broadcasted_iota(I32, (devices, LANES), 0)
    first = lax.broadcasted_iota(I32, (LANES, 2 * LANES), 0)
    second = lax.broadcasted_iota(I32, (LANES, 2 * LANES), 1)
    before = ((first < second) | (second >= LANES)).astype(F32).astype(BF16)
    base = jnp.zeros((devices, LANES), F32)
    hi_rows, lo_rows, digits = [], [], [[], []]
    for r in range(count):
        b = bucket[r : r + 1, :]
        onehot = (dev_no == b).astype(F32)
        sums = jnp.dot(onehot.astype(BF16), before, preferred_element_type=F32)
        rank = jnp.sum(onehot * (sums[:, :LANES] + base), axis=0, keepdims=True)
        base = base + sums[:, LANES:]
        slot = b * capacity + rank.astype(I32)
        hi_rows.append(slot >> 7)
        lo_rows.append(slot & (LANES - 1))
        value = contact_nodes[r : r + 1, :] + 1
        digits[0].append((value >> 6).astype(F32))
        digits[1].append((value & 63).astype(F32))
    total = scatter_dot(hi_rows, lo_rows, digits, slot_rows)
    inverse[...] = (total[:slot_rows] * 64.0 + total[slot_rows:]).astype(I32) - 1
    gather_slots(coords, disp, rows, inverse, outgoing)
    for n in (2, 3, 4, 8, 9, 10):
        copies[n].wait()
    spread_rows(nodes_in, nodes, 4)
    nodes[...] = block_remap(nodes[...], own_count, width, px_no, py_no, *counts)
    spread_rows(vel_in, vel, 3)
    spread_rows(ext_in, ext, 3)
    size = stiff.shape[0]
    for j in range(size):
        splat[j * size : (j + 1) * size, :] = jnp.broadcast_to(stiff[:, j : j + 1], (size, LANES))
    for h in range(slow.shape[0]):
        slow[h : h + 1, :] = jnp.full((1, LANES), classes[h])
    ends = [pairs[0:1, :], pairs[1:2, :]]
    short = LANES - 2 * pairs.shape[1]
    if short:
        ends.append(jnp.full((1, short), -1))
    tile_no = lax.broadcasted_iota(I32, (LANES, LANES), 0)
    onehot = (tile_no == jnp.concatenate(ends, axis=1)).astype(F32)
    select[0] = onehot
    select[1] = jnp.transpose(onehot)


def corner_forces(disp, recvs, nodes, thick, splat):
    rows = disp.shape[0] // 3
    quarter = recvs[0].shape[0] // 3
    elem_rows = thick.shape[0]

    def table_row(c, h):
        if h < rows:
            return disp[c * rows + h : c * rows + h + 1, :]
        b, q = divmod(h - rows, quarter)
        return recvs[b][c * quarter + q : c * quarter + q + 1, :]

    corners = [
        lookup(table_row, rows + 4 * quarter, nodes[k * elem_rows : (k + 1) * elem_rows, :])
        for k in range(4)
    ]
    factor = thick[...]
    forces = []
    for i in range(12):
        total = None
        for j in range(12):
            term = splat[j * 12 + i : j * 12 + i + 1, :] * corners[j % 4][j // 4]
            total = term if total is None else total + term
        forces.append(factor * total)
    return forces


def assemble(force_row, nodes, own, outs):
    rows = own.shape[0] // 3
    quarter = outs[0].shape[0] // 3
    sums = scatter_add(
        lambda r: nodes[r : r + 1, :], force_row, nodes.shape[0], rows + 4 * quarter
    )
    for c in range(3):
        own[c * rows : (c + 1) * rows, :] = sums[c][:rows]
        for b in range(4):
            start = rows + b * quarter
            outs[b][c * quarter : (c + 1) * quarter, :] = sums[c][start : start + quarter]


def force_kernel(disp, recv1, recv3, recv0, recv2, nodes, thick, splat, held):
    elem_rows = thick.shape[0]
    forces = corner_forces(disp, (recv0, recv1, recv2, recv3), nodes, thick, splat)
    for i in range(12):
        held[i * elem_rows : (i + 1) * elem_rows, :] = forces[i]


def assemble_kernel(held, nodes, after, own, out0, out1, out2, out3):
    count = nodes.shape[0]
    assemble(
        lambda c, r: held[c * count + r : c * count + r + 1, :], nodes, own, (out0, out1, out2, out3)
    )


def later_kernel(
    disp,
    recv1,
    recv3,
    recv0,
    recv2,
    nodes,
    thick,
    splat,
    held,
    slow,
    own,
    out0,
    out1,
    out2,
    out3,
):
    elem_rows = thick.shape[0]
    forces = corner_forces(disp, (recv0, recv1, recv2, recv3), nodes, thick, splat)
    kept = slow[...] == 1
    forces = [
        jnp.where(kept, held[i * elem_rows : (i + 1) * elem_rows, :], forces[i])
        for i in range(12)
    ]

    def force_row(c, r):
        k, h = divmod(r, elem_rows)
        return forces[c * 4 + k][h : h + 1, :]

    assemble(force_row, nodes, own, (out0, out1, out2, out3))


def thirds(values):
    parts = []
    for _ in range(3):
        top = values.astype(BF16)
        parts.append(top)
        values = values - top.astype(F32)
    return jnp.concatenate(parts, axis=1)


def dot_thirds(onehot, values):
    width = values.shape[1]
    sums = jnp.dot(onehot.astype(BF16), thirds(values), preferred_element_type=F32)
    return sums[:, :width] + sums[:, width : 2 * width] + sums[:, 2 * width :]


def contact_kernel(pair_count, select, arrived, after, pushes):
    tiles = arrived.shape[0]
    points = jnp.concatenate([arrived[:, c, :] for c in range(3)], axis=1)
    picked = dot_thirds(select[1, : 2 * pair_count, :tiles], points)
    first, second = picked[:pair_count], picked[pair_count:]
    group = LANES // 4
    pushed = []
    for start in range(0, pair_count, group):
        stop = min(start + group, pair_count)
        block = jnp.concatenate(
            [second[start:stop, c * LANES : (c + 1) * LANES] for c in range(3)]
            + [jnp.zeros((LANES - 3 * (stop - start), LANES), F32)],
            axis=0,
        )
        turned = jnp.transpose(block)
        for p in range(start, stop):
            gaps = []
            for c in range(3):
                column = c * (stop - start) + p - start
                gaps.append(
                    jnp.broadcast_to(
                        first[p : p + 1, c * LANES : (c + 1) * LANES], (LANES, LANES)
                    )
                    - jnp.broadcast_to(turned[:, column : column + 1], (LANES, LANES))
                )
            dist = gaps[0] * gaps[0] + gaps[1] * gaps[1] + gaps[2] * gaps[2]
            weight = jnp.exp(dist * (-1.0 / REACH))
            pushed.append(
                jnp.concatenate(
                    [jnp.sum(weight * gaps[c], axis=0, keepdims=True) for c in range(3)], axis=1
                )
            )
    total = PENALTY * dot_thirds(select[0, :tiles, :pair_count], jnp.concatenate(pushed, axis=0))
    for c in range(3):
        pushes[:, c, :] = total[:, c * LANES : (c + 1) * LANES]


def update_kernel(first, last, final, *refs):
    refs = list(refs)
    own, back1, back3, back0, back2, lists, ext, inv_mass, vel, disp = refs[:10]
    refs = refs[10:]
    if first:
        returned, inverse = refs[:2]
        refs = refs[2:]
    else:
        contact_in = refs.pop(0)
    if last and not final:
        coords, inverse = refs[:2]
        refs = refs[2:]
    backs = (back0, back1, back2, back3)
    rows = disp.shape[0] // 3
    quarter = back0.shape[0] // 3
    new_vel, new_disp = refs[:2]
    refs = refs[2:]

    def back_row(c, r):
        b, q = divmod(r, quarter)
        return backs[b][c * quarter + q : c * quarter + q + 1, :]

    halo = scatter_add(lambda r: lists[r : r + 1, :], back_row, 4 * quarter, rows)
    if first:
        contact_out = refs.pop(0)
        contact = scatter_add(
            lambda r: inverse[r : r + 1, :],
            lambda c, r: returned[r, c : c + 1, :],
            inverse.shape[0],
            rows,
        )
        for c in range(3):
            contact_out[c * rows : (c + 1) * rows, :] = contact[c]
    else:
        contact = [contact_in[c * rows : (c + 1) * rows, :] for c in range(3)]
    for c in range(3):
        span = slice(c * rows, (c + 1) * rows)
        internal = own[span, :] + halo[c]
        accel = inv_mass[...] * (ext[span, :] - internal + contact[c])
        vel_c = vel[span, :] + DT * accel
        disp_c = disp[span, :] + DT * vel_c
        if final:
            for h in range(rows):
                new_vel[c : c + 1, h * LANES : (h + 1) * LANES] = vel_c[h : h + 1, :]
                new_disp[c : c + 1, h * LANES : (h + 1) * LANES] = disp_c[h : h + 1, :]
        else:
            new_vel[span, :] = vel_c
            new_disp[span, :] = disp_c
    if not final:
        gather_halo(new_disp, rows, lists, refs[:4])
        if last:
            gather_slots(coords, new_disp, rows, inverse, refs[4])


def vmem(count):
    return [pl.BlockSpec(memory_space=pltpu.VMEM)] * count


def shape(*dims):
    return jax.ShapeDtypeStruct(dims, F32)


def call(kernel, inputs, outputs, name, smem=(), far=(), scratch=(), vmem_bytes=VMEM_BYTES):
    specs = [
        pl.BlockSpec(
            memory_space=pltpu.SMEM if i in smem else pl.ANY if i in far else pltpu.VMEM
        )
        for i in range(len(inputs))
    ]
    return pl.pallas_call(
        kernel,
        out_shape=tuple(outputs),
        in_specs=specs,
        out_specs=tuple(vmem(len(outputs))),
        scratch_shapes=list(scratch),
        compiler_params=pltpu.CompilerParams(vmem_limit_bytes=vmem_bytes),
        name=name,
    )(*inputs)


def partners():
    px, py = lax.axis_size("px"), lax.axis_size("py")
    number = lambda i, j: i * py + j
    swaps = [[] for _ in range(4)]
    for i in range(px):
        for j in range(py):
            me = number(i, j)
            swaps[0].append((me, number(i ^ 1, j)))
            other = i - 1 if i % 2 == 0 else i + 1
            swaps[1].append((me, number(other, j) if 0 <= other < px else number(i, j ^ 1)))
            swaps[2].append((me, number(i, j ^ 1)))
            other = j - 1 if j % 2 == 0 else j + 1
            swaps[3].append((me, number(i, other % py)))
    return swaps


def exchange(blocks):
    swaps = partners()
    return [lax.ppermute(blocks[n], ("px", "py"), swaps[n]) for n in (1, 3, 0, 2)]


def swap(slots, devices, capacity):
    axes = ("px", "py")
    if capacity == LANES:
        return lax.all_to_all(slots, axes, 0, 0, tiled=True)
    ratio = LANES // capacity
    parts = jnp.transpose(slots.reshape(-1, 3, ratio, capacity), (0, 2, 1, 3)).reshape(
        devices, 3, capacity
    )
    moved = lax.all_to_all(parts, axes, 0, 0, tiled=True)
    return jnp.transpose(moved.reshape(-1, ratio, 3, capacity), (0, 2, 1, 3)).reshape(
        -1, 3, LANES
    )


def body(
    coords,
    displacement,
    velocity,
    inv_mass,
    ext_force,
    thickness,
    stiffness,
    elem_nodes,
    block_class,
    halo_lists,
    contact_nodes,
    contact_bucket,
    tile_pairs,
):
    rows = coords.shape[1] // LANES
    quarter = halo_lists.shape[1] // LANES
    elem_rows = elem_nodes.shape[1] // LANES
    devices = lax.axis_size("px") * lax.axis_size("py")
    capacity = 2 * contact_nodes.shape[0] // devices
    slot_rows = devices * capacity // LANES
    inv_mass = inv_mass.reshape(rows, LANES)
    thickness = thickness.reshape(elem_rows, LANES)
    nodal = shape(3 * rows, LANES)
    sent = [shape(3 * quarter, LANES)] * 4
    slots = shape(slot_rows, 3, LANES)

    sources = [
        coords,
        displacement,
        velocity,
        ext_force,
        elem_nodes,
        halo_lists,
        contact_bucket.reshape(-1, LANES),
        contact_nodes.reshape(-1, LANES),
        stiffness,
        block_class,
        tile_pairs,
    ]
    memories = [pltpu.SMEM if source is block_class else pltpu.VMEM for source in sources]
    coords, disp, vel, ext, nodes, lists, inverse, outgoing, splat, slow, select, *sends = call(
        functools.partial(
            setup_kernel, devices, capacity, (lax.axis_size("px"), lax.axis_size("py"))
        ),
        sources,
        [nodal] * 4
        + [
            jax.ShapeDtypeStruct((4 * elem_rows, LANES), I32),
            jax.ShapeDtypeStruct((4 * quarter, LANES), I32),
            jax.ShapeDtypeStruct((slot_rows, LANES), I32),
            slots,
            shape(144, LANES),
            jax.ShapeDtypeStruct((elem_rows, LANES), I32),
            shape(2, LANES, LANES),
        ]
        + sent,
        "setup",
        far=range(len(sources)),
        scratch=[
            memory(source.shape, source.dtype) for memory, source in zip(memories, sources)
        ]
        + [pltpu.SemaphoreType.DMA((len(sources),))],
        vmem_bytes=WHOLE_VMEM,
    )
    for step_no in range(STEPS):
        for sub_no in range(SUBS):
            first = sub_no == 0
            last = sub_no == SUBS - 1
            final = last and step_no == STEPS - 1
            if first:
                arrived = swap(outgoing, devices, capacity)
            recvs = exchange(sends)
            field = [disp, *recvs, nodes, thickness, splat]
            if first:
                (held,) = call(
                    force_kernel, field, [shape(12 * elem_rows, LANES)], "forces"
                )
                (pushes,) = call(
                    functools.partial(contact_kernel, tile_pairs.shape[1]),
                    [select, arrived, held],
                    [slots],
                    "contact",
                    far=(2,),
                )
                returned = swap(pushes, devices, capacity)
                own, *rest = call(
                    assemble_kernel, [held, nodes, pushes], [nodal] + sent, "assemble", far=(2,)
                )
            else:
                own, *rest = call(
                    later_kernel, field + [held, slow], [nodal] + sent, "forces_assemble"
                )
            backs = exchange(rest[:4])
            inputs = [own, *backs]
            inputs += [lists, ext, inv_mass, vel, disp]
            inputs += [returned, inverse] if first else [contact]
            outputs = [shape(3, rows * LANES)] * 2 if final else [nodal] * 2
            if first:
                outputs.append(nodal)
            if last and not final:
                inputs += [coords, inverse]
            if not final:
                outputs += sent
                if last:
                    outputs.append(slots)
            vel, disp, *rest = call(
                functools.partial(update_kernel, first, last, final), inputs, outputs, "update"
            )
            if first:
                contact = rest.pop(0)
            if not final:
                sends = rest[:4]
                if last:
                    outgoing = rest[4]
    return (disp, vel)


def solution(mesh):
    placed = (
        P(None, ("px", "py")),
        P(None, ("px", "py")),
        P(None, ("px", "py")),
        P(("px", "py")),
        P(None, ("px", "py")),
        P(("px", "py")),
        P(),
        P(None, ("px", "py")),
        P(("px", "py")),
        P(None, ("px", "py")),
        P(("px", "py")),
        P(("px", "py"), None),
        P(None, ("px", "py")),
    )
    return jax.shard_map(
        body,
        mesh=mesh,
        in_specs=placed,
        out_specs=(P(None, ("px", "py")), P(None, ("px", "py"))),
        check_vma=False,
    )
```

```python
import functools

import jax
import jax.numpy as jnp
from jax import lax
from jax.experimental import pallas as pl
from jax.experimental.pallas import tpu as pltpu
from jax.sharding import PartitionSpec as P

LANES = 128
EBLK = 128
STEPS = 2
SUBS = 2

FAR = 10000.0
DT = 0.05
PENALTY = 0.5
REACH = 4.0

F32 = jnp.float32
BF16 = jnp.bfloat16
I32 = jnp.int32

VMEM_BYTES = 32 * 1024 * 1024
WHOLE_VMEM = 64 * 1024 * 1024


def lookup(table_row, rows, index, start=None):
    parts = []
    for at in range(0, index.shape[0], 8):
        block = index[at : at + 8]
        hi = block >> 7
        lo = block & (LANES - 1)
        if start is None:
            found = [jnp.zeros(block.shape, F32) for _ in range(3)]
        else:
            found = [start[c][at : at + 8] for c in range(3)]
        for h in rows:
            here = hi == h
            for c in range(3):
                row = jnp.broadcast_to(table_row(c, h), block.shape)
                got = jnp.take_along_axis(row, lo, axis=1, mode="promise_in_bounds")
                found[c] = jnp.where(here, got, found[c])
        parts.append(found)
    return [jnp.concatenate([part[c] for part in parts], axis=0) for c in range(3)]


def halves(values):
    top = values.astype(BF16).astype(F32)
    return [top, values - top]


def scatter_dot(hi_rows, lo_rows, value_rows, rows, total=None):
    row_no = lax.broadcasted_iota(I32, (rows, LANES), 0)
    lane_no = lax.broadcasted_iota(I32, (LANES, LANES), 0)
    group = 2
    for start in range(0, len(hi_rows), group):
        lefts, rights = [], []
        for r in range(start, start + group):
            here = row_no == hi_rows[r]
            lefts.append(
                jnp.concatenate(
                    [
                        jnp.where(here, jnp.broadcast_to(vals[r], (rows, LANES)), 0.0)
                        for vals in value_rows
                    ],
                    axis=0,
                ).astype(BF16)
            )
            rights.append((lane_no == lo_rows[r]).astype(F32).astype(BF16))
        part = lax.dot_general(
            jnp.concatenate(lefts, axis=1),
            jnp.concatenate(rights, axis=1),
            (((1,), (1,)), ((), ())),
            preferred_element_type=F32,
        )
        total = part if total is None else total + part
    return total


def scatter_some(index_row, value_row, numbers, rows, total=None):
    hi_rows, lo_rows = [], []
    value_rows = [[] for _ in range(6)]
    for r in numbers:
        idx = index_row(r)
        hi_rows.append(idx >> 7)
        lo_rows.append(idx & (LANES - 1))
        for c in range(3):
            for part, vals in enumerate(halves(value_row(c, r))):
                value_rows[2 * c + part].append(vals)
    return scatter_dot(hi_rows, lo_rows, value_rows, rows, total)


def add_halves(total, rows):
    return [
        total[2 * c * rows : (2 * c + 1) * rows] + total[(2 * c + 1) * rows : (2 * c + 2) * rows]
        for c in range(3)
    ]


def scatter_add(index_row, value_row, count, rows):
    return add_halves(scatter_some(index_row, value_row, range(count), rows), rows)


def spread_rows(source, target, groups):
    rows = source.shape[1] // LANES
    for g in range(groups):
        for h in range(rows):
            target[g * rows + h : g * rows + h + 1, :] = source[
                g : g + 1, h * LANES : (h + 1) * LANES
            ]


def gather_halo(disp, rows, lists, sends):
    found = lookup(lambda c, h: disp[c * rows + h : c * rows + h + 1, :], range(rows), lists[...])
    quarter = lists.shape[0] // 4
    for b in range(4):
        for c in range(3):
            sends[b][c * quarter : (c + 1) * quarter, :] = found[c][b * quarter : (b + 1) * quarter]


def gather_slots(coords, disp, rows, inverse, outgoing):
    slot_node = inverse[...]
    used = slot_node >= 0
    found = lookup(
        lambda c, h: coords[c * rows + h : c * rows + h + 1, :]
        + disp[c * rows + h : c * rows + h + 1, :],
        range(rows),
        jnp.maximum(slot_node, 0),
    )
    for c in range(3):
        outgoing[:, c, :] = jnp.where(used, found[c], FAR)


def block_remap(index, own_count, width, px_no, py_no, px_count, py_count):
    block = (index - own_count) >> (width.bit_length() - 1)
    along_x = block < 2
    place = jnp.where(along_x, px_no, py_no)
    ends = jnp.where(along_x, px_count - 1, py_count - 1)
    edge = jnp.where((block & 1) == 0, 0, ends)
    moved = index ^ ((1 - (place & 1)) * width)
    moved = jnp.where(place == edge, -1, moved)
    return jnp.where(index < own_count, index, moved)


def setup_kernel(devices, capacity, counts, *refs):
    sources = refs[:11]
    (coords, disp, vel, ext, nodes, lists, inverse, outgoing, splat, slow, select) = refs[11:22]
    sends = refs[22:26]
    buffers = refs[26:37]
    sems = refs[37]
    (coords_in, disp_in, vel_in, ext_in, nodes_in, lists_in, bucket, contact_nodes) = buffers[:8]
    (stiff, classes, pairs) = buffers[8:]
    copies = [
        pltpu.make_async_copy(source, target, sems.at[n])
        for n, (source, target) in enumerate(zip(sources, buffers))
    ]
    for copy in copies:
        copy.start()
    copies[1].wait()
    copies[5].wait()
    px_no = lax.axis_index("px")
    py_no = lax.axis_index("py")
    own_count = coords_in.shape[1]
    rows = own_count // LANES
    spread_rows(disp_in, disp, 3)
    width = lists_in.shape[1]
    quarter = width // LANES
    for b in range(4):
        place = px_no if b < 2 else py_no
        count = counts[b // 2]
        to_high = (place & 1) ^ (1 - b % 2)
        row = (b // 2) * 2
        missing = (place == to_high * (count - 1)).astype(I32)
        for q in range(quarter):
            span = slice(q * LANES, (q + 1) * LANES)
            chosen = jnp.where(
                jnp.full((1, LANES), to_high) == 1,
                lists_in[row + 1 : row + 2, span],
                lists_in[row : row + 1, span],
            )
            lists[b * quarter + q : b * quarter + q + 1, :] = jnp.where(
                jnp.full((1, LANES), missing) == 1, -1, chosen
            )
    gather_halo(disp, rows, lists, sends)
    for n in (0, 6, 7):
        copies[n].wait()
    spread_rows(coords_in, coords, 3)
    count = bucket.shape[0]
    slot_rows = inverse.shape[0]
    dev_no = lax.broadcasted_iota(I32, (devices, LANES), 0)
    first = lax.broadcasted_iota(I32, (LANES, 2 * LANES), 0)
    second = lax.broadcasted_iota(I32, (LANES, 2 * LANES), 1)
    before = ((first < second) | (second >= LANES)).astype(F32).astype(BF16)
    base = jnp.zeros((devices, LANES), F32)
    hi_rows, lo_rows, digits = [], [], [[], []]
    for r in range(count):
        b = bucket[r : r + 1, :]
        onehot = (dev_no == b).astype(F32)
        sums = jnp.dot(onehot.astype(BF16), before, preferred_element_type=F32)
        rank = jnp.sum(onehot * (sums[:, :LANES] + base), axis=0, keepdims=True)
        base = base + sums[:, LANES:]
        slot = b * capacity + rank.astype(I32)
        hi_rows.append(slot >> 7)
        lo_rows.append(slot & (LANES - 1))
        value = contact_nodes[r : r + 1, :] + 1
        digits[0].append((value >> 6).astype(F32))
        digits[1].append((value & 63).astype(F32))
    total = scatter_dot(hi_rows, lo_rows, digits, slot_rows)
    inverse[...] = (total[:slot_rows] * 64.0 + total[slot_rows:]).astype(I32) - 1
    gather_slots(coords, disp, rows, inverse, outgoing)
    for n in (2, 3, 4, 8, 9, 10):
        copies[n].wait()
    spread_rows(nodes_in, nodes, 4)
    nodes[...] = block_remap(nodes[...], own_count, width, px_no, py_no, *counts)
    spread_rows(vel_in, vel, 3)
    spread_rows(ext_in, ext, 3)
    size = stiff.shape[0]
    for j in range(size):
        splat[j * size : (j + 1) * size, :] = jnp.broadcast_to(stiff[:, j : j + 1], (size, LANES))
    for h in range(slow.shape[0]):
        slow[h : h + 1, :] = jnp.full((1, LANES), classes[h])
    ends = [pairs[0:1, :], pairs[1:2, :]]
    short = LANES - 2 * pairs.shape[1]
    if short:
        ends.append(jnp.full((1, short), -1))
    tile_no = lax.broadcasted_iota(I32, (LANES, LANES), 0)
    onehot = (tile_no == jnp.concatenate(ends, axis=1)).astype(F32)
    select[0] = onehot
    select[1] = jnp.transpose(onehot)


def own_kernel(disp, nodes, found):
    rows = disp.shape[0] // 3
    count = nodes.shape[0]
    values = lookup(
        lambda c, h: disp[c * rows + h : c * rows + h + 1, :], range(rows), nodes[...]
    )
    for c in range(3):
        found[c * count : (c + 1) * count, :] = values[c]


def corner_forces(found, rows, recvs, nodes, thick, splat):
    quarter = recvs[0].shape[0] // 3
    elem_rows = thick.shape[0]

    def table_row(c, h):
        b, q = divmod(h - rows, quarter)
        return recvs[b][c * quarter + q : c * quarter + q + 1, :]

    count = nodes.shape[0]
    corners = []
    for k in range(4):
        span = slice(k * elem_rows, (k + 1) * elem_rows)
        own = [found[c * count + span.start : c * count + span.stop, :] for c in range(3)]
        corners.append(
            lookup(table_row, range(rows, rows + 4 * quarter), nodes[span, :], own)
        )
    factor = thick[...]
    forces = []
    for i in range(12):
        total = None
        for j in range(12):
            term = splat[j * 12 + i : j * 12 + i + 1, :] * corners[j % 4][j // 4]
            total = term if total is None else total + term
        forces.append(factor * total)
    return forces


def assemble(force_row, nodes, own, outs):
    rows = own.shape[0] // 3
    quarter = outs[0].shape[0] // 3
    sums = scatter_add(
        lambda r: nodes[r : r + 1, :], force_row, nodes.shape[0], rows + 4 * quarter
    )
    for c in range(3):
        own[c * rows : (c + 1) * rows, :] = sums[c][:rows]
        for b in range(4):
            start = rows + b * quarter
            outs[b][c * quarter : (c + 1) * quarter, :] = sums[c][start : start + quarter]


def force_kernel(rows, found, recv1, recv3, recv0, recv2, nodes, thick, splat, held):
    elem_rows = thick.shape[0]
    forces = corner_forces(found, rows, (recv0, recv1, recv2, recv3), nodes, thick, splat)
    for i in range(12):
        held[i * elem_rows : (i + 1) * elem_rows, :] = forces[i]


def assemble_kernel(held, nodes, after, own, out0, out1, out2, out3):
    count = nodes.shape[0]
    assemble(
        lambda c, r: held[c * count + r : c * count + r + 1, :], nodes, own, (out0, out1, out2, out3)
    )


def later_kernel(
    rows,
    found,
    recv1,
    recv3,
    recv0,
    recv2,
    nodes,
    thick,
    splat,
    held,
    slow,
    own,
    out0,
    out1,
    out2,
    out3,
):
    elem_rows = thick.shape[0]
    forces = corner_forces(found, rows, (recv0, recv1, recv2, recv3), nodes, thick, splat)
    kept = slow[...] == 1
    forces = [
        jnp.where(kept, held[i * elem_rows : (i + 1) * elem_rows, :], forces[i])
        for i in range(12)
    ]

    def force_row(c, r):
        k, h = divmod(r, elem_rows)
        return forces[c * 4 + k][h : h + 1, :]

    assemble(force_row, nodes, own, (out0, out1, out2, out3))


def thirds(values):
    parts = []
    for _ in range(3):
        top = values.astype(BF16)
        parts.append(top)
        values = values - top.astype(F32)
    return jnp.concatenate(parts, axis=1)


def dot_thirds(onehot, values):
    width = values.shape[1]
    sums = jnp.dot(onehot.astype(BF16), thirds(values), preferred_element_type=F32)
    return sums[:, :width] + sums[:, width : 2 * width] + sums[:, 2 * width :]


def contact_kernel(pair_count, select, arrived, after, pushes):
    tiles = arrived.shape[0]
    points = jnp.concatenate([arrived[:, c, :] for c in range(3)], axis=1)
    picked = dot_thirds(select[1, : 2 * pair_count, :tiles], points)
    first, second = picked[:pair_count], picked[pair_count:]
    group = LANES // 4
    pushed = []
    for start in range(0, pair_count, group):
        stop = min(start + group, pair_count)
        block = jnp.concatenate(
            [second[start:stop, c * LANES : (c + 1) * LANES] for c in range(3)]
            + [jnp.zeros((LANES - 3 * (stop - start), LANES), F32)],
            axis=0,
        )
        turned = jnp.transpose(block)
        for p in range(start, stop):
            gaps = []
            for c in range(3):
                column = c * (stop - start) + p - start
                gaps.append(
                    jnp.broadcast_to(
                        first[p : p + 1, c * LANES : (c + 1) * LANES], (LANES, LANES)
                    )
                    - jnp.broadcast_to(turned[:, column : column + 1], (LANES, LANES))
                )
            dist = gaps[0] * gaps[0] + gaps[1] * gaps[1] + gaps[2] * gaps[2]
            weight = jnp.exp(dist * (-1.0 / REACH))
            pushed.append(
                jnp.concatenate(
                    [jnp.sum(weight * gaps[c], axis=0, keepdims=True) for c in range(3)], axis=1
                )
            )
    total = PENALTY * dot_thirds(select[0, :tiles, :pair_count], jnp.concatenate(pushed, axis=0))
    for c in range(3):
        pushes[:, c, :] = total[:, c * LANES : (c + 1) * LANES]


def update_kernel(first, last, final, *refs):
    refs = list(refs)
    own, back1, back3, back0, back2, lists, ext, inv_mass, vel, disp = refs[:10]
    refs = refs[10:]
    if first:
        returned, inverse = refs[:2]
        refs = refs[2:]
    else:
        contact_in = refs.pop(0)
    if last and not final:
        coords, inverse = refs[:2]
        refs = refs[2:]
    backs = (back0, back1, back2, back3)
    rows = disp.shape[0] // 3
    quarter = back0.shape[0] // 3
    new_vel, new_disp = refs[:2]
    refs = refs[2:]

    def back_row(c, r):
        b, q = divmod(r, quarter)
        return backs[b][c * quarter + q : c * quarter + q + 1, :]

    halo = scatter_add(lambda r: lists[r : r + 1, :], back_row, 4 * quarter, rows)
    if first:
        contact_out = refs.pop(0)
        contact = scatter_add(
            lambda r: inverse[r : r + 1, :],
            lambda c, r: returned[r, c : c + 1, :],
            inverse.shape[0],
            rows,
        )
        for c in range(3):
            contact_out[c * rows : (c + 1) * rows, :] = contact[c]
    else:
        contact = [contact_in[c * rows : (c + 1) * rows, :] for c in range(3)]
    for c in range(3):
        span = slice(c * rows, (c + 1) * rows)
        internal = own[span, :] + halo[c]
        accel = inv_mass[...] * (ext[span, :] - internal + contact[c])
        vel_c = vel[span, :] + DT * accel
        disp_c = disp[span, :] + DT * vel_c
        if final:
            for h in range(rows):
                new_vel[c : c + 1, h * LANES : (h + 1) * LANES] = vel_c[h : h + 1, :]
                new_disp[c : c + 1, h * LANES : (h + 1) * LANES] = disp_c[h : h + 1, :]
        else:
            new_vel[span, :] = vel_c
            new_disp[span, :] = disp_c
    if not final:
        gather_halo(new_disp, rows, lists, refs[:4])
        if last:
            gather_slots(coords, new_disp, rows, inverse, refs[4])


def vmem(count):
    return [pl.BlockSpec(memory_space=pltpu.VMEM)] * count


def shape(*dims):
    return jax.ShapeDtypeStruct(dims, F32)


def call(kernel, inputs, outputs, name, smem=(), far=(), scratch=(), vmem_bytes=VMEM_BYTES):
    specs = [
        pl.BlockSpec(
            memory_space=pltpu.SMEM if i in smem else pl.ANY if i in far else pltpu.VMEM
        )
        for i in range(len(inputs))
    ]
    return pl.pallas_call(
        kernel,
        out_shape=tuple(outputs),
        in_specs=specs,
        out_specs=tuple(vmem(len(outputs))),
        scratch_shapes=list(scratch),
        compiler_params=pltpu.CompilerParams(vmem_limit_bytes=vmem_bytes),
        name=name,
    )(*inputs)


def partners():
    px, py = lax.axis_size("px"), lax.axis_size("py")
    number = lambda i, j: i * py + j
    swaps = [[] for _ in range(4)]
    for i in range(px):
        for j in range(py):
            me = number(i, j)
            swaps[0].append((me, number(i ^ 1, j)))
            other = i - 1 if i % 2 == 0 else i + 1
            swaps[1].append((me, number(other, j) if 0 <= other < px else number(i, j ^ 1)))
            swaps[2].append((me, number(i, j ^ 1)))
            other = j - 1 if j % 2 == 0 else j + 1
            swaps[3].append((me, number(i, other % py)))
    return swaps


def exchange(blocks):
    swaps = partners()
    return [lax.ppermute(blocks[n], ("px", "py"), swaps[n]) for n in (1, 3, 0, 2)]


def swap(slots, devices, capacity):
    axes = ("px", "py")
    if capacity == LANES:
        return lax.all_to_all(slots, axes, 0, 0, tiled=True)
    ratio = LANES // capacity
    parts = jnp.transpose(slots.reshape(-1, 3, ratio, capacity), (0, 2, 1, 3)).reshape(
        devices, 3, capacity
    )
    moved = lax.all_to_all(parts, axes, 0, 0, tiled=True)
    return jnp.transpose(moved.reshape(-1, ratio, 3, capacity), (0, 2, 1, 3)).reshape(
        -1, 3, LANES
    )


def body(
    coords,
    displacement,
    velocity,
    inv_mass,
    ext_force,
    thickness,
    stiffness,
    elem_nodes,
    block_class,
    halo_lists,
    contact_nodes,
    contact_bucket,
    tile_pairs,
):
    rows = coords.shape[1] // LANES
    quarter = halo_lists.shape[1] // LANES
    elem_rows = elem_nodes.shape[1] // LANES
    devices = lax.axis_size("px") * lax.axis_size("py")
    capacity = 2 * contact_nodes.shape[0] // devices
    slot_rows = devices * capacity // LANES
    inv_mass = inv_mass.reshape(rows, LANES)
    thickness = thickness.reshape(elem_rows, LANES)
    nodal = shape(3 * rows, LANES)
    sent = [shape(3 * quarter, LANES)] * 4
    slots = shape(slot_rows, 3, LANES)

    sources = [
        coords,
        displacement,
        velocity,
        ext_force,
        elem_nodes,
        halo_lists,
        contact_bucket.reshape(-1, LANES),
        contact_nodes.reshape(-1, LANES),
        stiffness,
        block_class,
        tile_pairs,
    ]
    memories = [pltpu.SMEM if source is block_class else pltpu.VMEM for source in sources]
    coords, disp, vel, ext, nodes, lists, inverse, outgoing, splat, slow, select, *sends = call(
        functools.partial(
            setup_kernel, devices, capacity, (lax.axis_size("px"), lax.axis_size("py"))
        ),
        sources,
        [nodal] * 4
        + [
            jax.ShapeDtypeStruct((4 * elem_rows, LANES), I32),
            jax.ShapeDtypeStruct((4 * quarter, LANES), I32),
            jax.ShapeDtypeStruct((slot_rows, LANES), I32),
            slots,
            shape(144, LANES),
            jax.ShapeDtypeStruct((elem_rows, LANES), I32),
            shape(2, LANES, LANES),
        ]
        + sent,
        "setup",
        far=range(len(sources)),
        scratch=[
            memory(source.shape, source.dtype) for memory, source in zip(memories, sources)
        ]
        + [pltpu.SemaphoreType.DMA((len(sources),))],
        vmem_bytes=WHOLE_VMEM,
    )
    for step_no in range(STEPS):
        for sub_no in range(SUBS):
            first = sub_no == 0
            last = sub_no == SUBS - 1
            final = last and step_no == STEPS - 1
            if first:
                arrived = swap(outgoing, devices, capacity)
            recvs = exchange(sends)
            (found,) = call(own_kernel, [disp, nodes], [shape(12 * elem_rows, LANES)], "own_corners")
            field = [found, *recvs, nodes, thickness, splat]
            if first:
                (held,) = call(
                    functools.partial(force_kernel, rows),
                    field,
                    [shape(12 * elem_rows, LANES)],
                    "forces",
                )
                (pushes,) = call(
                    functools.partial(contact_kernel, tile_pairs.shape[1]),
                    [select, arrived, held],
                    [slots],
                    "contact",
                    far=(2,),
                )
                returned = swap(pushes, devices, capacity)
                own, *rest = call(
                    assemble_kernel, [held, nodes, pushes], [nodal] + sent, "assemble", far=(2,)
                )
            else:
                own, *rest = call(
                    functools.partial(later_kernel, rows),
                    field + [held, slow],
                    [nodal] + sent,
                    "forces_assemble",
                )
            backs = exchange(rest[:4])
            inputs = [own, *backs]
            inputs += [lists, ext, inv_mass, vel, disp]
            inputs += [returned, inverse] if first else [contact]
            outputs = [shape(3, rows * LANES)] * 2 if final else [nodal] * 2
            if first:
                outputs.append(nodal)
            if last and not final:
                inputs += [coords, inverse]
            if not final:
                outputs += sent
                if last:
                    outputs.append(slots)
            vel, disp, *rest = call(
                functools.partial(update_kernel, first, last, final), inputs, outputs, "update"
            )
            if first:
                contact = rest.pop(0)
            if not final:
                sends = rest[:4]
                if last:
                    outgoing = rest[4]
    return (disp, vel)


def solution(mesh):
    placed = (
        P(None, ("px", "py")),
        P(None, ("px", "py")),
        P(None, ("px", "py")),
        P(("px", "py")),
        P(None, ("px", "py")),
        P(("px", "py")),
        P(),
        P(None, ("px", "py")),
        P(("px", "py")),
        P(None, ("px", "py")),
        P(("px", "py")),
        P(("px", "py"), None),
        P(None, ("px", "py")),
    )
    return jax.shard_map(
        body,
        mesh=mesh,
        in_specs=placed,
        out_specs=(P(None, ("px", "py")), P(None, ("px", "py"))),
        check_vma=False,
    )
```

```python
import functools

import jax
import jax.numpy as jnp
from jax import lax
from jax.experimental import pallas as pl
from jax.experimental.pallas import tpu as pltpu
from jax.sharding import PartitionSpec as P

LANES = 128
EBLK = 128
STEPS = 2
SUBS = 2

FAR = 10000.0
DT = 0.05
PENALTY = 0.5
REACH = 4.0

F32 = jnp.float32
BF16 = jnp.bfloat16
I32 = jnp.int32

VMEM_BYTES = 32 * 1024 * 1024
WHOLE_VMEM = 64 * 1024 * 1024


def lookup(table_row, rows, index, start=None):
    parts = []
    for at in range(0, index.shape[0], 8):
        block = index[at : at + 8]
        hi = block >> 7
        lo = block & (LANES - 1)
        if start is None:
            found = [jnp.zeros(block.shape, F32) for _ in range(3)]
        else:
            found = [start[c][at : at + 8] for c in range(3)]
        for h in rows:
            here = hi == h
            for c in range(3):
                row = jnp.broadcast_to(table_row(c, h), block.shape)
                got = jnp.take_along_axis(row, lo, axis=1, mode="promise_in_bounds")
                found[c] = jnp.where(here, got, found[c])
        parts.append(found)
    return [jnp.concatenate([part[c] for part in parts], axis=0) for c in range(3)]


def halves(values):
    top = values.astype(BF16).astype(F32)
    return [top, values - top]


def scatter_dot(hi_rows, lo_rows, value_rows, rows, first=0):
    row_no = first + lax.broadcasted_iota(I32, (rows, LANES), 0)
    total = None
    lane_no = lax.broadcasted_iota(I32, (LANES, LANES), 0)
    group = 2
    for start in range(0, len(hi_rows), group):
        lefts, rights = [], []
        for r in range(start, start + group):
            here = row_no == hi_rows[r]
            lefts.append(
                jnp.concatenate(
                    [
                        jnp.where(here, jnp.broadcast_to(vals[r], (rows, LANES)), 0.0)
                        for vals in value_rows
                    ],
                    axis=0,
                ).astype(BF16)
            )
            rights.append((lane_no == lo_rows[r]).astype(F32).astype(BF16))
        part = lax.dot_general(
            jnp.concatenate(lefts, axis=1),
            jnp.concatenate(rights, axis=1),
            (((1,), (1,)), ((), ())),
            preferred_element_type=F32,
        )
        total = part if total is None else total + part
    return total


def scatter_add(index_row, value_row, count, rows, first=0):
    hi_rows, lo_rows = [], []
    value_rows = [[] for _ in range(6)]
    for r in range(count):
        idx = index_row(r)
        hi_rows.append(idx >> 7)
        lo_rows.append(idx & (LANES - 1))
        for c in range(3):
            for part, vals in enumerate(halves(value_row(c, r))):
                value_rows[2 * c + part].append(vals)
    total = scatter_dot(hi_rows, lo_rows, value_rows, rows, first)
    return [
        total[2 * c * rows : (2 * c + 1) * rows] + total[(2 * c + 1) * rows : (2 * c + 2) * rows]
        for c in range(3)
    ]


def spread_rows(source, target, groups):
    rows = source.shape[1] // LANES
    for g in range(groups):
        for h in range(rows):
            target[g * rows + h : g * rows + h + 1, :] = source[
                g : g + 1, h * LANES : (h + 1) * LANES
            ]


def gather_halo(disp, rows, lists, sends):
    found = lookup(lambda c, h: disp[c * rows + h : c * rows + h + 1, :], range(rows), lists[...])
    quarter = lists.shape[0] // 4
    for b in range(4):
        for c in range(3):
            sends[b][c * quarter : (c + 1) * quarter, :] = found[c][b * quarter : (b + 1) * quarter]


def gather_slots(position_row, rows, inverse, outgoing):
    slot_node = inverse[...]
    found = lookup(position_row, range(rows), jnp.maximum(slot_node, 0))
    for c in range(3):
        outgoing[:, c, :] = jnp.where(slot_node >= 0, found[c], FAR)


def block_remap(index, own_count, width, px_no, py_no, px_count, py_count):
    block = (index - own_count) >> (width.bit_length() - 1)
    along_x = block < 2
    place = jnp.where(along_x, px_no, py_no)
    ends = jnp.where(along_x, px_count - 1, py_count - 1)
    edge = jnp.where((block & 1) == 0, 0, ends)
    moved = index ^ ((1 - (place & 1)) * width)
    moved = jnp.where(place == edge, -1, moved)
    return jnp.where(index < own_count, index, moved)


def slots_kernel(devices, capacity, *refs):
    sources, (inverse, outgoing) = refs[:4], refs[4:6]
    buffers, sems = refs[6:10], refs[10]
    coords, disp, bucket, contact_nodes = buffers
    copies = [
        pltpu.make_async_copy(source, target, sems.at[n])
        for n, (source, target) in enumerate(zip(sources, buffers))
    ]
    for copy in copies:
        copy.start()
    for copy in copies[2:]:
        copy.wait()
    count = bucket.shape[0]
    slot_rows = inverse.shape[0]
    dev_no = lax.broadcasted_iota(I32, (devices, LANES), 0)
    first = lax.broadcasted_iota(I32, (LANES, 2 * LANES), 0)
    second = lax.broadcasted_iota(I32, (LANES, 2 * LANES), 1)
    before = ((first < second) | (second >= LANES)).astype(F32).astype(BF16)
    base = jnp.zeros((devices, LANES), F32)
    hi_rows, lo_rows, digits = [], [], [[], []]
    for r in range(count):
        b = bucket[r : r + 1, :]
        onehot = (dev_no == b).astype(F32)
        sums = jnp.dot(onehot.astype(BF16), before, preferred_element_type=F32)
        rank = jnp.sum(onehot * (sums[:, :LANES] + base), axis=0, keepdims=True)
        base = base + sums[:, LANES:]
        slot = b * capacity + rank.astype(I32)
        hi_rows.append(slot >> 7)
        lo_rows.append(slot & (LANES - 1))
        value = contact_nodes[r : r + 1, :] + 1
        digits[0].append((value >> 6).astype(F32))
        digits[1].append((value & 63).astype(F32))
    total = scatter_dot(hi_rows, lo_rows, digits, slot_rows)
    inverse[...] = (total[:slot_rows] * 64.0 + total[slot_rows:]).astype(I32) - 1
    for copy in copies[:2]:
        copy.wait()

    def position_row(c, h):
        span = slice(h * LANES, (h + 1) * LANES)
        return coords[c : c + 1, span] + disp[c : c + 1, span]

    gather_slots(position_row, coords.shape[1] // LANES, inverse, outgoing)


def halo_kernel(
    counts, disp_in, lists_in, nodes_in, stiff, after, disp, lists, nodes, splat, *sends
):
    px_no = lax.axis_index("px")
    py_no = lax.axis_index("py")
    own_count = disp_in.shape[1]
    rows = own_count // LANES
    spread_rows(disp_in, disp, 3)
    width = lists_in.shape[1]
    quarter = width // LANES
    for b in range(4):
        place = px_no if b < 2 else py_no
        count = counts[b // 2]
        to_high = (place & 1) ^ (1 - b % 2)
        row = (b // 2) * 2
        missing = (place == to_high * (count - 1)).astype(I32)
        for q in range(quarter):
            span = slice(q * LANES, (q + 1) * LANES)
            chosen = jnp.where(
                jnp.full((1, LANES), to_high) == 1,
                lists_in[row + 1 : row + 2, span],
                lists_in[row : row + 1, span],
            )
            lists[b * quarter + q : b * quarter + q + 1, :] = jnp.where(
                jnp.full((1, LANES), missing) == 1, -1, chosen
            )
    gather_halo(disp, rows, lists, sends)
    spread_rows(nodes_in, nodes, 4)
    nodes[...] = block_remap(nodes[...], own_count, width, px_no, py_no, *counts)
    size = stiff.shape[0]
    for j in range(size):
        splat[j * size : (j + 1) * size, :] = jnp.broadcast_to(stiff[:, j : j + 1], (size, LANES))


def rest_kernel(coords_in, vel_in, ext_in, classes, pairs, after, coords, vel, ext, slow, select):
    spread_rows(coords_in, coords, 3)
    spread_rows(vel_in, vel, 3)
    spread_rows(ext_in, ext, 3)
    blocks = classes.shape[1]
    row = jnp.concatenate([classes[...], jnp.zeros((1, LANES - blocks), I32)], axis=1)
    slow[...] = jnp.transpose(jnp.broadcast_to(row, (LANES, LANES)))[:blocks]
    ends = [pairs[0:1, :], pairs[1:2, :]]
    short = LANES - 2 * pairs.shape[1]
    if short:
        ends.append(jnp.full((1, short), -1))
    tile_no = lax.broadcasted_iota(I32, (LANES, LANES), 0)
    onehot = (tile_no == jnp.concatenate(ends, axis=1)).astype(F32)
    select[0] = onehot
    select[1] = jnp.transpose(onehot)


def own_kernel(disp, nodes, found):
    rows = disp.shape[0] // 3
    count = nodes.shape[0]
    values = lookup(
        lambda c, h: disp[c * rows + h : c * rows + h + 1, :], range(rows), nodes[...]
    )
    for c in range(3):
        found[c * count : (c + 1) * count, :] = values[c]


def corner_forces(found, rows, recvs, nodes, thick, splat):
    quarter = recvs[0].shape[0] // 3
    elem_rows = thick.shape[0]

    def table_row(c, h):
        b, q = divmod(h - rows, quarter)
        return recvs[b][c * quarter + q : c * quarter + q + 1, :]

    count = nodes.shape[0]
    corners = []
    for k in range(4):
        span = slice(k * elem_rows, (k + 1) * elem_rows)
        own = [found[c * count + span.start : c * count + span.stop, :] for c in range(3)]
        corners.append(
            lookup(table_row, range(rows, rows + 4 * quarter), nodes[span, :], own)
        )
    factor = thick[...]
    forces = []
    for i in range(12):
        total = None
        for j in range(12):
            term = splat[j * 12 + i : j * 12 + i + 1, :] * corners[j % 4][j // 4]
            total = term if total is None else total + term
        forces.append(factor * total)
    return forces


def stored_row(forces, nodes):
    count = nodes.shape[0]
    return lambda c, r: forces[c * count + r : c * count + r + 1, :]


def sum_own(force_row, nodes, own):
    rows = own.shape[0] // 3
    sums = scatter_add(lambda r: nodes[r : r + 1, :], force_row, nodes.shape[0], rows)
    for c in range(3):
        own[c * rows : (c + 1) * rows, :] = sums[c]


def sum_halo(force_row, nodes, rows, outs):
    quarter = outs[0].shape[0] // 3
    sums = scatter_add(
        lambda r: nodes[r : r + 1, :], force_row, nodes.shape[0], 4 * quarter, rows
    )
    for c in range(3):
        for b in range(4):
            outs[b][c * quarter : (c + 1) * quarter, :] = sums[c][b * quarter : (b + 1) * quarter]


def force_kernel(rows, found, recv1, recv3, recv0, recv2, nodes, thick, splat, held):
    elem_rows = thick.shape[0]
    forces = corner_forces(found, rows, (recv0, recv1, recv2, recv3), nodes, thick, splat)
    for i in range(12):
        held[i * elem_rows : (i + 1) * elem_rows, :] = forces[i]


def halo_sum_kernel(rows, held, nodes, after, *outs):
    sum_halo(stored_row(held, nodes), nodes, rows, outs)


def own_sum_kernel(held, nodes, after, own):
    sum_own(stored_row(held, nodes), nodes, own)


def later_kernel(
    rows,
    found,
    recv1,
    recv3,
    recv0,
    recv2,
    nodes,
    thick,
    splat,
    held,
    slow,
    mixed,
    *outs,
):
    elem_rows = thick.shape[0]
    forces = corner_forces(found, rows, (recv0, recv1, recv2, recv3), nodes, thick, splat)
    kept = slow[...] == 1
    for i in range(12):
        span = slice(i * elem_rows, (i + 1) * elem_rows)
        forces[i] = jnp.where(kept, held[span, :], forces[i])
        mixed[span, :] = forces[i]

    def force_row(c, r):
        k, h = divmod(r, elem_rows)
        return forces[c * 4 + k][h : h + 1, :]

    sum_halo(force_row, nodes, rows, outs)


def returned_sums(backs, lists, rows):
    quarter = backs[0].shape[0] // 3

    def back_row(c, r):
        b, q = divmod(r, quarter)
        return backs[b][c * quarter + q : c * quarter + q + 1, :]

    return scatter_add(lambda r: lists[r : r + 1, :], back_row, 4 * quarter, rows)


def internal_kernel(own, back1, back3, back0, back2, lists, internal):
    rows = own.shape[0] // 3
    sums = returned_sums((back0, back1, back2, back3), lists, rows)
    for c in range(3):
        span = slice(c * rows, (c + 1) * rows)
        internal[span, :] = own[span, :] + sums[c]


def sends_kernel(disp, lists, after, *sends):
    gather_halo(disp, disp.shape[0] // 3, lists, sends)


def thirds(values):
    parts = []
    for _ in range(3):
        top = values.astype(BF16)
        parts.append(top)
        values = values - top.astype(F32)
    return jnp.concatenate(parts, axis=1)


def dot_thirds(onehot, values):
    width = values.shape[1]
    sums = jnp.dot(onehot.astype(BF16), thirds(values), preferred_element_type=F32)
    return sums[:, :width] + sums[:, width : 2 * width] + sums[:, 2 * width :]


def contact_kernel(pair_count, select, arrived, after, pushes):
    tiles = arrived.shape[0]
    points = jnp.concatenate([arrived[:, c, :] for c in range(3)], axis=1)
    picked = dot_thirds(select[1, : 2 * pair_count, :tiles], points)
    first, second = picked[:pair_count], picked[pair_count:]
    group = LANES // 4
    pushed = []
    for start in range(0, pair_count, group):
        stop = min(start + group, pair_count)
        block = jnp.concatenate(
            [second[start:stop, c * LANES : (c + 1) * LANES] for c in range(3)]
            + [jnp.zeros((LANES - 3 * (stop - start), LANES), F32)],
            axis=0,
        )
        turned = jnp.transpose(block)
        for p in range(start, stop):
            gaps = []
            for c in range(3):
                column = c * (stop - start) + p - start
                gaps.append(
                    jnp.broadcast_to(
                        first[p : p + 1, c * LANES : (c + 1) * LANES], (LANES, LANES)
                    )
                    - jnp.broadcast_to(turned[:, column : column + 1], (LANES, LANES))
                )
            dist = gaps[0] * gaps[0] + gaps[1] * gaps[1] + gaps[2] * gaps[2]
            weight = jnp.exp(dist * (-1.0 / REACH))
            pushed.append(
                jnp.concatenate(
                    [jnp.sum(weight * gaps[c], axis=0, keepdims=True) for c in range(3)], axis=1
                )
            )
    total = PENALTY * dot_thirds(select[0, :tiles, :pair_count], jnp.concatenate(pushed, axis=0))
    for c in range(3):
        pushes[:, c, :] = total[:, c * LANES : (c + 1) * LANES]


def advance(internal, contact, ext, inv_mass, vel, disp, rows):
    for c in range(3):
        span = slice(c * rows, (c + 1) * rows)
        accel = inv_mass[...] * (ext[span, :] - internal[c] + contact[c])
        vel_c = vel[span, :] + DT * accel
        yield c, vel_c, disp[span, :] + DT * vel_c


def components(array):
    rows = array.shape[0] // 3
    return [array[c * rows : (c + 1) * rows, :] for c in range(3)]


def first_update_kernel(
    internal, returned, inverse, lists, ext, inv_mass, vel, disp, new_vel, new_disp, contact, *sends
):
    rows = disp.shape[0] // 3
    sums = scatter_add(
        lambda r: inverse[r : r + 1, :],
        lambda c, r: returned[r, c : c + 1, :],
        inverse.shape[0],
        rows,
    )
    steps = advance(components(internal), sums, ext, inv_mass, vel, disp, rows)
    for c, vel_c, disp_c in steps:
        span = slice(c * rows, (c + 1) * rows)
        contact[span, :] = sums[c]
        new_vel[span, :] = vel_c
        new_disp[span, :] = disp_c
    gather_halo(new_disp, rows, lists, sends)


def update_kernel(case, *refs):
    refs = list(refs)
    own, back1, back3, back0, back2, lists, ext, inv_mass, vel, disp, contact = refs[:11]
    rows = disp.shape[0] // 3
    sums = returned_sums((back0, back1, back2, back3), lists, rows)
    internal = [mine + more for mine, more in zip(components(own), sums)]
    steps = advance(internal, components(contact), ext, inv_mass, vel, disp, rows)
    if case == "final":
        new_vel, new_disp = refs[11:]
        for c, vel_c, disp_c in steps:
            for h in range(rows):
                new_vel[c : c + 1, h * LANES : (h + 1) * LANES] = vel_c[h : h + 1, :]
                new_disp[c : c + 1, h * LANES : (h + 1) * LANES] = disp_c[h : h + 1, :]
        return
    if case == "last":
        coords, inverse, new_vel, new_disp, outgoing = refs[11:]
    else:
        new_vel, new_disp, *sends = refs[11:]
    for c, vel_c, disp_c in steps:
        new_vel[c * rows : (c + 1) * rows, :] = vel_c
        new_disp[c * rows : (c + 1) * rows, :] = disp_c
    if case == "last":

        def position_row(c, h):
            span = slice(c * rows + h, c * rows + h + 1)
            return coords[span, :] + new_disp[span, :]

        gather_slots(position_row, rows, inverse, outgoing)
    else:
        gather_halo(new_disp, rows, lists, sends)


def vmem(count):
    return [pl.BlockSpec(memory_space=pltpu.VMEM)] * count


def shape(*dims):
    return jax.ShapeDtypeStruct(dims, F32)


def call(kernel, inputs, outputs, name, smem=(), far=(), scratch=(), vmem_bytes=VMEM_BYTES):
    specs = [
        pl.BlockSpec(
            memory_space=pltpu.SMEM if i in smem else pl.ANY if i in far else pltpu.VMEM
        )
        for i in range(len(inputs))
    ]
    return pl.pallas_call(
        kernel,
        out_shape=tuple(outputs),
        in_specs=specs,
        out_specs=tuple(vmem(len(outputs))),
        scratch_shapes=list(scratch),
        compiler_params=pltpu.CompilerParams(vmem_limit_bytes=vmem_bytes),
        name=name,
    )(*inputs)


def partners():
    px, py = lax.axis_size("px"), lax.axis_size("py")
    number = lambda i, j: i * py + j
    swaps = [[] for _ in range(4)]
    for i in range(px):
        for j in range(py):
            me = number(i, j)
            swaps[0].append((me, number(i ^ 1, j)))
            other = i - 1 if i % 2 == 0 else i + 1
            swaps[1].append((me, number(other, j) if 0 <= other < px else number(i, j ^ 1)))
            swaps[2].append((me, number(i, j ^ 1)))
            other = j - 1 if j % 2 == 0 else j + 1
            swaps[3].append((me, number(i, other % py)))
    return swaps


def exchange(blocks):
    swaps = partners()
    return [lax.ppermute(blocks[n], ("px", "py"), swaps[n]) for n in (1, 3, 0, 2)]


def swap(slots, devices, capacity):
    axes = ("px", "py")
    if capacity == LANES:
        return lax.all_to_all(slots, axes, 0, 0, tiled=True)
    ratio = LANES // capacity
    parts = jnp.transpose(slots.reshape(-1, 3, ratio, capacity), (0, 2, 1, 3)).reshape(
        devices, 3, capacity
    )
    moved = lax.all_to_all(parts, axes, 0, 0, tiled=True)
    return jnp.transpose(moved.reshape(-1, ratio, 3, capacity), (0, 2, 1, 3)).reshape(
        -1, 3, LANES
    )


def body(
    coords,
    displacement,
    velocity,
    inv_mass,
    ext_force,
    thickness,
    stiffness,
    elem_nodes,
    block_class,
    halo_lists,
    contact_nodes,
    contact_bucket,
    tile_pairs,
):
    rows = coords.shape[1] // LANES
    quarter = halo_lists.shape[1] // LANES
    elem_rows = elem_nodes.shape[1] // LANES
    devices = lax.axis_size("px") * lax.axis_size("py")
    capacity = 2 * contact_nodes.shape[0] // devices
    slot_rows = devices * capacity // LANES
    inv_mass = inv_mass.reshape(rows, LANES)
    thickness = thickness.reshape(elem_rows, LANES)
    nodal = shape(3 * rows, LANES)
    sent = [shape(3 * quarter, LANES)] * 4
    slots = shape(slot_rows, 3, LANES)

    counts = (lax.axis_size("px"), lax.axis_size("py"))
    corner_values = shape(12 * elem_rows, LANES)

    sources = [
        coords,
        displacement,
        contact_bucket.reshape(-1, LANES),
        contact_nodes.reshape(-1, LANES),
    ]
    inverse, outgoing = call(
        functools.partial(slots_kernel, devices, capacity),
        sources,
        [jax.ShapeDtypeStruct((slot_rows, LANES), I32), slots],
        "slots",
        far=range(4),
        scratch=[pltpu.VMEM(source.shape, source.dtype) for source in sources]
        + [pltpu.SemaphoreType.DMA((4,))],
        vmem_bytes=WHOLE_VMEM,
    )
    disp, lists, nodes, splat, *sends = call(
        functools.partial(halo_kernel, counts),
        [displacement, halo_lists, elem_nodes, stiffness, inverse],
        [
            nodal,
            jax.ShapeDtypeStruct((4 * quarter, LANES), I32),
            jax.ShapeDtypeStruct((4 * elem_rows, LANES), I32),
            shape(144, LANES),
        ]
        + sent,
        "halo",
        far=(4,),
    )
    coords, vel, ext, slow, select = call(
        rest_kernel,
        [coords, velocity, ext_force, block_class.reshape(1, -1), tile_pairs, lists],
        [nodal] * 3
        + [jax.ShapeDtypeStruct((elem_rows, LANES), I32), shape(2, LANES, LANES)],
        "rest",
        far=(5,),
    )
    for step_no in range(STEPS):
        for sub_no in range(SUBS):
            first = sub_no == 0
            last = sub_no == SUBS - 1
            final = last and step_no == STEPS - 1
            if first:
                arrived = swap(outgoing, devices, capacity)
                if step_no:
                    sends = call(sends_kernel, [disp, lists, outgoing], sent, "sends", far=(2,))
            recvs = exchange(sends)
            (found,) = call(own_kernel, [disp, nodes], [corner_values], "own_corners")
            field = [found, *recvs, nodes, thickness, splat]
            if first:
                (held,) = call(
                    functools.partial(force_kernel, rows), field, [corner_values], "forces"
                )
                (pushes,) = call(
                    functools.partial(contact_kernel, tile_pairs.shape[1]),
                    [select, arrived, held],
                    [slots],
                    "contact",
                    far=(2,),
                )
                returned = swap(pushes, devices, capacity)
                outs = call(
                    functools.partial(halo_sum_kernel, rows),
                    [held, nodes, pushes],
                    sent,
                    "halo_sum",
                    far=(2,),
                )
                forces = held
            else:
                forces, *outs = call(
                    functools.partial(later_kernel, rows),
                    field + [held, slow],
                    [corner_values] + sent,
                    "forces_halo_sum",
                )
            backs = exchange(outs)
            (own,) = call(own_sum_kernel, [forces, nodes, outs[0]], [nodal], "own_sum", far=(2,))
            state = [lists, ext, inv_mass, vel, disp]
            if first:
                (internal,) = call(
                    internal_kernel, [own, *backs, lists], [nodal], "internal"
                )
                vel, disp, contact, *sends = call(
                    first_update_kernel,
                    [internal, returned, inverse] + state,
                    [nodal] * 3 + sent,
                    "first_update",
                )
                continue
            inputs = [own, *backs] + state + [contact]
            if final:
                vel, disp = call(
                    functools.partial(update_kernel, "final"),
                    inputs,
                    [shape(3, rows * LANES)] * 2,
                    "final_update",
                )
            elif last:
                vel, disp, outgoing = call(
                    functools.partial(update_kernel, "last"),
                    inputs + [coords, inverse],
                    [nodal] * 2 + [slots],
                    "last_update",
                )
            else:
                vel, disp, *sends = call(
                    functools.partial(update_kernel, "inner"),
                    inputs,
                    [nodal] * 2 + sent,
                    "update",
                )
    return (disp, vel)


def solution(mesh):
    placed = (
        P(None, ("px", "py")),
        P(None, ("px", "py")),
        P(None, ("px", "py")),
        P(("px", "py")),
        P(None, ("px", "py")),
        P(("px", "py")),
        P(),
        P(None, ("px", "py")),
        P(("px", "py")),
        P(None, ("px", "py")),
        P(("px", "py")),
        P(("px", "py"), None),
        P(None, ("px", "py")),
    )
    return jax.shard_map(
        body,
        mesh=mesh,
        in_specs=placed,
        out_specs=(P(None, ("px", "py")), P(None, ("px", "py"))),
        check_vma=False,
    )
```

```python
import functools

import jax
import jax.numpy as jnp
from jax import lax
from jax.experimental import pallas as pl
from jax.experimental.pallas import tpu as pltpu
from jax.sharding import PartitionSpec as P

LANES = 128
EBLK = 128
STEPS = 2
SUBS = 2

FAR = 10000.0
DT = 0.05
PENALTY = 0.5
REACH = 4.0

F32 = jnp.float32
BF16 = jnp.bfloat16
I32 = jnp.int32

VMEM_BYTES = 32 * 1024 * 1024
WHOLE_VMEM = 64 * 1024 * 1024


def lookup(table_row, rows, index, start=None):
    parts = []
    for at in range(0, index.shape[0], 8):
        block = index[at : at + 8]
        hi = block >> 7
        lo = block & (LANES - 1)
        if start is None:
            found = [jnp.zeros(block.shape, F32) for _ in range(3)]
        else:
            found = [start[c][at : at + 8] for c in range(3)]
        for h in rows:
            here = hi == h
            for c in range(3):
                row = jnp.broadcast_to(table_row(c, h), block.shape)
                got = jnp.take_along_axis(row, lo, axis=1, mode="promise_in_bounds")
                found[c] = jnp.where(here, got, found[c])
        parts.append(found)
    return [jnp.concatenate([part[c] for part in parts], axis=0) for c in range(3)]


def halves(values):
    top = values.astype(BF16).astype(F32)
    return [top, values - top]


def scatter_dot(hi_rows, lo_rows, value_rows, rows, first=0):
    row_no = first + lax.broadcasted_iota(I32, (rows, LANES), 0)
    total = None
    lane_no = lax.broadcasted_iota(I32, (LANES, LANES), 0)
    group = 2
    for start in range(0, len(hi_rows), group):
        lefts, rights = [], []
        for r in range(start, start + group):
            here = row_no == hi_rows[r]
            lefts.append(
                jnp.concatenate(
                    [
                        jnp.where(here, jnp.broadcast_to(vals[r], (rows, LANES)), 0.0)
                        for vals in value_rows
                    ],
                    axis=0,
                ).astype(BF16)
            )
            rights.append((lane_no == lo_rows[r]).astype(F32).astype(BF16))
        part = lax.dot_general(
            jnp.concatenate(lefts, axis=1),
            jnp.concatenate(rights, axis=1),
            (((1,), (1,)), ((), ())),
            preferred_element_type=F32,
        )
        total = part if total is None else total + part
    return total


def scatter_add(index_row, value_row, count, rows, first=0):
    hi_rows, lo_rows = [], []
    value_rows = [[] for _ in range(6)]
    for r in range(count):
        idx = index_row(r)
        hi_rows.append(idx >> 7)
        lo_rows.append(idx & (LANES - 1))
        for c in range(3):
            for part, vals in enumerate(halves(value_row(c, r))):
                value_rows[2 * c + part].append(vals)
    total = scatter_dot(hi_rows, lo_rows, value_rows, rows, first)
    return [
        total[2 * c * rows : (2 * c + 1) * rows] + total[(2 * c + 1) * rows : (2 * c + 2) * rows]
        for c in range(3)
    ]


def spread_rows(source, target, groups):
    rows = source.shape[1] // LANES
    for g in range(groups):
        for h in range(rows):
            target[g * rows + h : g * rows + h + 1, :] = source[
                g : g + 1, h * LANES : (h + 1) * LANES
            ]


def gather_halo(disp, rows, lists, sends):
    found = lookup(lambda c, h: disp[c * rows + h : c * rows + h + 1, :], range(rows), lists[...])
    quarter = lists.shape[0] // 4
    for b in range(4):
        for c in range(3):
            sends[b][c * quarter : (c + 1) * quarter, :] = found[c][b * quarter : (b + 1) * quarter]


def gather_slots(position_row, rows, inverse, outgoing):
    slot_node = inverse[...]
    found = lookup(position_row, range(rows), jnp.maximum(slot_node, 0))
    for c in range(3):
        outgoing[:, c, :] = jnp.where(slot_node >= 0, found[c], FAR)


def block_remap(index, own_count, width, px_no, py_no, px_count, py_count):
    block = (index - own_count) >> (width.bit_length() - 1)
    along_x = block < 2
    place = jnp.where(along_x, px_no, py_no)
    ends = jnp.where(along_x, px_count - 1, py_count - 1)
    edge = jnp.where((block & 1) == 0, 0, ends)
    moved = index ^ ((1 - (place & 1)) * width)
    moved = jnp.where(place == edge, -1, moved)
    return jnp.where(index < own_count, index, moved)


def slots_kernel(devices, capacity, *refs):
    sources, (inverse, outgoing) = refs[:4], refs[4:6]
    buffers, sems = refs[6:10], refs[10]
    coords, disp, bucket, contact_nodes = buffers
    copies = [
        pltpu.make_async_copy(source, target, sems.at[n])
        for n, (source, target) in enumerate(zip(sources, buffers))
    ]
    for copy in copies:
        copy.start()
    for copy in copies[2:]:
        copy.wait()
    count = bucket.shape[0]
    slot_rows = inverse.shape[0]
    dev_no = lax.broadcasted_iota(I32, (devices, LANES), 0)
    first = lax.broadcasted_iota(I32, (LANES, 2 * LANES), 0)
    second = lax.broadcasted_iota(I32, (LANES, 2 * LANES), 1)
    before = ((first < second) | (second >= LANES)).astype(F32).astype(BF16)
    base = jnp.zeros((devices, LANES), F32)
    hi_rows, lo_rows, digits = [], [], [[], []]
    for r in range(count):
        b = bucket[r : r + 1, :]
        onehot = (dev_no == b).astype(F32)
        sums = jnp.dot(onehot.astype(BF16), before, preferred_element_type=F32)
        rank = jnp.sum(onehot * (sums[:, :LANES] + base), axis=0, keepdims=True)
        base = base + sums[:, LANES:]
        slot = b * capacity + rank.astype(I32)
        hi_rows.append(slot >> 7)
        lo_rows.append(slot & (LANES - 1))
        value = contact_nodes[r : r + 1, :] + 1
        digits[0].append((value >> 6).astype(F32))
        digits[1].append((value & 63).astype(F32))
    total = scatter_dot(hi_rows, lo_rows, digits, slot_rows)
    inverse[...] = (total[:slot_rows] * 64.0 + total[slot_rows:]).astype(I32) - 1
    for copy in copies[:2]:
        copy.wait()

    def position_row(c, h):
        span = slice(h * LANES, (h + 1) * LANES)
        return coords[c : c + 1, span] + disp[c : c + 1, span]

    gather_slots(position_row, coords.shape[1] // LANES, inverse, outgoing)


def halo_kernel(
    counts, disp_in, lists_in, nodes_in, stiff, after, disp, lists, nodes, splat, *sends
):
    px_no = lax.axis_index("px")
    py_no = lax.axis_index("py")
    own_count = disp_in.shape[1]
    rows = own_count // LANES
    spread_rows(disp_in, disp, 3)
    width = lists_in.shape[1]
    quarter = width // LANES
    for b in range(4):
        place = px_no if b < 2 else py_no
        count = counts[b // 2]
        to_high = (place & 1) ^ (1 - b % 2)
        row = (b // 2) * 2
        missing = (place == to_high * (count - 1)).astype(I32)
        for q in range(quarter):
            span = slice(q * LANES, (q + 1) * LANES)
            chosen = jnp.where(
                jnp.full((1, LANES), to_high) == 1,
                lists_in[row + 1 : row + 2, span],
                lists_in[row : row + 1, span],
            )
            lists[b * quarter + q : b * quarter + q + 1, :] = jnp.where(
                jnp.full((1, LANES), missing) == 1, -1, chosen
            )
    gather_halo(disp, rows, lists, sends)
    spread_rows(nodes_in, nodes, 4)
    nodes[...] = block_remap(nodes[...], own_count, width, px_no, py_no, *counts)
    size = stiff.shape[0]
    for j in range(size):
        splat[j * size : (j + 1) * size, :] = jnp.broadcast_to(stiff[:, j : j + 1], (size, LANES))


def rest_kernel(coords_in, vel_in, ext_in, classes, pairs, after, coords, vel, ext, slow, select):
    spread_rows(coords_in, coords, 3)
    spread_rows(vel_in, vel, 3)
    spread_rows(ext_in, ext, 3)
    blocks = classes.shape[1]
    row = jnp.concatenate([classes[...], jnp.zeros((1, LANES - blocks), I32)], axis=1)
    slow[...] = jnp.transpose(jnp.broadcast_to(row, (LANES, LANES)))[:blocks]
    ends = [pairs[0:1, :], pairs[1:2, :]]
    short = LANES - 2 * pairs.shape[1]
    if short:
        ends.append(jnp.full((1, short), -1))
    tile_no = lax.broadcasted_iota(I32, (LANES, LANES), 0)
    onehot = (tile_no == jnp.concatenate(ends, axis=1)).astype(F32)
    select[0] = onehot
    select[1] = jnp.transpose(onehot)


def own_kernel(disp, nodes, found):
    rows = disp.shape[0] // 3
    count = nodes.shape[0]
    values = lookup(
        lambda c, h: disp[c * rows + h : c * rows + h + 1, :], range(rows), nodes[...]
    )
    for c in range(3):
        found[c * count : (c + 1) * count, :] = values[c]


def corner_forces(found, rows, recvs, nodes, thick, splat):
    quarter = recvs[0].shape[0] // 3
    elem_rows = thick.shape[0]

    def table_row(c, h):
        b, q = divmod(h - rows, quarter)
        return recvs[b][c * quarter + q : c * quarter + q + 1, :]

    count = nodes.shape[0]
    corners = []
    for k in range(4):
        span = slice(k * elem_rows, (k + 1) * elem_rows)
        own = [found[c * count + span.start : c * count + span.stop, :] for c in range(3)]
        corners.append(
            lookup(table_row, range(rows, rows + 4 * quarter), nodes[span, :], own)
        )
    factor = thick[...]
    forces = []
    for i in range(12):
        total = None
        for j in range(12):
            term = splat[j * 12 + i : j * 12 + i + 1, :] * corners[j % 4][j // 4]
            total = term if total is None else total + term
        forces.append(factor * total)
    return forces


def stored_row(forces, nodes):
    count = nodes.shape[0]
    return lambda c, r: forces[c * count + r : c * count + r + 1, :]


def sum_own(force_row, nodes, own):
    rows = own.shape[0] // 3
    sums = scatter_add(lambda r: nodes[r : r + 1, :], force_row, nodes.shape[0], rows)
    for c in range(3):
        own[c * rows : (c + 1) * rows, :] = sums[c]


def sum_halo(force_row, nodes, rows, outs):
    quarter = outs[0].shape[0] // 3
    sums = scatter_add(
        lambda r: nodes[r : r + 1, :], force_row, nodes.shape[0], 4 * quarter, rows
    )
    for c in range(3):
        for b in range(4):
            outs[b][c * quarter : (c + 1) * quarter, :] = sums[c][b * quarter : (b + 1) * quarter]


def force_kernel(rows, found, recv1, recv3, recv0, recv2, nodes, thick, splat, held):
    elem_rows = thick.shape[0]
    forces = corner_forces(found, rows, (recv0, recv1, recv2, recv3), nodes, thick, splat)
    for i in range(12):
        held[i * elem_rows : (i + 1) * elem_rows, :] = forces[i]


def halo_sum_kernel(rows, held, nodes, after, *outs):
    sum_halo(stored_row(held, nodes), nodes, rows, outs)


def own_sum_kernel(held, nodes, after, own):
    sum_own(stored_row(held, nodes), nodes, own)


def later_kernel(
    rows,
    found,
    recv1,
    recv3,
    recv0,
    recv2,
    nodes,
    thick,
    splat,
    held,
    slow,
    mixed,
    *outs,
):
    elem_rows = thick.shape[0]
    forces = corner_forces(found, rows, (recv0, recv1, recv2, recv3), nodes, thick, splat)
    kept = slow[...] == 1
    for i in range(12):
        span = slice(i * elem_rows, (i + 1) * elem_rows)
        forces[i] = jnp.where(kept, held[span, :], forces[i])
        mixed[span, :] = forces[i]

    def force_row(c, r):
        k, h = divmod(r, elem_rows)
        return forces[c * 4 + k][h : h + 1, :]

    sum_halo(force_row, nodes, rows, outs)


def returned_sums(backs, lists, rows):
    quarter = backs[0].shape[0] // 3

    def back_row(c, r):
        b, q = divmod(r, quarter)
        return backs[b][c * quarter + q : c * quarter + q + 1, :]

    return scatter_add(lambda r: lists[r : r + 1, :], back_row, 4 * quarter, rows)


def internal_kernel(own, back1, back3, back0, back2, lists, internal):
    rows = own.shape[0] // 3
    sums = returned_sums((back0, back1, back2, back3), lists, rows)
    for c in range(3):
        span = slice(c * rows, (c + 1) * rows)
        internal[span, :] = own[span, :] + sums[c]


def sends_kernel(disp, lists, after, *sends):
    gather_halo(disp, disp.shape[0] // 3, lists, sends)


def thirds(values):
    parts = []
    for _ in range(3):
        top = values.astype(BF16)
        parts.append(top)
        values = values - top.astype(F32)
    return jnp.concatenate(parts, axis=1)


def dot_thirds(onehot, values):
    width = values.shape[1]
    sums = jnp.dot(onehot.astype(BF16), thirds(values), preferred_element_type=F32)
    return sums[:, :width] + sums[:, width : 2 * width] + sums[:, 2 * width :]


def contact_kernel(pair_count, select, arrived, after, pushes):
    tiles = arrived.shape[0]
    points = jnp.concatenate([arrived[:, c, :] for c in range(3)], axis=1)
    picked = dot_thirds(select[1, : 2 * pair_count, :tiles], points)
    first, second = picked[:pair_count], picked[pair_count:]
    group = LANES // 4
    pushed = []
    for start in range(0, pair_count, group):
        stop = min(start + group, pair_count)
        block = jnp.concatenate(
            [second[start:stop, c * LANES : (c + 1) * LANES] for c in range(3)]
            + [jnp.zeros((LANES - 3 * (stop - start), LANES), F32)],
            axis=0,
        )
        turned = jnp.transpose(block)
        for p in range(start, stop):
            gaps = []
            for c in range(3):
                column = c * (stop - start) + p - start
                gaps.append(
                    jnp.broadcast_to(
                        first[p : p + 1, c * LANES : (c + 1) * LANES], (LANES, LANES)
                    )
                    - jnp.broadcast_to(turned[:, column : column + 1], (LANES, LANES))
                )
            dist = gaps[0] * gaps[0] + gaps[1] * gaps[1] + gaps[2] * gaps[2]
            weight = jnp.exp(dist * (-1.0 / REACH))
            pushed.append(
                jnp.concatenate(
                    [jnp.sum(weight * gaps[c], axis=0, keepdims=True) for c in range(3)], axis=1
                )
            )
    total = PENALTY * dot_thirds(select[0, :tiles, :pair_count], jnp.concatenate(pushed, axis=0))
    for c in range(3):
        pushes[:, c, :] = total[:, c * LANES : (c + 1) * LANES]


def advance(internal, contact, ext, inv_mass, vel, disp, rows):
    for c in range(3):
        span = slice(c * rows, (c + 1) * rows)
        accel = inv_mass[...] * (ext[span, :] - internal[c] + contact[c])
        vel_c = vel[span, :] + DT * accel
        yield c, vel_c, disp[span, :] + DT * vel_c


def components(array):
    rows = array.shape[0] // 3
    return [array[c * rows : (c + 1) * rows, :] for c in range(3)]


def first_update_kernel(
    internal, returned, inverse, lists, ext, inv_mass, vel, disp, new_vel, new_disp, contact, *sends
):
    rows = disp.shape[0] // 3
    sums = scatter_add(
        lambda r: inverse[r : r + 1, :],
        lambda c, r: returned[r, c : c + 1, :],
        inverse.shape[0],
        rows,
    )
    steps = advance(components(internal), sums, ext, inv_mass, vel, disp, rows)
    for c, vel_c, disp_c in steps:
        span = slice(c * rows, (c + 1) * rows)
        contact[span, :] = sums[c]
        new_vel[span, :] = vel_c
        new_disp[span, :] = disp_c
    gather_halo(new_disp, rows, lists, sends)


def update_kernel(case, *refs):
    refs = list(refs)
    own, back1, back3, back0, back2, lists, ext, inv_mass, vel, disp, contact = refs[:11]
    rows = disp.shape[0] // 3
    sums = returned_sums((back0, back1, back2, back3), lists, rows)
    internal = [mine + more for mine, more in zip(components(own), sums)]
    steps = advance(internal, components(contact), ext, inv_mass, vel, disp, rows)
    if case == "final":
        new_vel, new_disp = refs[11:]
        for c, vel_c, disp_c in steps:
            for h in range(rows):
                new_vel[c : c + 1, h * LANES : (h + 1) * LANES] = vel_c[h : h + 1, :]
                new_disp[c : c + 1, h * LANES : (h + 1) * LANES] = disp_c[h : h + 1, :]
        return
    if case == "last":
        coords, inverse, new_vel, new_disp, outgoing = refs[11:]
    else:
        new_vel, new_disp, *sends = refs[11:]
    for c, vel_c, disp_c in steps:
        new_vel[c * rows : (c + 1) * rows, :] = vel_c
        new_disp[c * rows : (c + 1) * rows, :] = disp_c
    if case == "last":

        def position_row(c, h):
            span = slice(c * rows + h, c * rows + h + 1)
            return coords[span, :] + new_disp[span, :]

        gather_slots(position_row, rows, inverse, outgoing)
    else:
        gather_halo(new_disp, rows, lists, sends)


def vmem(count):
    return [pl.BlockSpec(memory_space=pltpu.VMEM)] * count


def shape(*dims):
    return jax.ShapeDtypeStruct(dims, F32)


def call(kernel, inputs, outputs, name, smem=(), far=(), scratch=(), vmem_bytes=VMEM_BYTES):
    specs = [
        pl.BlockSpec(
            memory_space=pltpu.SMEM if i in smem else pl.ANY if i in far else pltpu.VMEM
        )
        for i in range(len(inputs))
    ]
    return pl.pallas_call(
        kernel,
        out_shape=tuple(outputs),
        in_specs=specs,
        out_specs=tuple(vmem(len(outputs))),
        scratch_shapes=list(scratch),
        compiler_params=pltpu.CompilerParams(vmem_limit_bytes=vmem_bytes),
        name=name,
    )(*inputs)


def partners():
    px, py = lax.axis_size("px"), lax.axis_size("py")
    number = lambda i, j: i * py + j
    swaps = [[] for _ in range(4)]
    for i in range(px):
        for j in range(py):
            me = number(i, j)
            swaps[0].append((me, number(i ^ 1, j)))
            other = i - 1 if i % 2 == 0 else i + 1
            swaps[1].append((me, number(other, j) if 0 <= other < px else number(i, j ^ 1)))
            swaps[2].append((me, number(i, j ^ 1)))
            other = j - 1 if j % 2 == 0 else j + 1
            swaps[3].append((me, number(i, other % py)))
    return swaps


def exchange(blocks):
    swaps = partners()
    return [lax.ppermute(blocks[n], ("px", "py"), swaps[n]) for n in (1, 3, 0, 2)]


def swap(slots, devices, capacity):
    axes = ("px", "py")
    if capacity == LANES:
        return lax.all_to_all(slots, axes, 0, 0, tiled=True)
    ratio = LANES // capacity
    parts = jnp.transpose(slots.reshape(-1, 3, ratio, capacity), (0, 2, 1, 3)).reshape(
        devices, 3, capacity
    )
    moved = lax.all_to_all(parts, axes, 0, 0, tiled=True)
    return jnp.transpose(moved.reshape(-1, ratio, 3, capacity), (0, 2, 1, 3)).reshape(
        -1, 3, LANES
    )


def body(
    coords,
    displacement,
    velocity,
    inv_mass,
    ext_force,
    thickness,
    stiffness,
    elem_nodes,
    block_class,
    halo_lists,
    contact_nodes,
    contact_bucket,
    tile_pairs,
):
    rows = coords.shape[1] // LANES
    quarter = halo_lists.shape[1] // LANES
    elem_rows = elem_nodes.shape[1] // LANES
    devices = lax.axis_size("px") * lax.axis_size("py")
    capacity = 2 * contact_nodes.shape[0] // devices
    slot_rows = devices * capacity // LANES
    inv_mass = inv_mass.reshape(rows, LANES)
    thickness = thickness.reshape(elem_rows, LANES)
    nodal = shape(3 * rows, LANES)
    sent = [shape(3 * quarter, LANES)] * 4
    slots = shape(slot_rows, 3, LANES)

    counts = (lax.axis_size("px"), lax.axis_size("py"))
    corner_values = shape(12 * elem_rows, LANES)

    sources = [
        coords,
        displacement,
        contact_bucket.reshape(-1, LANES),
        contact_nodes.reshape(-1, LANES),
    ]
    inverse, outgoing = call(
        functools.partial(slots_kernel, devices, capacity),
        sources,
        [jax.ShapeDtypeStruct((slot_rows, LANES), I32), slots],
        "slots",
        far=range(4),
        scratch=[pltpu.VMEM(source.shape, source.dtype) for source in sources]
        + [pltpu.SemaphoreType.DMA((4,))],
        vmem_bytes=WHOLE_VMEM,
    )
    disp, lists, nodes, splat, *sends = call(
        functools.partial(halo_kernel, counts),
        [displacement, halo_lists, elem_nodes, stiffness, inverse],
        [
            nodal,
            jax.ShapeDtypeStruct((4 * quarter, LANES), I32),
            jax.ShapeDtypeStruct((4 * elem_rows, LANES), I32),
            shape(144, LANES),
        ]
        + sent,
        "halo",
        far=(4,),
    )
    coords, vel, ext, slow, select = call(
        rest_kernel,
        [coords, velocity, ext_force, block_class.reshape(1, -1), tile_pairs, lists],
        [nodal] * 3
        + [jax.ShapeDtypeStruct((elem_rows, LANES), I32), shape(2, LANES, LANES)],
        "rest",
        far=(5,),
    )
    for step_no in range(STEPS):
        for sub_no in range(SUBS):
            first = sub_no == 0
            last = sub_no == SUBS - 1
            final = last and step_no == STEPS - 1
            if first:
                arrived = swap(outgoing, devices, capacity)
                if step_no:
                    sends = call(sends_kernel, [disp, lists, outgoing], sent, "sends", far=(2,))
            recvs = exchange(sends)
            (found,) = call(own_kernel, [disp, nodes], [corner_values], "own_corners")
            field = [found, *recvs, nodes, thickness, splat]
            if first:
                (held,) = call(
                    functools.partial(force_kernel, rows), field, [corner_values], "forces"
                )
                (pushes,) = call(
                    functools.partial(contact_kernel, tile_pairs.shape[1]),
                    [select, arrived, held],
                    [slots],
                    "contact",
                    far=(2,),
                )
                returned = swap(pushes, devices, capacity)
                outs = call(
                    functools.partial(halo_sum_kernel, rows),
                    [held, nodes, pushes],
                    sent,
                    "halo_sum",
                    far=(2,),
                )
                forces = held
            else:
                forces, *outs = call(
                    functools.partial(later_kernel, rows),
                    field + [held, slow],
                    [corner_values] + sent,
                    "forces_halo_sum",
                )
            backs = exchange(outs)
            (own,) = call(own_sum_kernel, [forces, nodes, outs[2]], [nodal], "own_sum", far=(2,))
            state = [lists, ext, inv_mass, vel, disp]
            if first:
                (internal,) = call(
                    internal_kernel, [own, *backs, lists], [nodal], "internal"
                )
                vel, disp, contact, *sends = call(
                    first_update_kernel,
                    [internal, returned, inverse] + state,
                    [nodal] * 3 + sent,
                    "first_update",
                )
                continue
            inputs = [own, *backs] + state + [contact]
            if final:
                vel, disp = call(
                    functools.partial(update_kernel, "final"),
                    inputs,
                    [shape(3, rows * LANES)] * 2,
                    "final_update",
                )
            elif last:
                vel, disp, outgoing = call(
                    functools.partial(update_kernel, "last"),
                    inputs + [coords, inverse],
                    [nodal] * 2 + [slots],
                    "last_update",
                )
            else:
                vel, disp, *sends = call(
                    functools.partial(update_kernel, "inner"),
                    inputs,
                    [nodal] * 2 + sent,
                    "update",
                )
    return (disp, vel)


def solution(mesh):
    placed = (
        P(None, ("px", "py")),
        P(None, ("px", "py")),
        P(None, ("px", "py")),
        P(("px", "py")),
        P(None, ("px", "py")),
        P(("px", "py")),
        P(),
        P(None, ("px", "py")),
        P(("px", "py")),
        P(None, ("px", "py")),
        P(("px", "py")),
        P(("px", "py"), None),
        P(None, ("px", "py")),
    )
    return jax.shard_map(
        body,
        mesh=mesh,
        in_specs=placed,
        out_specs=(P(None, ("px", "py")), P(None, ("px", "py"))),
        check_vma=False,
    )
```

```python
import functools

import jax
import jax.numpy as jnp
from jax import lax
from jax.experimental import pallas as pl
from jax.experimental.pallas import tpu as pltpu
from jax.sharding import PartitionSpec as P

LANES = 128
EBLK = 128
STEPS = 2
SUBS = 2

FAR = 10000.0
DT = 0.05
PENALTY = 0.5
REACH = 4.0

F32 = jnp.float32
BF16 = jnp.bfloat16
I32 = jnp.int32

VMEM_BYTES = 32 * 1024 * 1024
WHOLE_VMEM = 64 * 1024 * 1024


def lookup(table_row, rows, index, start=None):
    parts = []
    for at in range(0, index.shape[0], 8):
        block = index[at : at + 8]
        hi = block >> 7
        lo = block & (LANES - 1)
        if start is None:
            found = [jnp.zeros(block.shape, F32) for _ in range(3)]
        else:
            found = [start[c][at : at + 8] for c in range(3)]
        for h in rows:
            here = hi == h
            for c in range(3):
                row = jnp.broadcast_to(table_row(c, h), block.shape)
                got = jnp.take_along_axis(row, lo, axis=1, mode="promise_in_bounds")
                found[c] = jnp.where(here, got, found[c])
        parts.append(found)
    return [jnp.concatenate([part[c] for part in parts], axis=0) for c in range(3)]


def halves(values):
    top = values.astype(BF16).astype(F32)
    return [top, values - top]


def scatter_dot(hi_rows, lo_rows, value_rows, rows, first=0):
    row_no = first + lax.broadcasted_iota(I32, (rows, LANES), 0)
    total = None
    lane_no = lax.broadcasted_iota(I32, (LANES, LANES), 0)
    group = 2
    for start in range(0, len(hi_rows), group):
        lefts, rights = [], []
        for r in range(start, start + group):
            here = row_no == hi_rows[r]
            lefts.append(
                jnp.concatenate(
                    [
                        jnp.where(here, jnp.broadcast_to(vals[r], (rows, LANES)), 0.0)
                        for vals in value_rows
                    ],
                    axis=0,
                ).astype(BF16)
            )
            rights.append((lane_no == lo_rows[r]).astype(F32).astype(BF16))
        part = lax.dot_general(
            jnp.concatenate(lefts, axis=1),
            jnp.concatenate(rights, axis=1),
            (((1,), (1,)), ((), ())),
            preferred_element_type=F32,
        )
        total = part if total is None else total + part
    return total


def scatter_add(index_row, value_row, count, rows, first=0):
    hi_rows, lo_rows = [], []
    value_rows = [[] for _ in range(6)]
    for r in range(count):
        idx = index_row(r)
        hi_rows.append(idx >> 7)
        lo_rows.append(idx & (LANES - 1))
        for c in range(3):
            for part, vals in enumerate(halves(value_row(c, r))):
                value_rows[2 * c + part].append(vals)
    total = scatter_dot(hi_rows, lo_rows, value_rows, rows, first)
    return [
        total[2 * c * rows : (2 * c + 1) * rows] + total[(2 * c + 1) * rows : (2 * c + 2) * rows]
        for c in range(3)
    ]


def spread_rows(source, target, groups):
    rows = source.shape[1] // LANES
    for g in range(groups):
        for h in range(rows):
            target[g * rows + h : g * rows + h + 1, :] = source[
                g : g + 1, h * LANES : (h + 1) * LANES
            ]


def gather_halo(disp, rows, lists, sends):
    found = lookup(lambda c, h: disp[c * rows + h : c * rows + h + 1, :], range(rows), lists[...])
    quarter = lists.shape[0] // 4
    for b in range(4):
        for c in range(3):
            sends[b][c * quarter : (c + 1) * quarter, :] = found[c][b * quarter : (b + 1) * quarter]


def gather_slots(position_row, rows, inverse, outgoing):
    slot_node = inverse[...]
    found = lookup(position_row, range(rows), jnp.maximum(slot_node, 0))
    for c in range(3):
        outgoing[:, c, :] = jnp.where(slot_node >= 0, found[c], FAR)


def block_remap(index, own_count, width, px_no, py_no, px_count, py_count):
    block = (index - own_count) >> (width.bit_length() - 1)
    along_x = block < 2
    place = jnp.where(along_x, px_no, py_no)
    ends = jnp.where(along_x, px_count - 1, py_count - 1)
    edge = jnp.where((block & 1) == 0, 0, ends)
    moved = index ^ ((1 - (place & 1)) * width)
    moved = jnp.where(place == edge, -1, moved)
    return jnp.where(index < own_count, index, moved)


def slots_kernel(devices, capacity, *refs):
    sources, (inverse, outgoing) = refs[:4], refs[4:6]
    buffers, sems = refs[6:10], refs[10]
    coords, disp, bucket, contact_nodes = buffers
    copies = [
        pltpu.make_async_copy(source, target, sems.at[n])
        for n, (source, target) in enumerate(zip(sources, buffers))
    ]
    for copy in copies:
        copy.start()
    for copy in copies[2:]:
        copy.wait()
    count = bucket.shape[0]
    slot_rows = inverse.shape[0]
    dev_no = lax.broadcasted_iota(I32, (devices, LANES), 0)
    first = lax.broadcasted_iota(I32, (LANES, 2 * LANES), 0)
    second = lax.broadcasted_iota(I32, (LANES, 2 * LANES), 1)
    before = ((first < second) | (second >= LANES)).astype(F32).astype(BF16)
    base = jnp.zeros((devices, LANES), F32)
    hi_rows, lo_rows, digits = [], [], [[], []]
    for r in range(count):
        b = bucket[r : r + 1, :]
        onehot = (dev_no == b).astype(F32)
        sums = jnp.dot(onehot.astype(BF16), before, preferred_element_type=F32)
        rank = jnp.sum(onehot * (sums[:, :LANES] + base), axis=0, keepdims=True)
        base = base + sums[:, LANES:]
        slot = b * capacity + rank.astype(I32)
        hi_rows.append(slot >> 7)
        lo_rows.append(slot & (LANES - 1))
        value = contact_nodes[r : r + 1, :] + 1
        digits[0].append((value >> 6).astype(F32))
        digits[1].append((value & 63).astype(F32))
    total = scatter_dot(hi_rows, lo_rows, digits, slot_rows)
    inverse[...] = (total[:slot_rows] * 64.0 + total[slot_rows:]).astype(I32) - 1
    for copy in copies[:2]:
        copy.wait()

    def position_row(c, h):
        span = slice(h * LANES, (h + 1) * LANES)
        return coords[c : c + 1, span] + disp[c : c + 1, span]

    gather_slots(position_row, coords.shape[1] // LANES, inverse, outgoing)


def prepare_kernel(counts, *refs):
    (disp_in, lists_in, nodes_in, stiff, coords_in, vel_in, ext_in) = refs[:7]
    (classes, pairs, thick_in, mass_in, after) = refs[7:12]
    (disp, lists, nodes, splat, coords, vel, ext, slow, select, thick, mass) = refs[12:23]
    sends = refs[23:]
    px_no = lax.axis_index("px")
    py_no = lax.axis_index("py")
    own_count = disp_in.shape[1]
    rows = own_count // LANES
    spread_rows(disp_in, disp, 3)
    width = lists_in.shape[1]
    quarter = width // LANES
    for b in range(4):
        place = px_no if b < 2 else py_no
        count = counts[b // 2]
        to_high = (place & 1) ^ (1 - b % 2)
        row = (b // 2) * 2
        missing = (place == to_high * (count - 1)).astype(I32)
        for q in range(quarter):
            span = slice(q * LANES, (q + 1) * LANES)
            chosen = jnp.where(
                jnp.full((1, LANES), to_high) == 1,
                lists_in[row + 1 : row + 2, span],
                lists_in[row : row + 1, span],
            )
            lists[b * quarter + q : b * quarter + q + 1, :] = jnp.where(
                jnp.full((1, LANES), missing) == 1, -1, chosen
            )
    gather_halo(disp, rows, lists, sends)
    spread_rows(nodes_in, nodes, 4)
    nodes[...] = block_remap(nodes[...], own_count, width, px_no, py_no, *counts)
    size = stiff.shape[0]
    for j in range(size):
        splat[j * size : (j + 1) * size, :] = jnp.broadcast_to(stiff[:, j : j + 1], (size, LANES))
    spread_rows(coords_in, coords, 3)
    spread_rows(vel_in, vel, 3)
    spread_rows(ext_in, ext, 3)
    blocks = classes.shape[1]
    row = jnp.concatenate([classes[...], jnp.zeros((1, LANES - blocks), I32)], axis=1)
    slow[...] = jnp.transpose(jnp.broadcast_to(row, (LANES, LANES)))[:blocks]
    ends = [pairs[0:1, :], pairs[1:2, :]]
    short = LANES - 2 * pairs.shape[1]
    if short:
        ends.append(jnp.full((1, short), -1))
    tile_no = lax.broadcasted_iota(I32, (LANES, LANES), 0)
    onehot = (tile_no == jnp.concatenate(ends, axis=1)).astype(F32)
    select[0] = onehot
    select[1] = jnp.transpose(onehot)
    thick[...] = thick_in[...]
    mass[...] = mass_in[...]


def own_kernel(disp, nodes, found):
    rows = disp.shape[0] // 3
    count = nodes.shape[0]
    values = lookup(
        lambda c, h: disp[c * rows + h : c * rows + h + 1, :], range(rows), nodes[...]
    )
    for c in range(3):
        found[c * count : (c + 1) * count, :] = values[c]


def corner_forces(found, rows, recvs, nodes, thick, splat):
    quarter = recvs[0].shape[0] // 3
    elem_rows = thick.shape[0]

    def table_row(c, h):
        b, q = divmod(h - rows, quarter)
        return recvs[b][c * quarter + q : c * quarter + q + 1, :]

    count = nodes.shape[0]
    corners = []
    for k in range(4):
        span = slice(k * elem_rows, (k + 1) * elem_rows)
        own = [found[c * count + span.start : c * count + span.stop, :] for c in range(3)]
        corners.append(
            lookup(table_row, range(rows, rows + 4 * quarter), nodes[span, :], own)
        )
    factor = thick[...]
    forces = []
    for i in range(12):
        total = None
        for j in range(12):
            term = splat[j * 12 + i : j * 12 + i + 1, :] * corners[j % 4][j // 4]
            total = term if total is None else total + term
        forces.append(factor * total)
    return forces


def stored_row(forces, nodes):
    count = nodes.shape[0]
    return lambda c, r: forces[c * count + r : c * count + r + 1, :]


def sum_own(force_row, nodes, own):
    rows = own.shape[0] // 3
    sums = scatter_add(lambda r: nodes[r : r + 1, :], force_row, nodes.shape[0], rows)
    for c in range(3):
        own[c * rows : (c + 1) * rows, :] = sums[c]


def sum_halo(force_row, nodes, rows, outs):
    quarter = outs[0].shape[0] // 3
    sums = scatter_add(
        lambda r: nodes[r : r + 1, :], force_row, nodes.shape[0], 4 * quarter, rows
    )
    for c in range(3):
        for b in range(4):
            outs[b][c * quarter : (c + 1) * quarter, :] = sums[c][b * quarter : (b + 1) * quarter]


def force_kernel(rows, found, recv1, recv3, recv0, recv2, nodes, thick, splat, held):
    elem_rows = thick.shape[0]
    forces = corner_forces(found, rows, (recv0, recv1, recv2, recv3), nodes, thick, splat)
    for i in range(12):
        held[i * elem_rows : (i + 1) * elem_rows, :] = forces[i]


def halo_sum_kernel(rows, held, nodes, after, *outs):
    sum_halo(stored_row(held, nodes), nodes, rows, outs)


def own_sum_kernel(held, nodes, after, own):
    sum_own(stored_row(held, nodes), nodes, own)


def later_kernel(
    rows,
    found,
    recv1,
    recv3,
    recv0,
    recv2,
    nodes,
    thick,
    splat,
    held,
    slow,
    mixed,
    *outs,
):
    elem_rows = thick.shape[0]
    forces = corner_forces(found, rows, (recv0, recv1, recv2, recv3), nodes, thick, splat)
    kept = slow[...] == 1
    for i in range(12):
        span = slice(i * elem_rows, (i + 1) * elem_rows)
        forces[i] = jnp.where(kept, held[span, :], forces[i])
        mixed[span, :] = forces[i]

    def force_row(c, r):
        k, h = divmod(r, elem_rows)
        return forces[c * 4 + k][h : h + 1, :]

    sum_halo(force_row, nodes, rows, outs)


def returned_sums(backs, lists, rows):
    quarter = backs[0].shape[0] // 3

    def back_row(c, r):
        b, q = divmod(r, quarter)
        return backs[b][c * quarter + q : c * quarter + q + 1, :]

    return scatter_add(lambda r: lists[r : r + 1, :], back_row, 4 * quarter, rows)


def internal_kernel(own, back1, back3, back0, back2, lists, internal):
    rows = own.shape[0] // 3
    sums = returned_sums((back0, back1, back2, back3), lists, rows)
    for c in range(3):
        span = slice(c * rows, (c + 1) * rows)
        internal[span, :] = own[span, :] + sums[c]


def sends_kernel(disp, lists, after, *sends):
    gather_halo(disp, disp.shape[0] // 3, lists, sends)


def thirds(values):
    parts = []
    for _ in range(3):
        top = values.astype(BF16)
        parts.append(top)
        values = values - top.astype(F32)
    return jnp.concatenate(parts, axis=1)


def dot_thirds(onehot, values):
    width = values.shape[1]
    sums = jnp.dot(onehot.astype(BF16), thirds(values), preferred_element_type=F32)
    return sums[:, :width] + sums[:, width : 2 * width] + sums[:, 2 * width :]


def contact_kernel(pair_count, select, arrived, after, pushes):
    tiles = arrived.shape[0]
    points = jnp.concatenate([arrived[:, c, :] for c in range(3)], axis=1)
    picked = dot_thirds(select[1, : 2 * pair_count, :tiles], points)
    first, second = picked[:pair_count], picked[pair_count:]
    group = LANES // 4
    pushed = []
    for start in range(0, pair_count, group):
        stop = min(start + group, pair_count)
        block = jnp.concatenate(
            [second[start:stop, c * LANES : (c + 1) * LANES] for c in range(3)]
            + [jnp.zeros((LANES - 3 * (stop - start), LANES), F32)],
            axis=0,
        )
        turned = jnp.transpose(block)
        for p in range(start, stop):
            gaps = []
            for c in range(3):
                column = c * (stop - start) + p - start
                gaps.append(
                    jnp.broadcast_to(
                        first[p : p + 1, c * LANES : (c + 1) * LANES], (LANES, LANES)
                    )
                    - jnp.broadcast_to(turned[:, column : column + 1], (LANES, LANES))
                )
            dist = gaps[0] * gaps[0] + gaps[1] * gaps[1] + gaps[2] * gaps[2]
            weight = jnp.exp(dist * (-1.0 / REACH))
            pushed.append(
                jnp.concatenate(
                    [jnp.sum(weight * gaps[c], axis=0, keepdims=True) for c in range(3)], axis=1
                )
            )
    total = PENALTY * dot_thirds(select[0, :tiles, :pair_count], jnp.concatenate(pushed, axis=0))
    for c in range(3):
        pushes[:, c, :] = total[:, c * LANES : (c + 1) * LANES]


def advance(internal, contact, ext, inv_mass, vel, disp, rows):
    for c in range(3):
        span = slice(c * rows, (c + 1) * rows)
        accel = inv_mass[...] * (ext[span, :] - internal[c] + contact[c])
        vel_c = vel[span, :] + DT * accel
        yield c, vel_c, disp[span, :] + DT * vel_c


def components(array):
    rows = array.shape[0] // 3
    return [array[c * rows : (c + 1) * rows, :] for c in range(3)]


def first_update_kernel(
    internal, returned, inverse, lists, ext, inv_mass, vel, disp, new_vel, new_disp, contact, *sends
):
    rows = disp.shape[0] // 3
    sums = scatter_add(
        lambda r: inverse[r : r + 1, :],
        lambda c, r: returned[r, c : c + 1, :],
        inverse.shape[0],
        rows,
    )
    steps = advance(components(internal), sums, ext, inv_mass, vel, disp, rows)
    for c, vel_c, disp_c in steps:
        span = slice(c * rows, (c + 1) * rows)
        contact[span, :] = sums[c]
        new_vel[span, :] = vel_c
        new_disp[span, :] = disp_c
    gather_halo(new_disp, rows, lists, sends)


def update_kernel(case, *refs):
    refs = list(refs)
    own, back1, back3, back0, back2, lists, ext, inv_mass, vel, disp, contact = refs[:11]
    rows = disp.shape[0] // 3
    sums = returned_sums((back0, back1, back2, back3), lists, rows)
    internal = [mine + more for mine, more in zip(components(own), sums)]
    steps = advance(internal, components(contact), ext, inv_mass, vel, disp, rows)
    if case == "final":
        new_vel, new_disp = refs[11:]
        for c, vel_c, disp_c in steps:
            for h in range(rows):
                new_vel[c : c + 1, h * LANES : (h + 1) * LANES] = vel_c[h : h + 1, :]
                new_disp[c : c + 1, h * LANES : (h + 1) * LANES] = disp_c[h : h + 1, :]
        return
    if case == "last":
        coords, inverse, new_vel, new_disp, outgoing = refs[11:]
    else:
        new_vel, new_disp, *sends = refs[11:]
    for c, vel_c, disp_c in steps:
        new_vel[c * rows : (c + 1) * rows, :] = vel_c
        new_disp[c * rows : (c + 1) * rows, :] = disp_c
    if case == "last":

        def position_row(c, h):
            span = slice(c * rows + h, c * rows + h + 1)
            return coords[span, :] + new_disp[span, :]

        gather_slots(position_row, rows, inverse, outgoing)
    else:
        gather_halo(new_disp, rows, lists, sends)


def vmem(count):
    return [pl.BlockSpec(memory_space=pltpu.VMEM)] * count


def shape(*dims):
    return jax.ShapeDtypeStruct(dims, F32)


def call(kernel, inputs, outputs, name, smem=(), far=(), scratch=(), vmem_bytes=VMEM_BYTES):
    specs = [
        pl.BlockSpec(
            memory_space=pltpu.SMEM if i in smem else pl.ANY if i in far else pltpu.VMEM
        )
        for i in range(len(inputs))
    ]
    return pl.pallas_call(
        kernel,
        out_shape=tuple(outputs),
        in_specs=specs,
        out_specs=tuple(vmem(len(outputs))),
        scratch_shapes=list(scratch),
        compiler_params=pltpu.CompilerParams(vmem_limit_bytes=vmem_bytes),
        name=name,
    )(*inputs)


def partners():
    px, py = lax.axis_size("px"), lax.axis_size("py")
    number = lambda i, j: i * py + j
    swaps = [[] for _ in range(4)]
    for i in range(px):
        for j in range(py):
            me = number(i, j)
            swaps[0].append((me, number(i ^ 1, j)))
            other = i - 1 if i % 2 == 0 else i + 1
            swaps[1].append((me, number(other, j) if 0 <= other < px else number(i, j ^ 1)))
            swaps[2].append((me, number(i, j ^ 1)))
            other = j - 1 if j % 2 == 0 else j + 1
            swaps[3].append((me, number(i, other % py)))
    return swaps


def exchange(blocks):
    swaps = partners()
    return [lax.ppermute(blocks[n], ("px", "py"), swaps[n]) for n in (1, 3, 0, 2)]


def swap(slots, devices, capacity):
    axes = ("px", "py")
    if capacity == LANES:
        return lax.all_to_all(slots, axes, 0, 0, tiled=True)
    ratio = LANES // capacity
    parts = jnp.transpose(slots.reshape(-1, 3, ratio, capacity), (0, 2, 1, 3)).reshape(
        devices, 3, capacity
    )
    moved = lax.all_to_all(parts, axes, 0, 0, tiled=True)
    return jnp.transpose(moved.reshape(-1, ratio, 3, capacity), (0, 2, 1, 3)).reshape(
        -1, 3, LANES
    )


def body(
    coords,
    displacement,
    velocity,
    inv_mass,
    ext_force,
    thickness,
    stiffness,
    elem_nodes,
    block_class,
    halo_lists,
    contact_nodes,
    contact_bucket,
    tile_pairs,
):
    rows = coords.shape[1] // LANES
    quarter = halo_lists.shape[1] // LANES
    elem_rows = elem_nodes.shape[1] // LANES
    devices = lax.axis_size("px") * lax.axis_size("py")
    capacity = 2 * contact_nodes.shape[0] // devices
    slot_rows = devices * capacity // LANES
    inv_mass = inv_mass.reshape(rows, LANES)
    thickness = thickness.reshape(elem_rows, LANES)
    nodal = shape(3 * rows, LANES)
    sent = [shape(3 * quarter, LANES)] * 4
    slots = shape(slot_rows, 3, LANES)

    counts = (lax.axis_size("px"), lax.axis_size("py"))
    corner_values = shape(12 * elem_rows, LANES)

    sources = [
        coords,
        displacement,
        contact_bucket.reshape(-1, LANES),
        contact_nodes.reshape(-1, LANES),
    ]
    inverse, outgoing = call(
        functools.partial(slots_kernel, devices, capacity),
        sources,
        [jax.ShapeDtypeStruct((slot_rows, LANES), I32), slots],
        "slots",
        far=range(4),
        scratch=[pltpu.VMEM(source.shape, source.dtype) for source in sources]
        + [pltpu.SemaphoreType.DMA((4,))],
        vmem_bytes=WHOLE_VMEM,
    )
    (
        disp,
        lists,
        nodes,
        splat,
        coords,
        vel,
        ext,
        slow,
        select,
        thickness,
        inv_mass,
        *sends,
    ) = call(
        functools.partial(prepare_kernel, counts),
        [
            displacement,
            halo_lists,
            elem_nodes,
            stiffness,
            coords,
            velocity,
            ext_force,
            block_class.reshape(1, -1),
            tile_pairs,
            thickness,
            inv_mass,
            inverse,
        ],
        [
            nodal,
            jax.ShapeDtypeStruct((4 * quarter, LANES), I32),
            jax.ShapeDtypeStruct((4 * elem_rows, LANES), I32),
            shape(144, LANES),
        ]
        + [nodal] * 3
        + [
            jax.ShapeDtypeStruct((elem_rows, LANES), I32),
            shape(2, LANES, LANES),
            shape(elem_rows, LANES),
            shape(rows, LANES),
        ]
        + sent,
        "prepare",
        far=(11,),
    )
    for step_no in range(STEPS):
        for sub_no in range(SUBS):
            first = sub_no == 0
            last = sub_no == SUBS - 1
            final = last and step_no == STEPS - 1
            if first:
                arrived = swap(outgoing, devices, capacity)
                if step_no:
                    sends = call(sends_kernel, [disp, lists, outgoing], sent, "sends", far=(2,))
            recvs = exchange(sends)
            (found,) = call(own_kernel, [disp, nodes], [corner_values], "own_corners")
            field = [found, *recvs, nodes, thickness, splat]
            if first:
                (held,) = call(
                    functools.partial(force_kernel, rows), field, [corner_values], "forces"
                )
                (pushes,) = call(
                    functools.partial(contact_kernel, tile_pairs.shape[1]),
                    [select, arrived, held],
                    [slots],
                    "contact",
                    far=(2,),
                )
                returned = swap(pushes, devices, capacity)
                outs = call(
                    functools.partial(halo_sum_kernel, rows),
                    [held, nodes, pushes],
                    sent,
                    "halo_sum",
                    far=(2,),
                )
                forces = held
            else:
                forces, *outs = call(
                    functools.partial(later_kernel, rows),
                    field + [held, slow],
                    [corner_values] + sent,
                    "forces_halo_sum",
                )
            backs = exchange(outs)
            (own,) = call(own_sum_kernel, [forces, nodes, outs[2]], [nodal], "own_sum", far=(2,))
            state = [lists, ext, inv_mass, vel, disp]
            if first:
                (internal,) = call(
                    internal_kernel, [own, *backs, lists], [nodal], "internal"
                )
                vel, disp, contact, *sends = call(
                    first_update_kernel,
                    [internal, returned, inverse] + state,
                    [nodal] * 3 + sent,
                    "first_update",
                )
                continue
            inputs = [own, *backs] + state + [contact]
            if final:
                vel, disp = call(
                    functools.partial(update_kernel, "final"),
                    inputs,
                    [shape(3, rows * LANES)] * 2,
                    "final_update",
                )
            elif last:
                vel, disp, outgoing = call(
                    functools.partial(update_kernel, "last"),
                    inputs + [coords, inverse],
                    [nodal] * 2 + [slots],
                    "last_update",
                )
            else:
                vel, disp, *sends = call(
                    functools.partial(update_kernel, "inner"),
                    inputs,
                    [nodal] * 2 + sent,
                    "update",
                )
    return (disp, vel)


def solution(mesh):
    placed = (
        P(None, ("px", "py")),
        P(None, ("px", "py")),
        P(None, ("px", "py")),
        P(("px", "py")),
        P(None, ("px", "py")),
        P(("px", "py")),
        P(),
        P(None, ("px", "py")),
        P(("px", "py")),
        P(None, ("px", "py")),
        P(("px", "py")),
        P(("px", "py"), None),
        P(None, ("px", "py")),
    )
    return jax.shard_map(
        body,
        mesh=mesh,
        in_specs=placed,
        out_specs=(P(None, ("px", "py")), P(None, ("px", "py"))),
        check_vma=False,
    )
```

```python
import functools

import jax
import jax.numpy as jnp
from jax import lax
from jax.experimental import pallas as pl
from jax.experimental.pallas import tpu as pltpu
from jax.sharding import PartitionSpec as P

LANES = 128
EBLK = 128
STEPS = 2
SUBS = 2

FAR = 10000.0
DT = 0.05
PENALTY = 0.5
REACH = 4.0

F32 = jnp.float32
BF16 = jnp.bfloat16
I32 = jnp.int32

VMEM_BYTES = 32 * 1024 * 1024
WHOLE_VMEM = 64 * 1024 * 1024


def lookup(table_row, rows, index, start=None):
    parts = []
    for at in range(0, index.shape[0], 8):
        block = index[at : at + 8]
        hi = block >> 7
        lo = block & (LANES - 1)
        if start is None:
            found = [jnp.zeros(block.shape, F32) for _ in range(3)]
        else:
            found = [start[c][at : at + 8] for c in range(3)]
        for h in rows:
            here = hi == h
            for c in range(3):
                row = jnp.broadcast_to(table_row(c, h), block.shape)
                got = jnp.take_along_axis(row, lo, axis=1, mode="promise_in_bounds")
                found[c] = jnp.where(here, got, found[c])
        parts.append(found)
    return [jnp.concatenate([part[c] for part in parts], axis=0) for c in range(3)]


def halves(values):
    top = values.astype(BF16).astype(F32)
    return [top, values - top]


def scatter_dot(hi_rows, lo_rows, value_rows, rows, first=0):
    row_no = first + lax.broadcasted_iota(I32, (rows, LANES), 0)
    total = None
    lane_no = lax.broadcasted_iota(I32, (LANES, LANES), 0)
    group = 2
    for start in range(0, len(hi_rows), group):
        lefts, rights = [], []
        for r in range(start, start + group):
            here = row_no == hi_rows[r]
            lefts.append(
                jnp.concatenate(
                    [
                        jnp.where(here, jnp.broadcast_to(vals[r], (rows, LANES)), 0.0)
                        for vals in value_rows
                    ],
                    axis=0,
                ).astype(BF16)
            )
            rights.append((lane_no == lo_rows[r]).astype(F32).astype(BF16))
        part = lax.dot_general(
            jnp.concatenate(lefts, axis=1),
            jnp.concatenate(rights, axis=1),
            (((1,), (1,)), ((), ())),
            preferred_element_type=F32,
        )
        total = part if total is None else total + part
    return total


def scatter_add(index_row, value_row, count, rows, first=0):
    hi_rows, lo_rows = [], []
    value_rows = [[] for _ in range(6)]
    for r in range(count):
        idx = index_row(r)
        hi_rows.append(idx >> 7)
        lo_rows.append(idx & (LANES - 1))
        for c in range(3):
            for part, vals in enumerate(halves(value_row(c, r))):
                value_rows[2 * c + part].append(vals)
    total = scatter_dot(hi_rows, lo_rows, value_rows, rows, first)
    return [
        total[2 * c * rows : (2 * c + 1) * rows] + total[(2 * c + 1) * rows : (2 * c + 2) * rows]
        for c in range(3)
    ]


def spread_rows(source, target, groups):
    rows = source.shape[1] // LANES
    for g in range(groups):
        for h in range(rows):
            target[g * rows + h : g * rows + h + 1, :] = source[
                g : g + 1, h * LANES : (h + 1) * LANES
            ]


def gather_halo(disp, rows, lists, sends):
    found = lookup(lambda c, h: disp[c * rows + h : c * rows + h + 1, :], range(rows), lists[...])
    quarter = lists.shape[0] // 4
    for b in range(4):
        for c in range(3):
            sends[b][c * quarter : (c + 1) * quarter, :] = found[c][b * quarter : (b + 1) * quarter]


def gather_slots(position_row, rows, inverse, outgoing):
    slot_node = inverse[...]
    found = lookup(position_row, range(rows), jnp.maximum(slot_node, 0))
    for c in range(3):
        outgoing[:, c, :] = jnp.where(slot_node >= 0, found[c], FAR)


def block_remap(index, own_count, width, px_no, py_no, px_count, py_count):
    block = (index - own_count) >> (width.bit_length() - 1)
    along_x = block < 2
    place = jnp.where(along_x, px_no, py_no)
    ends = jnp.where(along_x, px_count - 1, py_count - 1)
    edge = jnp.where((block & 1) == 0, 0, ends)
    moved = index ^ ((1 - (place & 1)) * width)
    moved = jnp.where(place == edge, -1, moved)
    return jnp.where(index < own_count, index, moved)


def slots_kernel(devices, capacity, *refs):
    sources, (inverse, outgoing) = refs[:4], refs[4:6]
    buffers, sems = refs[6:10], refs[10]
    coords, disp, bucket, contact_nodes = buffers
    copies = [
        pltpu.make_async_copy(source, target, sems.at[n])
        for n, (source, target) in enumerate(zip(sources, buffers))
    ]
    for copy in copies:
        copy.start()
    for copy in copies[2:]:
        copy.wait()
    count = bucket.shape[0]
    slot_rows = inverse.shape[0]
    dev_no = lax.broadcasted_iota(I32, (devices, LANES), 0)
    first = lax.broadcasted_iota(I32, (LANES, 2 * LANES), 0)
    second = lax.broadcasted_iota(I32, (LANES, 2 * LANES), 1)
    before = ((first < second) | (second >= LANES)).astype(F32).astype(BF16)
    base = jnp.zeros((devices, LANES), F32)
    hi_rows, lo_rows, digits = [], [], [[], []]
    for r in range(count):
        b = bucket[r : r + 1, :]
        onehot = (dev_no == b).astype(F32)
        sums = jnp.dot(onehot.astype(BF16), before, preferred_element_type=F32)
        rank = jnp.sum(onehot * (sums[:, :LANES] + base), axis=0, keepdims=True)
        base = base + sums[:, LANES:]
        slot = b * capacity + rank.astype(I32)
        hi_rows.append(slot >> 7)
        lo_rows.append(slot & (LANES - 1))
        value = contact_nodes[r : r + 1, :] + 1
        digits[0].append((value >> 6).astype(F32))
        digits[1].append((value & 63).astype(F32))
    total = scatter_dot(hi_rows, lo_rows, digits, slot_rows)
    inverse[...] = (total[:slot_rows] * 64.0 + total[slot_rows:]).astype(I32) - 1
    for copy in copies[:2]:
        copy.wait()

    def position_row(c, h):
        span = slice(h * LANES, (h + 1) * LANES)
        return coords[c : c + 1, span] + disp[c : c + 1, span]

    gather_slots(position_row, coords.shape[1] // LANES, inverse, outgoing)


def prepare_kernel(counts, *refs):
    (disp_in, lists_in, nodes_in, stiff, pairs, thick_in, after) = refs[:7]
    (disp, lists, nodes, splat, select, thick) = refs[7:13]
    sends = refs[13:]
    px_no = lax.axis_index("px")
    py_no = lax.axis_index("py")
    own_count = disp_in.shape[1]
    rows = own_count // LANES
    spread_rows(disp_in, disp, 3)
    width = lists_in.shape[1]
    quarter = width // LANES
    for b in range(4):
        place = px_no if b < 2 else py_no
        count = counts[b // 2]
        to_high = (place & 1) ^ (1 - b % 2)
        row = (b // 2) * 2
        missing = (place == to_high * (count - 1)).astype(I32)
        for q in range(quarter):
            span = slice(q * LANES, (q + 1) * LANES)
            chosen = jnp.where(
                jnp.full((1, LANES), to_high) == 1,
                lists_in[row + 1 : row + 2, span],
                lists_in[row : row + 1, span],
            )
            lists[b * quarter + q : b * quarter + q + 1, :] = jnp.where(
                jnp.full((1, LANES), missing) == 1, -1, chosen
            )
    gather_halo(disp, rows, lists, sends)
    spread_rows(nodes_in, nodes, 4)
    nodes[...] = block_remap(nodes[...], own_count, width, px_no, py_no, *counts)
    size = stiff.shape[0]
    for j in range(size):
        splat[j * size : (j + 1) * size, :] = jnp.broadcast_to(stiff[:, j : j + 1], (size, LANES))
    ends = [pairs[0:1, :], pairs[1:2, :]]
    short = LANES - 2 * pairs.shape[1]
    if short:
        ends.append(jnp.full((1, short), -1))
    tile_no = lax.broadcasted_iota(I32, (LANES, LANES), 0)
    onehot = (tile_no == jnp.concatenate(ends, axis=1)).astype(F32)
    select[0] = onehot
    select[1] = jnp.transpose(onehot)
    thick[...] = thick_in[...]


def own_kernel(disp, nodes, found):
    rows = disp.shape[0] // 3
    count = nodes.shape[0]
    values = lookup(
        lambda c, h: disp[c * rows + h : c * rows + h + 1, :], range(rows), nodes[...]
    )
    for c in range(3):
        found[c * count : (c + 1) * count, :] = values[c]


def corner_forces(found, rows, recvs, nodes, thick, splat):
    quarter = recvs[0].shape[0] // 3
    elem_rows = thick.shape[0]

    def table_row(c, h):
        b, q = divmod(h - rows, quarter)
        return recvs[b][c * quarter + q : c * quarter + q + 1, :]

    count = nodes.shape[0]
    corners = []
    for k in range(4):
        span = slice(k * elem_rows, (k + 1) * elem_rows)
        own = [found[c * count + span.start : c * count + span.stop, :] for c in range(3)]
        corners.append(
            lookup(table_row, range(rows, rows + 4 * quarter), nodes[span, :], own)
        )
    factor = thick[...]
    forces = []
    for i in range(12):
        total = None
        for j in range(12):
            term = splat[j * 12 + i : j * 12 + i + 1, :] * corners[j % 4][j // 4]
            total = term if total is None else total + term
        forces.append(factor * total)
    return forces


def stored_row(forces, nodes):
    count = nodes.shape[0]
    return lambda c, r: forces[c * count + r : c * count + r + 1, :]


def sum_own(force_row, nodes, own):
    rows = own.shape[0] // 3
    sums = scatter_add(lambda r: nodes[r : r + 1, :], force_row, nodes.shape[0], rows)
    for c in range(3):
        own[c * rows : (c + 1) * rows, :] = sums[c]


def sum_halo(force_row, nodes, rows, outs):
    quarter = outs[0].shape[0] // 3
    sums = scatter_add(
        lambda r: nodes[r : r + 1, :], force_row, nodes.shape[0], 4 * quarter, rows
    )
    for c in range(3):
        for b in range(4):
            outs[b][c * quarter : (c + 1) * quarter, :] = sums[c][b * quarter : (b + 1) * quarter]


def force_kernel(rows, found, recv1, recv3, recv0, recv2, nodes, thick, splat, held):
    elem_rows = thick.shape[0]
    forces = corner_forces(found, rows, (recv0, recv1, recv2, recv3), nodes, thick, splat)
    for i in range(12):
        held[i * elem_rows : (i + 1) * elem_rows, :] = forces[i]


def halo_sum_kernel(rows, held, nodes, after, *outs):
    sum_halo(stored_row(held, nodes), nodes, rows, outs)


def own_sum_kernel(held, nodes, after, own):
    sum_own(stored_row(held, nodes), nodes, own)


def later_kernel(
    rows,
    found,
    recv1,
    recv3,
    recv0,
    recv2,
    nodes,
    thick,
    splat,
    held,
    slow,
    mixed,
    *outs,
):
    elem_rows = thick.shape[0]
    forces = corner_forces(found, rows, (recv0, recv1, recv2, recv3), nodes, thick, splat)
    kept = slow[...] == 1
    for i in range(12):
        span = slice(i * elem_rows, (i + 1) * elem_rows)
        forces[i] = jnp.where(kept, held[span, :], forces[i])
        mixed[span, :] = forces[i]

    def force_row(c, r):
        k, h = divmod(r, elem_rows)
        return forces[c * 4 + k][h : h + 1, :]

    sum_halo(force_row, nodes, rows, outs)


def returned_sums(backs, lists, rows):
    quarter = backs[0].shape[0] // 3

    def back_row(c, r):
        b, q = divmod(r, quarter)
        return backs[b][c * quarter + q : c * quarter + q + 1, :]

    return scatter_add(lambda r: lists[r : r + 1, :], back_row, 4 * quarter, rows)


def internal_kernel(own, back1, back3, back0, back2, lists, internal):
    rows = own.shape[0] // 3
    sums = returned_sums((back0, back1, back2, back3), lists, rows)
    for c in range(3):
        span = slice(c * rows, (c + 1) * rows)
        internal[span, :] = own[span, :] + sums[c]


def sends_kernel(disp, lists, after, *sends):
    gather_halo(disp, disp.shape[0] // 3, lists, sends)


def thirds(values):
    parts = []
    for _ in range(3):
        top = values.astype(BF16)
        parts.append(top)
        values = values - top.astype(F32)
    return jnp.concatenate(parts, axis=1)


def dot_thirds(onehot, values):
    width = values.shape[1]
    sums = jnp.dot(onehot.astype(BF16), thirds(values), preferred_element_type=F32)
    return sums[:, :width] + sums[:, width : 2 * width] + sums[:, 2 * width :]


def contact_kernel(pair_count, select, arrived, after, pushes):
    tiles = arrived.shape[0]
    points = jnp.concatenate([arrived[:, c, :] for c in range(3)], axis=1)
    picked = dot_thirds(select[1, : 2 * pair_count, :tiles], points)
    first, second = picked[:pair_count], picked[pair_count:]
    group = LANES // 4
    pushed = []
    for start in range(0, pair_count, group):
        stop = min(start + group, pair_count)
        block = jnp.concatenate(
            [second[start:stop, c * LANES : (c + 1) * LANES] for c in range(3)]
            + [jnp.zeros((LANES - 3 * (stop - start), LANES), F32)],
            axis=0,
        )
        turned = jnp.transpose(block)
        for p in range(start, stop):
            gaps = []
            for c in range(3):
                column = c * (stop - start) + p - start
                gaps.append(
                    jnp.broadcast_to(
                        first[p : p + 1, c * LANES : (c + 1) * LANES], (LANES, LANES)
                    )
                    - jnp.broadcast_to(turned[:, column : column + 1], (LANES, LANES))
                )
            dist = gaps[0] * gaps[0] + gaps[1] * gaps[1] + gaps[2] * gaps[2]
            weight = jnp.exp(dist * (-1.0 / REACH))
            pushed.append(
                jnp.concatenate(
                    [jnp.sum(weight * gaps[c], axis=0, keepdims=True) for c in range(3)], axis=1
                )
            )
    total = PENALTY * dot_thirds(select[0, :tiles, :pair_count], jnp.concatenate(pushed, axis=0))
    for c in range(3):
        pushes[:, c, :] = total[:, c * LANES : (c + 1) * LANES]


def advance(internal, contact, ext, inv_mass, vel, disp, rows):
    for c in range(3):
        span = slice(c * rows, (c + 1) * rows)
        accel = inv_mass[...] * (ext[span, :] - internal[c] + contact[c])
        vel_c = vel[span, :] + DT * accel
        yield c, vel_c, disp[span, :] + DT * vel_c


def components(array):
    rows = array.shape[0] // 3
    return [array[c * rows : (c + 1) * rows, :] for c in range(3)]


def first_update_kernel(starting, *refs):
    refs = list(refs)
    internal, returned, inverse, lists, inv_mass, disp, vel, ext = refs[:8]
    new_vel, new_disp, contact, *sends = refs[9 if starting else 8 :]
    rows = disp.shape[0] // 3
    if starting:
        classes = refs[8]
        *sends, ext_rows, slow = sends
        spread_rows(vel, new_vel, 3)
        spread_rows(ext, ext_rows, 3)
        vel, ext = new_vel, ext_rows
        blocks = classes.shape[1]
        row = jnp.concatenate([classes[...], jnp.zeros((1, LANES - blocks), I32)], axis=1)
        slow[...] = jnp.transpose(jnp.broadcast_to(row, (LANES, LANES)))[:blocks]
    sums = scatter_add(
        lambda r: inverse[r : r + 1, :],
        lambda c, r: returned[r, c : c + 1, :],
        inverse.shape[0],
        rows,
    )
    steps = advance(components(internal), sums, ext, inv_mass, vel, disp, rows)
    for c, vel_c, disp_c in steps:
        span = slice(c * rows, (c + 1) * rows)
        contact[span, :] = sums[c]
        new_vel[span, :] = vel_c
        new_disp[span, :] = disp_c
    gather_halo(new_disp, rows, lists, sends)


def update_kernel(case, *refs):
    refs = list(refs)
    own, back1, back3, back0, back2, lists, ext, inv_mass, vel, disp, contact = refs[:11]
    rows = disp.shape[0] // 3
    sums = returned_sums((back0, back1, back2, back3), lists, rows)
    internal = [mine + more for mine, more in zip(components(own), sums)]
    steps = advance(internal, components(contact), ext, inv_mass, vel, disp, rows)
    if case == "final":
        new_vel, new_disp = refs[11:]
        for c, vel_c, disp_c in steps:
            for h in range(rows):
                new_vel[c : c + 1, h * LANES : (h + 1) * LANES] = vel_c[h : h + 1, :]
                new_disp[c : c + 1, h * LANES : (h + 1) * LANES] = disp_c[h : h + 1, :]
        return
    if case == "last":
        coords, inverse, new_vel, new_disp, outgoing = refs[11:]
    else:
        new_vel, new_disp, *sends = refs[11:]
    for c, vel_c, disp_c in steps:
        new_vel[c * rows : (c + 1) * rows, :] = vel_c
        new_disp[c * rows : (c + 1) * rows, :] = disp_c
    if case == "last":

        def position_row(c, h):
            mine = coords[c : c + 1, h * LANES : (h + 1) * LANES]
            return mine + new_disp[c * rows + h : c * rows + h + 1, :]

        gather_slots(position_row, rows, inverse, outgoing)
    else:
        gather_halo(new_disp, rows, lists, sends)


def vmem(count):
    return [pl.BlockSpec(memory_space=pltpu.VMEM)] * count


def shape(*dims):
    return jax.ShapeDtypeStruct(dims, F32)


def call(kernel, inputs, outputs, name, smem=(), far=(), scratch=(), vmem_bytes=VMEM_BYTES):
    specs = [
        pl.BlockSpec(
            memory_space=pltpu.SMEM if i in smem else pl.ANY if i in far else pltpu.VMEM
        )
        for i in range(len(inputs))
    ]
    return pl.pallas_call(
        kernel,
        out_shape=tuple(outputs),
        in_specs=specs,
        out_specs=tuple(vmem(len(outputs))),
        scratch_shapes=list(scratch),
        compiler_params=pltpu.CompilerParams(vmem_limit_bytes=vmem_bytes),
        name=name,
    )(*inputs)


def partners():
    px, py = lax.axis_size("px"), lax.axis_size("py")
    number = lambda i, j: i * py + j
    swaps = [[] for _ in range(4)]
    for i in range(px):
        for j in range(py):
            me = number(i, j)
            swaps[0].append((me, number(i ^ 1, j)))
            other = i - 1 if i % 2 == 0 else i + 1
            swaps[1].append((me, number(other, j) if 0 <= other < px else number(i, j ^ 1)))
            swaps[2].append((me, number(i, j ^ 1)))
            other = j - 1 if j % 2 == 0 else j + 1
            swaps[3].append((me, number(i, other % py)))
    return swaps


def exchange(blocks):
    swaps = partners()
    return [lax.ppermute(blocks[n], ("px", "py"), swaps[n]) for n in (1, 3, 0, 2)]


def swap(slots, devices, capacity):
    axes = ("px", "py")
    if capacity == LANES:
        return lax.all_to_all(slots, axes, 0, 0, tiled=True)
    ratio = LANES // capacity
    parts = jnp.transpose(slots.reshape(-1, 3, ratio, capacity), (0, 2, 1, 3)).reshape(
        devices, 3, capacity
    )
    moved = lax.all_to_all(parts, axes, 0, 0, tiled=True)
    return jnp.transpose(moved.reshape(-1, ratio, 3, capacity), (0, 2, 1, 3)).reshape(
        -1, 3, LANES
    )


def body(
    coords,
    displacement,
    velocity,
    inv_mass,
    ext_force,
    thickness,
    stiffness,
    elem_nodes,
    block_class,
    halo_lists,
    contact_nodes,
    contact_bucket,
    tile_pairs,
):
    rows = coords.shape[1] // LANES
    quarter = halo_lists.shape[1] // LANES
    elem_rows = elem_nodes.shape[1] // LANES
    devices = lax.axis_size("px") * lax.axis_size("py")
    capacity = 2 * contact_nodes.shape[0] // devices
    slot_rows = devices * capacity // LANES
    inv_mass = inv_mass.reshape(rows, LANES)
    thickness = thickness.reshape(elem_rows, LANES)
    nodal = shape(3 * rows, LANES)
    sent = [shape(3 * quarter, LANES)] * 4
    slots = shape(slot_rows, 3, LANES)

    counts = (lax.axis_size("px"), lax.axis_size("py"))
    corner_values = shape(12 * elem_rows, LANES)

    sources = [
        coords,
        displacement,
        contact_bucket.reshape(-1, LANES),
        contact_nodes.reshape(-1, LANES),
    ]
    inverse, outgoing = call(
        functools.partial(slots_kernel, devices, capacity),
        sources,
        [jax.ShapeDtypeStruct((slot_rows, LANES), I32), slots],
        "slots",
        far=range(4),
        scratch=[pltpu.VMEM(source.shape, source.dtype) for source in sources]
        + [pltpu.SemaphoreType.DMA((4,))],
        vmem_bytes=WHOLE_VMEM,
    )
    disp, lists, nodes, splat, select, thickness, *sends = call(
        functools.partial(prepare_kernel, counts),
        [displacement, halo_lists, elem_nodes, stiffness, tile_pairs, thickness, outgoing],
        [
            nodal,
            jax.ShapeDtypeStruct((4 * quarter, LANES), I32),
            jax.ShapeDtypeStruct((4 * elem_rows, LANES), I32),
            shape(144, LANES),
            shape(2, LANES, LANES),
            shape(elem_rows, LANES),
        ]
        + sent,
        "prepare",
        far=(6,),
    )
    vel = velocity
    for step_no in range(STEPS):
        for sub_no in range(SUBS):
            first = sub_no == 0
            last = sub_no == SUBS - 1
            final = last and step_no == STEPS - 1
            if first:
                arrived = swap(outgoing, devices, capacity)
                if step_no:
                    sends = call(sends_kernel, [disp, lists, outgoing], sent, "sends", far=(2,))
            recvs = exchange(sends)
            (found,) = call(own_kernel, [disp, nodes], [corner_values], "own_corners")
            field = [found, *recvs, nodes, thickness, splat]
            if first:
                (held,) = call(
                    functools.partial(force_kernel, rows), field, [corner_values], "forces"
                )
                (pushes,) = call(
                    functools.partial(contact_kernel, tile_pairs.shape[1]),
                    [select, arrived, held],
                    [slots],
                    "contact",
                    far=(2,),
                )
                returned = swap(pushes, devices, capacity)
                outs = call(
                    functools.partial(halo_sum_kernel, rows),
                    [held, nodes, pushes],
                    sent,
                    "halo_sum",
                    far=(2,),
                )
                forces = held
            else:
                forces, *outs = call(
                    functools.partial(later_kernel, rows),
                    field + [held, slow],
                    [corner_values] + sent,
                    "forces_halo_sum",
                )
            backs = exchange(outs)
            (own,) = call(own_sum_kernel, [forces, nodes, outs[2]], [nodal], "own_sum", far=(2,))
            if first:
                (internal,) = call(
                    internal_kernel, [own, *backs, lists], [nodal], "internal"
                )
                inputs = [internal, returned, inverse, lists, inv_mass, disp, vel]
                outputs = [nodal] * 3 + sent
                if step_no == 0:
                    inputs += [ext_force, block_class.reshape(1, -1)]
                    outputs += [nodal, jax.ShapeDtypeStruct((elem_rows, LANES), I32)]
                else:
                    inputs.append(ext)
                vel, disp, contact, *sends = call(
                    functools.partial(first_update_kernel, step_no == 0),
                    inputs,
                    outputs,
                    "first_update",
                )
                if step_no == 0:
                    *sends, ext, slow = sends
                continue
            inputs = [own, *backs, lists, ext, inv_mass, vel, disp, contact]
            if final:
                vel, disp = call(
                    functools.partial(update_kernel, "final"),
                    inputs,
                    [shape(3, rows * LANES)] * 2,
                    "final_update",
                )
            elif last:
                vel, disp, outgoing = call(
                    functools.partial(update_kernel, "last"),
                    inputs + [coords, inverse],
                    [nodal] * 2 + [slots],
                    "last_update",
                )
            else:
                vel, disp, *sends = call(
                    functools.partial(update_kernel, "inner"),
                    inputs,
                    [nodal] * 2 + sent,
                    "update",
                )
    return (disp, vel)


def solution(mesh):
    placed = (
        P(None, ("px", "py")),
        P(None, ("px", "py")),
        P(None, ("px", "py")),
        P(("px", "py")),
        P(None, ("px", "py")),
        P(("px", "py")),
        P(),
        P(None, ("px", "py")),
        P(("px", "py")),
        P(None, ("px", "py")),
        P(("px", "py")),
        P(("px", "py"), None),
        P(None, ("px", "py")),
    )
    return jax.shard_map(
        body,
        mesh=mesh,
        in_specs=placed,
        out_specs=(P(None, ("px", "py")), P(None, ("px", "py"))),
        check_vma=False,
    )
```

```python
import functools

import jax
import jax.numpy as jnp
from jax import lax
from jax.experimental import pallas as pl
from jax.experimental.pallas import tpu as pltpu
from jax.sharding import PartitionSpec as P

LANES = 128
EBLK = 128
STEPS = 2
SUBS = 2

FAR = 10000.0
DT = 0.05
PENALTY = 0.5
REACH = 4.0

F32 = jnp.float32
BF16 = jnp.bfloat16
I32 = jnp.int32

VMEM_BYTES = 32 * 1024 * 1024
WHOLE_VMEM = 64 * 1024 * 1024


BESIDE = (1, 3, 0, 2)
ALONE = (1, 3, 0, 2)


def lookup(table_row, rows, index, start=None):
    parts = []
    for at in range(0, index.shape[0], 8):
        block = index[at : at + 8]
        hi = block >> 7
        lo = block & (LANES - 1)
        if start is None:
            found = [jnp.zeros(block.shape, F32) for _ in range(3)]
        else:
            found = [start[c][at : at + 8] for c in range(3)]
        for h in rows:
            here = hi == h
            for c in range(3):
                row = jnp.broadcast_to(table_row(c, h), block.shape)
                got = jnp.take_along_axis(row, lo, axis=1, mode="promise_in_bounds")
                found[c] = jnp.where(here, got, found[c])
        parts.append(found)
    return [jnp.concatenate([part[c] for part in parts], axis=0) for c in range(3)]


def halves(values):
    top = values.astype(BF16).astype(F32)
    return [top, values - top]


def scatter_dot(hi_rows, lo_rows, value_rows, rows, first=0):
    row_no = first + lax.broadcasted_iota(I32, (rows, LANES), 0)
    total = None
    lane_no = lax.broadcasted_iota(I32, (LANES, LANES), 0)
    group = 2
    for start in range(0, len(hi_rows), group):
        lefts, rights = [], []
        for r in range(start, start + group):
            here = row_no == hi_rows[r]
            lefts.append(
                jnp.concatenate(
                    [
                        jnp.where(here, jnp.broadcast_to(vals[r], (rows, LANES)), 0.0)
                        for vals in value_rows
                    ],
                    axis=0,
                ).astype(BF16)
            )
            rights.append((lane_no == lo_rows[r]).astype(F32).astype(BF16))
        part = lax.dot_general(
            jnp.concatenate(lefts, axis=1),
            jnp.concatenate(rights, axis=1),
            (((1,), (1,)), ((), ())),
            preferred_element_type=F32,
        )
        total = part if total is None else total + part
    return total


def scatter_add(index_row, value_row, count, rows, first=0):
    hi_rows, lo_rows = [], []
    value_rows = [[] for _ in range(6)]
    for r in range(count):
        idx = index_row(r)
        hi_rows.append(idx >> 7)
        lo_rows.append(idx & (LANES - 1))
        for c in range(3):
            for part, vals in enumerate(halves(value_row(c, r))):
                value_rows[2 * c + part].append(vals)
    total = scatter_dot(hi_rows, lo_rows, value_rows, rows, first)
    return [
        total[2 * c * rows : (2 * c + 1) * rows] + total[(2 * c + 1) * rows : (2 * c + 2) * rows]
        for c in range(3)
    ]


def in_place(refs, order):
    return [refs[order.index(n)] for n in range(4)]


def spread_rows(source, target, groups):
    rows = source.shape[1] // LANES
    for g in range(groups):
        for h in range(rows):
            target[g * rows + h : g * rows + h + 1, :] = source[
                g : g + 1, h * LANES : (h + 1) * LANES
            ]


def gather_halo(disp, rows, lists, sends):
    found = lookup(lambda c, h: disp[c * rows + h : c * rows + h + 1, :], range(rows), lists[...])
    quarter = lists.shape[0] // 4
    for b in range(4):
        for c in range(3):
            sends[b][c * quarter : (c + 1) * quarter, :] = found[c][b * quarter : (b + 1) * quarter]


def gather_slots(position_row, rows, inverse, outgoing):
    slot_node = inverse[...]
    found = lookup(position_row, range(rows), jnp.maximum(slot_node, 0))
    for c in range(3):
        outgoing[:, c, :] = jnp.where(slot_node >= 0, found[c], FAR)


def block_remap(index, own_count, width, px_no, py_no, px_count, py_count):
    block = (index - own_count) >> (width.bit_length() - 1)
    along_x = block < 2
    place = jnp.where(along_x, px_no, py_no)
    ends = jnp.where(along_x, px_count - 1, py_count - 1)
    edge = jnp.where((block & 1) == 0, 0, ends)
    moved = index ^ ((1 - (place & 1)) * width)
    moved = jnp.where(place == edge, -1, moved)
    return jnp.where(index < own_count, index, moved)


def slots_kernel(devices, capacity, *refs):
    sources, (inverse, outgoing) = refs[:4], refs[4:6]
    buffers, sems = refs[6:10], refs[10]
    coords, disp, bucket, contact_nodes = buffers
    copies = [
        pltpu.make_async_copy(source, target, sems.at[n])
        for n, (source, target) in enumerate(zip(sources, buffers))
    ]
    for copy in copies:
        copy.start()
    for copy in copies[2:]:
        copy.wait()
    count = bucket.shape[0]
    slot_rows = inverse.shape[0]
    dev_no = lax.broadcasted_iota(I32, (devices, LANES), 0)
    first = lax.broadcasted_iota(I32, (LANES, 2 * LANES), 0)
    second = lax.broadcasted_iota(I32, (LANES, 2 * LANES), 1)
    before = ((first < second) | (second >= LANES)).astype(F32).astype(BF16)
    base = jnp.zeros((devices, LANES), F32)
    hi_rows, lo_rows, digits = [], [], [[], []]
    for r in range(count):
        b = bucket[r : r + 1, :]
        onehot = (dev_no == b).astype(F32)
        sums = jnp.dot(onehot.astype(BF16), before, preferred_element_type=F32)
        rank = jnp.sum(onehot * (sums[:, :LANES] + base), axis=0, keepdims=True)
        base = base + sums[:, LANES:]
        slot = b * capacity + rank.astype(I32)
        hi_rows.append(slot >> 7)
        lo_rows.append(slot & (LANES - 1))
        value = contact_nodes[r : r + 1, :] + 1
        digits[0].append((value >> 6).astype(F32))
        digits[1].append((value & 63).astype(F32))
    total = scatter_dot(hi_rows, lo_rows, digits, slot_rows)
    inverse[...] = (total[:slot_rows] * 64.0 + total[slot_rows:]).astype(I32) - 1
    for copy in copies[:2]:
        copy.wait()

    def position_row(c, h):
        span = slice(h * LANES, (h + 1) * LANES)
        return coords[c : c + 1, span] + disp[c : c + 1, span]

    gather_slots(position_row, coords.shape[1] // LANES, inverse, outgoing)


def prepare_kernel(counts, *refs):
    (disp_in, lists_in, nodes_in, stiff, after) = refs[:5]
    (disp, lists, nodes, splat) = refs[5:9]
    sends = refs[9:]
    px_no = lax.axis_index("px")
    py_no = lax.axis_index("py")
    own_count = disp_in.shape[1]
    rows = own_count // LANES
    spread_rows(disp_in, disp, 3)
    width = lists_in.shape[1]
    quarter = width // LANES
    for b in range(4):
        place = px_no if b < 2 else py_no
        count = counts[b // 2]
        to_high = (place & 1) ^ (1 - b % 2)
        row = (b // 2) * 2
        missing = (place == to_high * (count - 1)).astype(I32)
        for q in range(quarter):
            span = slice(q * LANES, (q + 1) * LANES)
            chosen = jnp.where(
                jnp.full((1, LANES), to_high) == 1,
                lists_in[row + 1 : row + 2, span],
                lists_in[row : row + 1, span],
            )
            lists[b * quarter + q : b * quarter + q + 1, :] = jnp.where(
                jnp.full((1, LANES), missing) == 1, -1, chosen
            )
    gather_halo(disp, rows, lists, sends)
    spread_rows(nodes_in, nodes, 4)
    nodes[...] = block_remap(nodes[...], own_count, width, px_no, py_no, *counts)
    size = stiff.shape[0]
    for j in range(size):
        splat[j * size : (j + 1) * size, :] = jnp.broadcast_to(stiff[:, j : j + 1], (size, LANES))


def masks_kernel(pairs, classes, after, select, spread, slow):
    pair_count = pairs.shape[1]
    row = pairs[0:1, :]
    if pair_count < LANES:
        row = jnp.concatenate([row, jnp.full((1, LANES - pair_count), -1)], axis=1)
    onehot = (lax.broadcasted_iota(I32, (LANES, LANES), 0) == row).astype(F32)
    select[0] = onehot
    select[1] = jnp.transpose(onehot)
    tiles = spread.shape[0] // 3
    tile_no = lax.broadcasted_iota(I32, (tiles, LANES), 0)
    tile_no = jnp.concatenate([tile_no] * 3, axis=0)
    for p in range(pair_count):
        other = jnp.broadcast_to(pairs[1:2, p : p + 1], tile_no.shape)
        spread[:, p * LANES : (p + 1) * LANES] = (tile_no == other).astype(F32).astype(BF16)
    blocks = classes.shape[1]
    row = jnp.concatenate([classes[...], jnp.zeros((1, LANES - blocks), I32)], axis=1)
    slow[...] = jnp.transpose(jnp.broadcast_to(row, (LANES, LANES)))[:blocks]


def own_kernel(disp, nodes, found):
    rows = disp.shape[0] // 3
    count = nodes.shape[0]
    values = lookup(
        lambda c, h: disp[c * rows + h : c * rows + h + 1, :], range(rows), nodes[...]
    )
    for c in range(3):
        found[c * count : (c + 1) * count, :] = values[c]


def corner_forces(found, rows, recvs, nodes, thick, splat):
    quarter = recvs[0].shape[0] // 3
    elem_rows = thick.shape[0]

    def table_row(c, h):
        b, q = divmod(h - rows, quarter)
        return recvs[b][c * quarter + q : c * quarter + q + 1, :]

    count = nodes.shape[0]
    corners = []
    for k in range(4):
        span = slice(k * elem_rows, (k + 1) * elem_rows)
        own = [found[c * count + span.start : c * count + span.stop, :] for c in range(3)]
        corners.append(
            lookup(table_row, range(rows, rows + 4 * quarter), nodes[span, :], own)
        )
    factor = thick[...]
    forces = []
    for i in range(12):
        total = None
        for j in range(12):
            term = splat[j * 12 + i : j * 12 + i + 1, :] * corners[j % 4][j // 4]
            total = term if total is None else total + term
        forces.append(factor * total)
    return forces


def stored_row(forces, nodes):
    count = nodes.shape[0]
    return lambda c, r: forces[c * count + r : c * count + r + 1, :]


def sum_own(force_row, nodes, own):
    rows = own.shape[0] // 3
    sums = scatter_add(lambda r: nodes[r : r + 1, :], force_row, nodes.shape[0], rows)
    for c in range(3):
        own[c * rows : (c + 1) * rows, :] = sums[c]


def sum_halo(force_row, nodes, rows, outs):
    quarter = outs[0].shape[0] // 3
    sums = scatter_add(
        lambda r: nodes[r : r + 1, :], force_row, nodes.shape[0], 4 * quarter, rows
    )
    for c in range(3):
        for b in range(4):
            outs[b][c * quarter : (c + 1) * quarter, :] = sums[c][b * quarter : (b + 1) * quarter]


def force_kernel(rows, found, *refs):
    recvs = in_place(refs[:4], BESIDE)
    nodes, thick, splat, held = refs[4:]
    elem_rows = thick.shape[0]
    forces = corner_forces(found, rows, recvs, nodes, thick, splat)
    for i in range(12):
        held[i * elem_rows : (i + 1) * elem_rows, :] = forces[i]


def halo_sum_kernel(rows, held, nodes, after, *outs):
    sum_halo(stored_row(held, nodes), nodes, rows, outs)


def own_sum_kernel(held, nodes, after, own):
    sum_own(stored_row(held, nodes), nodes, own)


def later_kernel(rows, found, *refs):
    recvs = in_place(refs[:4], ALONE)
    nodes, thick, splat, held, slow, mixed = refs[4:10]
    outs = refs[10:]
    elem_rows = thick.shape[0]
    forces = corner_forces(found, rows, recvs, nodes, thick, splat)
    kept = slow[...] == 1
    for i in range(12):
        span = slice(i * elem_rows, (i + 1) * elem_rows)
        forces[i] = jnp.where(kept, held[span, :], forces[i])
        mixed[span, :] = forces[i]

    def force_row(c, r):
        k, h = divmod(r, elem_rows)
        return forces[c * 4 + k][h : h + 1, :]

    sum_halo(force_row, nodes, rows, outs)


def returned_sums(backs, lists, rows):
    quarter = backs[0].shape[0] // 3

    def back_row(c, r):
        b, q = divmod(r, quarter)
        return backs[b][c * quarter + q : c * quarter + q + 1, :]

    return scatter_add(lambda r: lists[r : r + 1, :], back_row, 4 * quarter, rows)


def sends_kernel(disp, lists, after, *sends):
    gather_halo(disp, disp.shape[0] // 3, lists, sends)


def thirds(values):
    parts = []
    for _ in range(3):
        top = values.astype(BF16)
        parts.append(top)
        values = values - top.astype(F32)
    return parts


def dot_thirds(onehot, values):
    width = values.shape[1]
    sums = jnp.dot(
        onehot.astype(BF16),
        jnp.concatenate(thirds(values), axis=1),
        preferred_element_type=F32,
    )
    return sums[:, :width] + sums[:, width : 2 * width] + sums[:, 2 * width :]


def contact_kernel(pair_count, select, spread, arrived, after, pushes):
    tiles = arrived.shape[0]
    points = [arrived[:, c, :] for c in range(3)]
    first = dot_thirds(select[1, :pair_count, :tiles], jnp.concatenate(points, axis=1))
    second = []
    for c in range(3):
        parts = [part.astype(F32) for part in thirds(points[c])]
        rest = LANES - 3 * tiles
        if rest:
            parts.append(jnp.zeros((rest, LANES), F32))
        turned = jnp.transpose(jnp.concatenate(parts, axis=0))[:, : 3 * tiles].astype(BF16)
        second.append(jnp.dot(turned, spread[...], preferred_element_type=F32))
    pushed = []
    for p in range(pair_count):
        gaps = [
            jnp.broadcast_to(first[p : p + 1, c * LANES : (c + 1) * LANES], (LANES, LANES))
            - second[c][:, p * LANES : (p + 1) * LANES]
            for c in range(3)
        ]
        dist = gaps[0] * gaps[0] + gaps[1] * gaps[1] + gaps[2] * gaps[2]
        weight = jnp.exp(dist * (-1.0 / REACH))
        pushed.append(
            jnp.concatenate(
                [jnp.sum(weight * gaps[c], axis=0, keepdims=True) for c in range(3)], axis=1
            )
        )
    total = PENALTY * dot_thirds(select[0, :tiles, :pair_count], jnp.concatenate(pushed, axis=0))
    for c in range(3):
        pushes[:, c, :] = total[:, c * LANES : (c + 1) * LANES]


def advance(internal, contact, ext, inv_mass, vel, disp, rows):
    for c in range(3):
        span = slice(c * rows, (c + 1) * rows)
        accel = inv_mass[...] * (ext[span, :] - internal[c] + contact[c])
        vel_c = vel[span, :] + DT * accel
        yield c, vel_c, disp[span, :] + DT * vel_c


def components(array):
    rows = array.shape[0] // 3
    return [array[c * rows : (c + 1) * rows, :] for c in range(3)]


def first_update_kernel(starting, *refs):
    refs = list(refs)
    own = refs[0]
    returned, inverse, lists, inv_mass, disp, vel, ext = refs[5:12]
    new_vel, new_disp, contact, *sends = refs[12:]
    rows = disp.shape[0] // 3
    backs = returned_sums(in_place(refs[1:5], BESIDE), lists, rows)
    internal = [mine + more for mine, more in zip(components(own), backs)]
    if starting:
        *sends, ext_rows = sends
        spread_rows(vel, new_vel, 3)
        spread_rows(ext, ext_rows, 3)
        vel, ext = new_vel, ext_rows
    sums = scatter_add(
        lambda r: inverse[r : r + 1, :],
        lambda c, r: returned[r, c : c + 1, :],
        inverse.shape[0],
        rows,
    )
    steps = advance(internal, sums, ext, inv_mass, vel, disp, rows)
    for c, vel_c, disp_c in steps:
        span = slice(c * rows, (c + 1) * rows)
        contact[span, :] = sums[c]
        new_vel[span, :] = vel_c
        new_disp[span, :] = disp_c
    gather_halo(new_disp, rows, lists, sends)


def update_kernel(case, *refs):
    own = refs[0]
    lists, ext, inv_mass, vel, disp, contact = refs[5:11]
    rows = disp.shape[0] // 3
    sums = returned_sums(in_place(refs[1:5], ALONE), lists, rows)
    internal = [mine + more for mine, more in zip(components(own), sums)]
    steps = advance(internal, components(contact), ext, inv_mass, vel, disp, rows)
    if case == "final":
        new_vel, new_disp = refs[11:]
        for c, vel_c, disp_c in steps:
            for h in range(rows):
                new_vel[c : c + 1, h * LANES : (h + 1) * LANES] = vel_c[h : h + 1, :]
                new_disp[c : c + 1, h * LANES : (h + 1) * LANES] = disp_c[h : h + 1, :]
        return
    if case == "last":
        coords, inverse, new_vel, new_disp, outgoing = refs[11:]
    else:
        new_vel, new_disp, *sends = refs[11:]
    for c, vel_c, disp_c in steps:
        new_vel[c * rows : (c + 1) * rows, :] = vel_c
        new_disp[c * rows : (c + 1) * rows, :] = disp_c
    if case == "last":

        def position_row(c, h):
            mine = coords[c : c + 1, h * LANES : (h + 1) * LANES]
            return mine + new_disp[c * rows + h : c * rows + h + 1, :]

        gather_slots(position_row, rows, inverse, outgoing)
    else:
        gather_halo(new_disp, rows, lists, sends)


def vmem(count):
    return [pl.BlockSpec(memory_space=pltpu.VMEM)] * count


def shape(*dims):
    return jax.ShapeDtypeStruct(dims, F32)


def call(kernel, inputs, outputs, name, smem=(), far=(), scratch=(), vmem_bytes=VMEM_BYTES):
    specs = [
        pl.BlockSpec(
            memory_space=pltpu.SMEM if i in smem else pl.ANY if i in far else pltpu.VMEM
        )
        for i in range(len(inputs))
    ]
    return pl.pallas_call(
        kernel,
        out_shape=tuple(outputs),
        in_specs=specs,
        out_specs=tuple(vmem(len(outputs))),
        scratch_shapes=list(scratch),
        compiler_params=pltpu.CompilerParams(vmem_limit_bytes=vmem_bytes),
        name=name,
    )(*inputs)


def partners():
    px, py = lax.axis_size("px"), lax.axis_size("py")
    number = lambda i, j: i * py + j
    swaps = [[] for _ in range(4)]
    for i in range(px):
        for j in range(py):
            me = number(i, j)
            swaps[0].append((me, number(i ^ 1, j)))
            other = i - 1 if i % 2 == 0 else i + 1
            swaps[1].append((me, number(other, j) if 0 <= other < px else number(i, j ^ 1)))
            swaps[2].append((me, number(i, j ^ 1)))
            other = j - 1 if j % 2 == 0 else j + 1
            swaps[3].append((me, number(i, other % py)))
    return swaps


def exchange(blocks, order):
    swaps = partners()
    return [lax.ppermute(blocks[n], ("px", "py"), swaps[n]) for n in order]


def swap(slots, devices, capacity):
    axes = ("px", "py")
    if capacity == LANES:
        return lax.all_to_all(slots, axes, 0, 0, tiled=True)
    ratio = LANES // capacity
    parts = jnp.transpose(slots.reshape(-1, 3, ratio, capacity), (0, 2, 1, 3)).reshape(
        devices, 3, capacity
    )
    moved = lax.all_to_all(parts, axes, 0, 0, tiled=True)
    return jnp.transpose(moved.reshape(-1, ratio, 3, capacity), (0, 2, 1, 3)).reshape(
        -1, 3, LANES
    )


def body(
    coords,
    displacement,
    velocity,
    inv_mass,
    ext_force,
    thickness,
    stiffness,
    elem_nodes,
    block_class,
    halo_lists,
    contact_nodes,
    contact_bucket,
    tile_pairs,
):
    rows = coords.shape[1] // LANES
    quarter = halo_lists.shape[1] // LANES
    elem_rows = elem_nodes.shape[1] // LANES
    devices = lax.axis_size("px") * lax.axis_size("py")
    capacity = 2 * contact_nodes.shape[0] // devices
    slot_rows = devices * capacity // LANES
    inv_mass = inv_mass.reshape(rows, LANES)
    thickness = thickness.reshape(elem_rows, LANES)
    nodal = shape(3 * rows, LANES)
    sent = [shape(3 * quarter, LANES)] * 4
    slots = shape(slot_rows, 3, LANES)

    counts = (lax.axis_size("px"), lax.axis_size("py"))
    corner_values = shape(12 * elem_rows, LANES)

    sources = [
        coords,
        displacement,
        contact_bucket.reshape(-1, LANES),
        contact_nodes.reshape(-1, LANES),
    ]
    inverse, outgoing = call(
        functools.partial(slots_kernel, devices, capacity),
        sources,
        [jax.ShapeDtypeStruct((slot_rows, LANES), I32), slots],
        "slots",
        far=range(4),
        scratch=[pltpu.VMEM(source.shape, source.dtype) for source in sources]
        + [pltpu.SemaphoreType.DMA((4,))],
        vmem_bytes=WHOLE_VMEM,
    )
    disp, lists, nodes, splat, *sends = call(
        functools.partial(prepare_kernel, counts),
        [displacement, halo_lists, elem_nodes, stiffness, inverse],
        [
            nodal,
            jax.ShapeDtypeStruct((4 * quarter, LANES), I32),
            jax.ShapeDtypeStruct((4 * elem_rows, LANES), I32),
            shape(144, LANES),
        ]
        + sent,
        "prepare",
        far=(4,),
    )
    pair_count = tile_pairs.shape[1]
    select, spread, slow = call(
        masks_kernel,
        [tile_pairs, block_class.reshape(1, -1), lists],
        [
            shape(2, LANES, LANES),
            jax.ShapeDtypeStruct((3 * slot_rows, pair_count * LANES), BF16),
            jax.ShapeDtypeStruct((elem_rows, LANES), I32),
        ],
        "masks",
        far=(2,),
    )
    vel = velocity
    for step_no in range(STEPS):
        for sub_no in range(SUBS):
            first = sub_no == 0
            last = sub_no == SUBS - 1
            final = last and step_no == STEPS - 1
            if first:
                arrived = swap(outgoing, devices, capacity)
                if step_no:
                    sends = call(sends_kernel, [disp, lists, outgoing], sent, "sends", far=(2,))
            recvs = exchange(sends, BESIDE if first else ALONE)
            (found,) = call(own_kernel, [disp, nodes], [corner_values], "own_corners")
            field = [found, *recvs, nodes, thickness, splat]
            if first:
                (held,) = call(
                    functools.partial(force_kernel, rows), field, [corner_values], "forces"
                )
                (pushes,) = call(
                    functools.partial(contact_kernel, pair_count),
                    [select, spread, arrived, held],
                    [slots],
                    "contact",
                    far=(3,),
                )
                returned = swap(pushes, devices, capacity)
                outs = call(
                    functools.partial(halo_sum_kernel, rows),
                    [held, nodes, pushes],
                    sent,
                    "halo_sum",
                    far=(2,),
                )
                forces = held
            else:
                forces, *outs = call(
                    functools.partial(later_kernel, rows),
                    field + [held, slow],
                    [corner_values] + sent,
                    "forces_halo_sum",
                )
            backs = exchange(outs, BESIDE if first else ALONE)
            (own,) = call(own_sum_kernel, [forces, nodes, outs[2]], [nodal], "own_sum", far=(2,))
            if first:
                inputs = [own, *backs, returned, inverse, lists, inv_mass, disp, vel]
                outputs = [nodal] * 3 + sent
                if step_no == 0:
                    inputs.append(ext_force)
                    outputs.append(nodal)
                else:
                    inputs.append(ext)
                vel, disp, contact, *sends = call(
                    functools.partial(first_update_kernel, step_no == 0),
                    inputs,
                    outputs,
                    "first_update",
                )
                if step_no == 0:
                    *sends, ext = sends
                continue
            inputs = [own, *backs, lists, ext, inv_mass, vel, disp, contact]
            if final:
                vel, disp = call(
                    functools.partial(update_kernel, "final"),
                    inputs,
                    [shape(3, rows * LANES)] * 2,
                    "final_update",
                )
            elif last:
                vel, disp, outgoing = call(
                    functools.partial(update_kernel, "last"),
                    inputs + [coords, inverse],
                    [nodal] * 2 + [slots],
                    "last_update",
                )
            else:
                vel, disp, *sends = call(
                    functools.partial(update_kernel, "inner"),
                    inputs,
                    [nodal] * 2 + sent,
                    "update",
                )
    return (disp, vel)


def solution(mesh):
    placed = (
        P(None, ("px", "py")),
        P(None, ("px", "py")),
        P(None, ("px", "py")),
        P(("px", "py")),
        P(None, ("px", "py")),
        P(("px", "py")),
        P(),
        P(None, ("px", "py")),
        P(("px", "py")),
        P(None, ("px", "py")),
        P(("px", "py")),
        P(("px", "py"), None),
        P(None, ("px", "py")),
    )
    return jax.shard_map(
        body,
        mesh=mesh,
        in_specs=placed,
        out_specs=(P(None, ("px", "py")), P(None, ("px", "py"))),
        check_vma=False,
    )
```

```python
import functools

import jax
import jax.numpy as jnp
from jax import lax
from jax.experimental import pallas as pl
from jax.experimental.pallas import tpu as pltpu
from jax.sharding import PartitionSpec as P

LANES = 128
EBLK = 128
STEPS = 2
SUBS = 2

FAR = 10000.0
DT = 0.05
PENALTY = 0.5
REACH = 4.0

F32 = jnp.float32
BF16 = jnp.bfloat16
I32 = jnp.int32

VMEM_BYTES = 32 * 1024 * 1024
WHOLE_VMEM = 64 * 1024 * 1024


BESIDE = (1, 3, 0, 2)
ALONE = (1, 3, 0, 2)


def lookup(table_row, rows, index, start=None):
    parts = []
    for at in range(0, index.shape[0], 8):
        block = index[at : at + 8]
        hi = block >> 7
        lo = block & (LANES - 1)
        if start is None:
            found = [jnp.zeros(block.shape, F32) for _ in range(3)]
        else:
            found = [start[c][at : at + 8] for c in range(3)]
        for h in rows:
            here = hi == h
            for c in range(3):
                row = jnp.broadcast_to(table_row(c, h), block.shape)
                got = jnp.take_along_axis(row, lo, axis=1, mode="promise_in_bounds")
                found[c] = jnp.where(here, got, found[c])
        parts.append(found)
    return [jnp.concatenate([part[c] for part in parts], axis=0) for c in range(3)]


def halves(values):
    top = values.astype(BF16).astype(F32)
    return [top, values - top]


def scatter_dot(hi_rows, lo_rows, value_rows, rows, first=0):
    row_no = first + lax.broadcasted_iota(I32, (rows, LANES), 0)
    total = None
    lane_no = lax.broadcasted_iota(I32, (LANES, LANES), 0)
    group = 2
    for start in range(0, len(hi_rows), group):
        lefts, rights = [], []
        for r in range(start, start + group):
            here = row_no == hi_rows[r]
            lefts.append(
                jnp.concatenate(
                    [
                        jnp.where(here, jnp.broadcast_to(vals[r], (rows, LANES)), 0.0)
                        for vals in value_rows
                    ],
                    axis=0,
                ).astype(BF16)
            )
            rights.append((lane_no == lo_rows[r]).astype(F32).astype(BF16))
        part = lax.dot_general(
            jnp.concatenate(lefts, axis=1),
            jnp.concatenate(rights, axis=1),
            (((1,), (1,)), ((), ())),
            preferred_element_type=F32,
        )
        total = part if total is None else total + part
    return total


def scatter_add(index_row, value_row, count, rows, first=0):
    hi_rows, lo_rows = [], []
    value_rows = [[] for _ in range(6)]
    for r in range(count):
        idx = index_row(r)
        hi_rows.append(idx >> 7)
        lo_rows.append(idx & (LANES - 1))
        for c in range(3):
            for part, vals in enumerate(halves(value_row(c, r))):
                value_rows[2 * c + part].append(vals)
    total = scatter_dot(hi_rows, lo_rows, value_rows, rows, first)
    return [
        total[2 * c * rows : (2 * c + 1) * rows] + total[(2 * c + 1) * rows : (2 * c + 2) * rows]
        for c in range(3)
    ]


def in_place(refs, order):
    return [refs[order.index(n)] for n in range(4)]


def spread_rows(source, target, groups):
    rows = source.shape[1] // LANES
    for g in range(groups):
        for h in range(rows):
            target[g * rows + h : g * rows + h + 1, :] = source[
                g : g + 1, h * LANES : (h + 1) * LANES
            ]


def gather_halo(disp, rows, lists, sends):
    found = lookup(lambda c, h: disp[c * rows + h : c * rows + h + 1, :], range(rows), lists[...])
    quarter = lists.shape[0] // 4
    for b in range(4):
        for c in range(3):
            sends[b][c * quarter : (c + 1) * quarter, :] = found[c][b * quarter : (b + 1) * quarter]


def gather_slots(position_row, rows, inverse, outgoing):
    slot_node = inverse[...]
    found = lookup(position_row, range(rows), jnp.maximum(slot_node, 0))
    for c in range(3):
        outgoing[:, c, :] = jnp.where(slot_node >= 0, found[c], FAR)


def block_remap(index, own_count, width, px_no, py_no, px_count, py_count):
    block = (index - own_count) >> (width.bit_length() - 1)
    along_x = block < 2
    place = jnp.where(along_x, px_no, py_no)
    ends = jnp.where(along_x, px_count - 1, py_count - 1)
    edge = jnp.where((block & 1) == 0, 0, ends)
    moved = index ^ ((1 - (place & 1)) * width)
    moved = jnp.where(place == edge, -1, moved)
    return jnp.where(index < own_count, index, moved)


def slots_kernel(devices, capacity, *refs):
    sources, (inverse, outgoing) = refs[:4], refs[4:6]
    buffers, sems = refs[6:10], refs[10]
    coords, disp, bucket, contact_nodes = buffers
    copies = [
        pltpu.make_async_copy(source, target, sems.at[n])
        for n, (source, target) in enumerate(zip(sources, buffers))
    ]
    for copy in copies:
        copy.start()
    for copy in copies[2:]:
        copy.wait()
    count = bucket.shape[0]
    slot_rows = inverse.shape[0]
    dev_no = lax.broadcasted_iota(I32, (devices, LANES), 0)
    first = lax.broadcasted_iota(I32, (LANES, 2 * LANES), 0)
    second = lax.broadcasted_iota(I32, (LANES, 2 * LANES), 1)
    before = ((first < second) | (second >= LANES)).astype(F32).astype(BF16)
    base = jnp.zeros((devices, LANES), F32)
    hi_rows, lo_rows, digits = [], [], [[], []]
    for r in range(count):
        b = bucket[r : r + 1, :]
        onehot = (dev_no == b).astype(F32)
        sums = jnp.dot(onehot.astype(BF16), before, preferred_element_type=F32)
        rank = jnp.sum(onehot * (sums[:, :LANES] + base), axis=0, keepdims=True)
        base = base + sums[:, LANES:]
        slot = b * capacity + rank.astype(I32)
        hi_rows.append(slot >> 7)
        lo_rows.append(slot & (LANES - 1))
        value = contact_nodes[r : r + 1, :] + 1
        digits[0].append((value >> 6).astype(F32))
        digits[1].append((value & 63).astype(F32))
    total = scatter_dot(hi_rows, lo_rows, digits, slot_rows)
    inverse[...] = (total[:slot_rows] * 64.0 + total[slot_rows:]).astype(I32) - 1
    for copy in copies[:2]:
        copy.wait()

    def position_row(c, h):
        span = slice(h * LANES, (h + 1) * LANES)
        return coords[c : c + 1, span] + disp[c : c + 1, span]

    gather_slots(position_row, coords.shape[1] // LANES, inverse, outgoing)


def prepare_kernel(counts, *refs):
    (disp_in, lists_in, nodes_in, stiff, after) = refs[:5]
    (disp, lists, nodes, splat) = refs[5:9]
    sends = refs[9:]
    px_no = lax.axis_index("px")
    py_no = lax.axis_index("py")
    own_count = disp_in.shape[1]
    rows = own_count // LANES
    spread_rows(disp_in, disp, 3)
    width = lists_in.shape[1]
    quarter = width // LANES
    for b in range(4):
        place = px_no if b < 2 else py_no
        count = counts[b // 2]
        to_high = (place & 1) ^ (1 - b % 2)
        row = (b // 2) * 2
        missing = (place == to_high * (count - 1)).astype(I32)
        for q in range(quarter):
            span = slice(q * LANES, (q + 1) * LANES)
            chosen = jnp.where(
                jnp.full((1, LANES), to_high) == 1,
                lists_in[row + 1 : row + 2, span],
                lists_in[row : row + 1, span],
            )
            lists[b * quarter + q : b * quarter + q + 1, :] = jnp.where(
                jnp.full((1, LANES), missing) == 1, -1, chosen
            )
    gather_halo(disp, rows, lists, sends)
    spread_rows(nodes_in, nodes, 4)
    nodes[...] = block_remap(nodes[...], own_count, width, px_no, py_no, *counts)
    size = stiff.shape[0]
    for j in range(size):
        splat[j * size : (j + 1) * size, :] = jnp.broadcast_to(stiff[:, j : j + 1], (size, LANES))


def masks_kernel(pairs, classes, after, select, spread, slow):
    pair_count = pairs.shape[1]
    row = pairs[0:1, :]
    if pair_count < LANES:
        row = jnp.concatenate([row, jnp.full((1, LANES - pair_count), -1)], axis=1)
    onehot = (lax.broadcasted_iota(I32, (LANES, LANES), 0) == row).astype(F32)
    select[0] = onehot
    select[1] = jnp.transpose(onehot)
    tiles = spread.shape[0] // 3
    tile_no = lax.broadcasted_iota(I32, (tiles, LANES), 0)
    tile_no = jnp.concatenate([tile_no] * 3, axis=0)
    for p in range(pair_count):
        other = jnp.broadcast_to(pairs[1:2, p : p + 1], tile_no.shape)
        spread[:, p * LANES : (p + 1) * LANES] = (tile_no == other).astype(F32).astype(BF16)
    blocks = classes.shape[1]
    row = jnp.concatenate([classes[...], jnp.zeros((1, LANES - blocks), I32)], axis=1)
    slow[...] = jnp.transpose(jnp.broadcast_to(row, (LANES, LANES)))[:blocks]


def own_kernel(disp, nodes, found):
    rows = disp.shape[0] // 3
    count = nodes.shape[0]
    values = lookup(
        lambda c, h: disp[c * rows + h : c * rows + h + 1, :], range(rows), nodes[...]
    )
    for c in range(3):
        found[c * count : (c + 1) * count, :] = values[c]


def corner_forces(found, rows, recvs, nodes, thick, splat):
    quarter = recvs[0].shape[0] // 3
    elem_rows = thick.shape[0]

    def table_row(c, h):
        b, q = divmod(h - rows, quarter)
        return recvs[b][c * quarter + q : c * quarter + q + 1, :]

    count = nodes.shape[0]
    corners = []
    for k in range(4):
        span = slice(k * elem_rows, (k + 1) * elem_rows)
        own = [found[c * count + span.start : c * count + span.stop, :] for c in range(3)]
        corners.append(
            lookup(table_row, range(rows, rows + 4 * quarter), nodes[span, :], own)
        )
    factor = thick[...]
    forces = []
    for i in range(12):
        total = None
        for j in range(12):
            term = splat[j * 12 + i : j * 12 + i + 1, :] * corners[j % 4][j // 4]
            total = term if total is None else total + term
        forces.append(factor * total)
    return forces


def stored_row(forces, nodes):
    count = nodes.shape[0]
    return lambda c, r: forces[c * count + r : c * count + r + 1, :]


def sum_own(force_row, nodes, own):
    rows = own.shape[0] // 3
    sums = scatter_add(lambda r: nodes[r : r + 1, :], force_row, nodes.shape[0], rows)
    for c in range(3):
        own[c * rows : (c + 1) * rows, :] = sums[c]


def sum_halo(force_row, nodes, rows, outs):
    quarter = outs[0].shape[0] // 3
    sums = scatter_add(
        lambda r: nodes[r : r + 1, :], force_row, nodes.shape[0], 4 * quarter, rows
    )
    for c in range(3):
        for b in range(4):
            outs[b][c * quarter : (c + 1) * quarter, :] = sums[c][b * quarter : (b + 1) * quarter]


def force_kernel(rows, found, *refs):
    recvs = in_place(refs[:4], BESIDE)
    nodes, thick, splat, held = refs[4:]
    elem_rows = thick.shape[0]
    forces = corner_forces(found, rows, recvs, nodes, thick, splat)
    for i in range(12):
        held[i * elem_rows : (i + 1) * elem_rows, :] = forces[i]


def halo_sum_kernel(rows, held, nodes, *outs):
    sum_halo(stored_row(held, nodes), nodes, rows, outs)


def after_kernel(kernel, place, *refs):
    kernel(*refs[:place], *refs[place + 1 :])


def own_sum_kernel(held, nodes, after, own):
    sum_own(stored_row(held, nodes), nodes, own)


def later_force_kernel(rows, found, *refs):
    recvs = in_place(refs[:4], ALONE)
    nodes, thick, splat, held, slow, mixed = refs[4:]
    elem_rows = thick.shape[0]
    forces = corner_forces(found, rows, recvs, nodes, thick, splat)
    kept = slow[...] == 1
    for i in range(12):
        span = slice(i * elem_rows, (i + 1) * elem_rows)
        mixed[span, :] = jnp.where(kept, held[span, :], forces[i])


def returned_sums(backs, lists, rows):
    quarter = backs[0].shape[0] // 3

    def back_row(c, r):
        b, q = divmod(r, quarter)
        return backs[b][c * quarter + q : c * quarter + q + 1, :]

    return scatter_add(lambda r: lists[r : r + 1, :], back_row, 4 * quarter, rows)


def sends_kernel(disp, lists, after, *sends):
    gather_halo(disp, disp.shape[0] // 3, lists, sends)


def thirds(values):
    parts = []
    for _ in range(3):
        top = values.astype(BF16)
        parts.append(top)
        values = values - top.astype(F32)
    return parts


def dot_thirds(onehot, values):
    width = values.shape[1]
    sums = jnp.dot(
        onehot.astype(BF16),
        jnp.concatenate(thirds(values), axis=1),
        preferred_element_type=F32,
    )
    return sums[:, :width] + sums[:, width : 2 * width] + sums[:, 2 * width :]


def contact_kernel(pair_count, select, spread, arrived, after, pushes):
    tiles = arrived.shape[0]
    points = [arrived[:, c, :] for c in range(3)]
    first = dot_thirds(select[1, :pair_count, :tiles], jnp.concatenate(points, axis=1))
    second = []
    for c in range(3):
        parts = [part.astype(F32) for part in thirds(points[c])]
        rest = LANES - 3 * tiles
        if rest:
            parts.append(jnp.zeros((rest, LANES), F32))
        turned = jnp.transpose(jnp.concatenate(parts, axis=0))[:, : 3 * tiles].astype(BF16)
        second.append(jnp.dot(turned, spread[...], preferred_element_type=F32))
    pushed = []
    for p in range(pair_count):
        gaps = [
            jnp.broadcast_to(first[p : p + 1, c * LANES : (c + 1) * LANES], (LANES, LANES))
            - second[c][:, p * LANES : (p + 1) * LANES]
            for c in range(3)
        ]
        dist = gaps[0] * gaps[0] + gaps[1] * gaps[1] + gaps[2] * gaps[2]
        weight = jnp.exp(dist * (-1.0 / REACH))
        pushed.append(
            jnp.concatenate(
                [jnp.sum(weight * gaps[c], axis=0, keepdims=True) for c in range(3)], axis=1
            )
        )
    total = PENALTY * dot_thirds(select[0, :tiles, :pair_count], jnp.concatenate(pushed, axis=0))
    for c in range(3):
        pushes[:, c, :] = total[:, c * LANES : (c + 1) * LANES]


def advance(internal, contact, ext, inv_mass, vel, disp, rows):
    for c in range(3):
        span = slice(c * rows, (c + 1) * rows)
        accel = inv_mass[...] * (ext[span, :] - internal[c] + contact[c])
        vel_c = vel[span, :] + DT * accel
        yield c, vel_c, disp[span, :] + DT * vel_c


def components(array):
    rows = array.shape[0] // 3
    return [array[c * rows : (c + 1) * rows, :] for c in range(3)]


def first_update_kernel(starting, *refs):
    refs = list(refs)
    own = refs[0]
    returned, inverse, lists, inv_mass, disp, vel, ext = refs[5:12]
    new_vel, new_disp, contact, *sends = refs[12:]
    rows = disp.shape[0] // 3
    backs = returned_sums(in_place(refs[1:5], BESIDE), lists, rows)
    internal = [mine + more for mine, more in zip(components(own), backs)]
    if starting:
        *sends, ext_rows = sends
        spread_rows(vel, new_vel, 3)
        spread_rows(ext, ext_rows, 3)
        vel, ext = new_vel, ext_rows
    sums = scatter_add(
        lambda r: inverse[r : r + 1, :],
        lambda c, r: returned[r, c : c + 1, :],
        inverse.shape[0],
        rows,
    )
    steps = advance(internal, sums, ext, inv_mass, vel, disp, rows)
    for c, vel_c, disp_c in steps:
        span = slice(c * rows, (c + 1) * rows)
        contact[span, :] = sums[c]
        new_vel[span, :] = vel_c
        new_disp[span, :] = disp_c
    gather_halo(new_disp, rows, lists, sends)


def update_kernel(case, *refs):
    own = refs[0]
    lists, ext, inv_mass, vel, disp, contact = refs[5:11]
    rows = disp.shape[0] // 3
    sums = returned_sums(in_place(refs[1:5], ALONE), lists, rows)
    internal = [mine + more for mine, more in zip(components(own), sums)]
    steps = advance(internal, components(contact), ext, inv_mass, vel, disp, rows)
    if case == "final":
        new_vel, new_disp = refs[11:]
        for c, vel_c, disp_c in steps:
            for h in range(rows):
                new_vel[c : c + 1, h * LANES : (h + 1) * LANES] = vel_c[h : h + 1, :]
                new_disp[c : c + 1, h * LANES : (h + 1) * LANES] = disp_c[h : h + 1, :]
        return
    if case == "last":
        coords, inverse, new_vel, new_disp, outgoing = refs[11:]
    else:
        new_vel, new_disp, *sends = refs[11:]
    for c, vel_c, disp_c in steps:
        new_vel[c * rows : (c + 1) * rows, :] = vel_c
        new_disp[c * rows : (c + 1) * rows, :] = disp_c
    if case == "last":

        def position_row(c, h):
            mine = coords[c : c + 1, h * LANES : (h + 1) * LANES]
            return mine + new_disp[c * rows + h : c * rows + h + 1, :]

        gather_slots(position_row, rows, inverse, outgoing)
    else:
        gather_halo(new_disp, rows, lists, sends)


def vmem(count):
    return [pl.BlockSpec(memory_space=pltpu.VMEM)] * count


def shape(*dims):
    return jax.ShapeDtypeStruct(dims, F32)


def call(kernel, inputs, outputs, name, smem=(), far=(), scratch=(), vmem_bytes=VMEM_BYTES):
    specs = [
        pl.BlockSpec(
            memory_space=pltpu.SMEM if i in smem else pl.ANY if i in far else pltpu.VMEM
        )
        for i in range(len(inputs))
    ]
    return pl.pallas_call(
        kernel,
        out_shape=tuple(outputs),
        in_specs=specs,
        out_specs=tuple(vmem(len(outputs))),
        scratch_shapes=list(scratch),
        compiler_params=pltpu.CompilerParams(vmem_limit_bytes=vmem_bytes),
        name=name,
    )(*inputs)


def partners():
    px, py = lax.axis_size("px"), lax.axis_size("py")
    number = lambda i, j: i * py + j
    swaps = [[] for _ in range(4)]
    for i in range(px):
        for j in range(py):
            me = number(i, j)
            swaps[0].append((me, number(i ^ 1, j)))
            other = i - 1 if i % 2 == 0 else i + 1
            swaps[1].append((me, number(other, j) if 0 <= other < px else number(i, j ^ 1)))
            swaps[2].append((me, number(i, j ^ 1)))
            other = j - 1 if j % 2 == 0 else j + 1
            swaps[3].append((me, number(i, other % py)))
    return swaps


def exchange(blocks, order):
    swaps = partners()
    return [lax.ppermute(blocks[n], ("px", "py"), swaps[n]) for n in order]


def swap(slots, devices, capacity):
    axes = ("px", "py")
    if capacity == LANES:
        return lax.all_to_all(slots, axes, 0, 0, tiled=True)
    ratio = LANES // capacity
    parts = jnp.transpose(slots.reshape(-1, 3, ratio, capacity), (0, 2, 1, 3)).reshape(
        devices, 3, capacity
    )
    moved = lax.all_to_all(parts, axes, 0, 0, tiled=True)
    return jnp.transpose(moved.reshape(-1, ratio, 3, capacity), (0, 2, 1, 3)).reshape(
        -1, 3, LANES
    )


def body(
    coords,
    displacement,
    velocity,
    inv_mass,
    ext_force,
    thickness,
    stiffness,
    elem_nodes,
    block_class,
    halo_lists,
    contact_nodes,
    contact_bucket,
    tile_pairs,
):
    rows = coords.shape[1] // LANES
    quarter = halo_lists.shape[1] // LANES
    elem_rows = elem_nodes.shape[1] // LANES
    devices = lax.axis_size("px") * lax.axis_size("py")
    capacity = 2 * contact_nodes.shape[0] // devices
    slot_rows = devices * capacity // LANES
    inv_mass = inv_mass.reshape(rows, LANES)
    thickness = thickness.reshape(elem_rows, LANES)
    nodal = shape(3 * rows, LANES)
    sent = [shape(3 * quarter, LANES)] * 4
    slots = shape(slot_rows, 3, LANES)

    counts = (lax.axis_size("px"), lax.axis_size("py"))
    corner_values = shape(12 * elem_rows, LANES)

    sources = [
        coords,
        displacement,
        contact_bucket.reshape(-1, LANES),
        contact_nodes.reshape(-1, LANES),
    ]
    inverse, outgoing = call(
        functools.partial(slots_kernel, devices, capacity),
        sources,
        [jax.ShapeDtypeStruct((slot_rows, LANES), I32), slots],
        "slots",
        far=range(4),
        scratch=[pltpu.VMEM(source.shape, source.dtype) for source in sources]
        + [pltpu.SemaphoreType.DMA((4,))],
        vmem_bytes=WHOLE_VMEM,
    )
    disp, lists, nodes, splat, *sends = call(
        functools.partial(prepare_kernel, counts),
        [displacement, halo_lists, elem_nodes, stiffness, inverse],
        [
            nodal,
            jax.ShapeDtypeStruct((4 * quarter, LANES), I32),
            jax.ShapeDtypeStruct((4 * elem_rows, LANES), I32),
            shape(144, LANES),
        ]
        + sent,
        "prepare",
        far=(4,),
    )
    pair_count = tile_pairs.shape[1]
    select, spread, slow = call(
        masks_kernel,
        [tile_pairs, block_class.reshape(1, -1), lists],
        [
            shape(2, LANES, LANES),
            jax.ShapeDtypeStruct((3 * slot_rows, pair_count * LANES), BF16),
            jax.ShapeDtypeStruct((elem_rows, LANES), I32),
        ],
        "masks",
        far=(2,),
    )
    vel = velocity
    for step_no in range(STEPS):
        for sub_no in range(SUBS):
            first = sub_no == 0
            last = sub_no == SUBS - 1
            final = last and step_no == STEPS - 1
            if first:
                arrived = swap(outgoing, devices, capacity)
                if step_no:
                    sends = call(sends_kernel, [disp, lists, outgoing], sent, "sends", far=(2,))
            recvs = exchange(sends, BESIDE if first else ALONE)
            (found,) = call(own_kernel, [disp, nodes], [corner_values], "own_corners")
            field = [found, *recvs, nodes, thickness, splat]
            if first:
                (held,) = call(
                    functools.partial(force_kernel, rows), field, [corner_values], "forces"
                )
                (pushes,) = call(
                    functools.partial(contact_kernel, pair_count),
                    [select, spread, arrived, held],
                    [slots],
                    "contact",
                    far=(3,),
                )
                returned = swap(pushes, devices, capacity)
                outs = call(
                    functools.partial(after_kernel, functools.partial(halo_sum_kernel, rows), 2),
                    [held, nodes, pushes],
                    sent,
                    "halo_sum",
                    far=(2,),
                )
                forces = held
            else:
                (forces,) = call(
                    functools.partial(later_force_kernel, rows),
                    field + [held, slow],
                    [corner_values],
                    "forces_later",
                )
                outs = call(
                    functools.partial(halo_sum_kernel, rows), [forces, nodes], sent, "halo_sum"
                )
            backs = exchange(outs, BESIDE if first else ALONE)
            (own,) = call(own_sum_kernel, [forces, nodes, outs[2]], [nodal], "own_sum", far=(2,))
            if first:
                inputs = [own, *backs, returned, inverse, lists, inv_mass, disp, vel]
                outputs = [nodal] * 3 + sent
                if step_no == 0:
                    inputs.append(ext_force)
                    outputs.append(nodal)
                else:
                    inputs.append(ext)
                vel, disp, contact, *sends = call(
                    functools.partial(first_update_kernel, step_no == 0),
                    inputs,
                    outputs,
                    "first_update",
                )
                if step_no == 0:
                    *sends, ext = sends
                continue
            inputs = [own, *backs, lists, ext, inv_mass, vel, disp, contact]
            if final:
                vel, disp = call(
                    functools.partial(update_kernel, "final"),
                    inputs,
                    [shape(3, rows * LANES)] * 2,
                    "final_update",
                )
            elif last:
                vel, disp, outgoing = call(
                    functools.partial(update_kernel, "last"),
                    inputs + [coords, inverse],
                    [nodal] * 2 + [slots],
                    "last_update",
                )
            else:
                vel, disp, *sends = call(
                    functools.partial(update_kernel, "inner"),
                    inputs,
                    [nodal] * 2 + sent,
                    "update",
                )
    return (disp, vel)


def solution(mesh):
    placed = (
        P(None, ("px", "py")),
        P(None, ("px", "py")),
        P(None, ("px", "py")),
        P(("px", "py")),
        P(None, ("px", "py")),
        P(("px", "py")),
        P(),
        P(None, ("px", "py")),
        P(("px", "py")),
        P(None, ("px", "py")),
        P(("px", "py")),
        P(("px", "py"), None),
        P(None, ("px", "py")),
    )
    return jax.shard_map(
        body,
        mesh=mesh,
        in_specs=placed,
        out_specs=(P(None, ("px", "py")), P(None, ("px", "py"))),
        check_vma=False,
    )
```

```python
import functools

import jax
import jax.numpy as jnp
from jax import lax
from jax.experimental import pallas as pl
from jax.experimental.pallas import tpu as pltpu
from jax.sharding import PartitionSpec as P

LANES = 128
EBLK = 128
STEPS = 2
SUBS = 2

FAR = 10000.0
DT = 0.05
PENALTY = 0.5
REACH = 4.0

F32 = jnp.float32
BF16 = jnp.bfloat16
I32 = jnp.int32

VMEM_BYTES = 32 * 1024 * 1024
WHOLE_VMEM = 64 * 1024 * 1024


BESIDE = (1, 3, 0, 2)
ALONE = (1, 3, 0, 2)


def lookup(table_row, rows, index, start=None):
    parts = []
    for at in range(0, index.shape[0], 8):
        block = index[at : at + 8]
        hi = block >> 7
        lo = block & (LANES - 1)
        if start is None:
            found = [jnp.zeros(block.shape, F32) for _ in range(3)]
        else:
            found = [start[c][at : at + 8] for c in range(3)]
        for h in rows:
            here = hi == h
            for c in range(3):
                row = jnp.broadcast_to(table_row(c, h), block.shape)
                got = jnp.take_along_axis(row, lo, axis=1, mode="promise_in_bounds")
                found[c] = jnp.where(here, got, found[c])
        parts.append(found)
    return [jnp.concatenate([part[c] for part in parts], axis=0) for c in range(3)]


def halves(values):
    top = values.astype(BF16).astype(F32)
    return [top, values - top]


def scatter_dot(hi_rows, lo_rows, value_rows, rows, first=0):
    row_no = first + lax.broadcasted_iota(I32, (rows, LANES), 0)
    total = None
    lane_no = lax.broadcasted_iota(I32, (LANES, LANES), 0)
    group = 2
    for start in range(0, len(hi_rows), group):
        lefts, rights = [], []
        for r in range(start, start + group):
            here = row_no == hi_rows[r]
            lefts.append(
                jnp.concatenate(
                    [
                        jnp.where(here, jnp.broadcast_to(vals[r], (rows, LANES)), 0.0)
                        for vals in value_rows
                    ],
                    axis=0,
                ).astype(BF16)
            )
            rights.append((lane_no == lo_rows[r]).astype(F32).astype(BF16))
        part = lax.dot_general(
            jnp.concatenate(lefts, axis=1),
            jnp.concatenate(rights, axis=1),
            (((1,), (1,)), ((), ())),
            preferred_element_type=F32,
        )
        total = part if total is None else total + part
    return total


def scatter_add(index_row, value_row, count, rows, first=0):
    hi_rows, lo_rows = [], []
    value_rows = [[] for _ in range(6)]
    for r in range(count):
        idx = index_row(r)
        hi_rows.append(idx >> 7)
        lo_rows.append(idx & (LANES - 1))
        for c in range(3):
            for part, vals in enumerate(halves(value_row(c, r))):
                value_rows[2 * c + part].append(vals)
    total = scatter_dot(hi_rows, lo_rows, value_rows, rows, first)
    return [
        total[2 * c * rows : (2 * c + 1) * rows] + total[(2 * c + 1) * rows : (2 * c + 2) * rows]
        for c in range(3)
    ]


def in_place(refs, order):
    return [refs[order.index(n)] for n in range(4)]


def spread_rows(source, target, groups):
    rows = source.shape[1] // LANES
    for g in range(groups):
        for h in range(rows):
            target[g * rows + h : g * rows + h + 1, :] = source[
                g : g + 1, h * LANES : (h + 1) * LANES
            ]


def gather_halo(disp, rows, lists, sends):
    found = lookup(lambda c, h: disp[c * rows + h : c * rows + h + 1, :], range(rows), lists[...])
    quarter = lists.shape[0] // 4
    for b in range(4):
        for c in range(3):
            sends[b][c * quarter : (c + 1) * quarter, :] = found[c][b * quarter : (b + 1) * quarter]


def gather_slots(position_row, rows, inverse, outgoing):
    slot_node = inverse[...]
    found = lookup(position_row, range(rows), jnp.maximum(slot_node, 0))
    for c in range(3):
        outgoing[:, c, :] = jnp.where(slot_node >= 0, found[c], FAR)


def block_remap(index, own_count, width, px_no, py_no, px_count, py_count):
    block = (index - own_count) >> (width.bit_length() - 1)
    along_x = block < 2
    place = jnp.where(along_x, px_no, py_no)
    ends = jnp.where(along_x, px_count - 1, py_count - 1)
    edge = jnp.where((block & 1) == 0, 0, ends)
    moved = index ^ ((1 - (place & 1)) * width)
    moved = jnp.where(place == edge, -1, moved)
    return jnp.where(index < own_count, index, moved)


def slots_kernel(devices, capacity, *refs):
    sources, (inverse, outgoing) = refs[:4], refs[4:6]
    buffers, sems = refs[6:10], refs[10]
    coords, disp, bucket, contact_nodes = buffers
    copies = [
        pltpu.make_async_copy(source, target, sems.at[n])
        for n, (source, target) in enumerate(zip(sources, buffers))
    ]
    for copy in copies:
        copy.start()
    for copy in copies[2:]:
        copy.wait()
    count = bucket.shape[0]
    slot_rows = inverse.shape[0]
    dev_no = lax.broadcasted_iota(I32, (devices, LANES), 0)
    first = lax.broadcasted_iota(I32, (LANES, 2 * LANES), 0)
    second = lax.broadcasted_iota(I32, (LANES, 2 * LANES), 1)
    before = ((first < second) | (second >= LANES)).astype(F32).astype(BF16)
    base = jnp.zeros((devices, LANES), F32)
    hi_rows, lo_rows, digits = [], [], [[], []]
    for r in range(count):
        b = bucket[r : r + 1, :]
        onehot = (dev_no == b).astype(F32)
        sums = jnp.dot(onehot.astype(BF16), before, preferred_element_type=F32)
        rank = jnp.sum(onehot * (sums[:, :LANES] + base), axis=0, keepdims=True)
        base = base + sums[:, LANES:]
        slot = b * capacity + rank.astype(I32)
        hi_rows.append(slot >> 7)
        lo_rows.append(slot & (LANES - 1))
        value = contact_nodes[r : r + 1, :] + 1
        digits[0].append((value >> 6).astype(F32))
        digits[1].append((value & 63).astype(F32))
    total = scatter_dot(hi_rows, lo_rows, digits, slot_rows)
    inverse[...] = (total[:slot_rows] * 64.0 + total[slot_rows:]).astype(I32) - 1
    for copy in copies[:2]:
        copy.wait()

    def position_row(c, h):
        span = slice(h * LANES, (h + 1) * LANES)
        return coords[c : c + 1, span] + disp[c : c + 1, span]

    gather_slots(position_row, coords.shape[1] // LANES, inverse, outgoing)


def prepare_kernel(counts, *refs):
    (disp_in, lists_in, nodes_in, stiff, after) = refs[:5]
    (disp, lists, nodes, splat) = refs[5:9]
    sends = refs[9:]
    px_no = lax.axis_index("px")
    py_no = lax.axis_index("py")
    own_count = disp_in.shape[1]
    rows = own_count // LANES
    spread_rows(disp_in, disp, 3)
    width = lists_in.shape[1]
    quarter = width // LANES
    for b in range(4):
        place = px_no if b < 2 else py_no
        count = counts[b // 2]
        to_high = (place & 1) ^ (1 - b % 2)
        row = (b // 2) * 2
        missing = (place == to_high * (count - 1)).astype(I32)
        for q in range(quarter):
            span = slice(q * LANES, (q + 1) * LANES)
            chosen = jnp.where(
                jnp.full((1, LANES), to_high) == 1,
                lists_in[row + 1 : row + 2, span],
                lists_in[row : row + 1, span],
            )
            lists[b * quarter + q : b * quarter + q + 1, :] = jnp.where(
                jnp.full((1, LANES), missing) == 1, -1, chosen
            )
    gather_halo(disp, rows, lists, sends)
    spread_rows(nodes_in, nodes, 4)
    nodes[...] = block_remap(nodes[...], own_count, width, px_no, py_no, *counts)
    size = stiff.shape[0]
    for j in range(size):
        splat[j * size : (j + 1) * size, :] = jnp.broadcast_to(stiff[:, j : j + 1], (size, LANES))


def masks_kernel(pairs, classes, after, select, spread, slow):
    pair_count = pairs.shape[1]
    row = pairs[0:1, :]
    if pair_count < LANES:
        row = jnp.concatenate([row, jnp.full((1, LANES - pair_count), -1)], axis=1)
    onehot = (lax.broadcasted_iota(I32, (LANES, LANES), 0) == row).astype(F32)
    select[0] = onehot
    select[1] = jnp.transpose(onehot)
    tiles = spread.shape[0] // 3
    tile_no = lax.broadcasted_iota(I32, (tiles, LANES), 0)
    tile_no = jnp.concatenate([tile_no] * 3, axis=0)
    for p in range(pair_count):
        other = jnp.broadcast_to(pairs[1:2, p : p + 1], tile_no.shape)
        spread[:, p * LANES : (p + 1) * LANES] = (tile_no == other).astype(F32).astype(BF16)
    blocks = classes.shape[1]
    row = jnp.concatenate([classes[...], jnp.zeros((1, LANES - blocks), I32)], axis=1)
    slow[...] = jnp.transpose(jnp.broadcast_to(row, (LANES, LANES)))[:blocks]


def own_kernel(disp, nodes, found):
    rows = disp.shape[0] // 3
    count = nodes.shape[0]
    values = lookup(
        lambda c, h: disp[c * rows + h : c * rows + h + 1, :], range(rows), nodes[...]
    )
    for c in range(3):
        found[c * count : (c + 1) * count, :] = values[c]


def corner_forces(found, rows, recvs, nodes, thick, splat):
    quarter = recvs[0].shape[0] // 3
    elem_rows = thick.shape[0]

    def table_row(c, h):
        b, q = divmod(h - rows, quarter)
        return recvs[b][c * quarter + q : c * quarter + q + 1, :]

    count = nodes.shape[0]
    corners = []
    for k in range(4):
        span = slice(k * elem_rows, (k + 1) * elem_rows)
        own = [found[c * count + span.start : c * count + span.stop, :] for c in range(3)]
        corners.append(
            lookup(table_row, range(rows, rows + 4 * quarter), nodes[span, :], own)
        )
    factor = thick[...]
    forces = []
    for i in range(12):
        total = None
        for j in range(12):
            term = splat[j * 12 + i : j * 12 + i + 1, :] * corners[j % 4][j // 4]
            total = term if total is None else total + term
        forces.append(factor * total)
    return forces


def stored_row(forces, nodes):
    count = nodes.shape[0]
    return lambda c, r: forces[c * count + r : c * count + r + 1, :]


def sum_own(force_row, nodes, own):
    rows = own.shape[0] // 3
    sums = scatter_add(lambda r: nodes[r : r + 1, :], force_row, nodes.shape[0], rows)
    for c in range(3):
        own[c * rows : (c + 1) * rows, :] = sums[c]


def sum_halo(force_row, nodes, rows, outs):
    quarter = outs[0].shape[0] // 3
    sums = scatter_add(
        lambda r: nodes[r : r + 1, :], force_row, nodes.shape[0], 4 * quarter, rows
    )
    for c in range(3):
        for b in range(4):
            outs[b][c * quarter : (c + 1) * quarter, :] = sums[c][b * quarter : (b + 1) * quarter]


def force_kernel(rows, found, *refs):
    recvs = in_place(refs[:4], BESIDE)
    nodes, thick, splat, held = refs[4:]
    elem_rows = thick.shape[0]
    forces = corner_forces(found, rows, recvs, nodes, thick, splat)
    for i in range(12):
        held[i * elem_rows : (i + 1) * elem_rows, :] = forces[i]


def halo_sum_kernel(rows, held, nodes, *outs):
    sum_halo(stored_row(held, nodes), nodes, rows, outs)


def after_kernel(kernel, place, *refs):
    kernel(*refs[:place], *refs[place + 1 :])


def own_sum_kernel(held, nodes, after, own):
    sum_own(stored_row(held, nodes), nodes, own)


def later_force_kernel(rows, found, *refs):
    recvs = in_place(refs[:4], ALONE)
    nodes, thick, splat, held, slow, mixed = refs[4:]
    elem_rows = thick.shape[0]
    forces = corner_forces(found, rows, recvs, nodes, thick, splat)
    kept = slow[...] == 1
    for i in range(12):
        span = slice(i * elem_rows, (i + 1) * elem_rows)
        mixed[span, :] = jnp.where(kept, held[span, :], forces[i])


def returned_sums(backs, lists, rows):
    quarter = backs[0].shape[0] // 3

    def back_row(c, r):
        b, q = divmod(r, quarter)
        return backs[b][c * quarter + q : c * quarter + q + 1, :]

    return scatter_add(lambda r: lists[r : r + 1, :], back_row, 4 * quarter, rows)


def contact_sum_kernel(returned, inverse, contact):
    rows = contact.shape[0] // 3
    sums = scatter_add(
        lambda r: inverse[r : r + 1, :],
        lambda c, r: returned[r, c : c + 1, :],
        inverse.shape[0],
        rows,
    )
    for c in range(3):
        contact[c * rows : (c + 1) * rows, :] = sums[c]


def sends_kernel(disp, lists, after, *sends):
    gather_halo(disp, disp.shape[0] // 3, lists, sends)


def thirds(values):
    parts = []
    for _ in range(3):
        top = values.astype(BF16)
        parts.append(top)
        values = values - top.astype(F32)
    return parts


def dot_thirds(onehot, values):
    width = values.shape[1]
    sums = jnp.dot(
        onehot.astype(BF16),
        jnp.concatenate(thirds(values), axis=1),
        preferred_element_type=F32,
    )
    return sums[:, :width] + sums[:, width : 2 * width] + sums[:, 2 * width :]


def contact_kernel(pair_count, select, spread, arrived, after, pushes):
    tiles = arrived.shape[0]
    points = [arrived[:, c, :] for c in range(3)]
    first = dot_thirds(select[1, :pair_count, :tiles], jnp.concatenate(points, axis=1))
    second = []
    for c in range(3):
        parts = [part.astype(F32) for part in thirds(points[c])]
        rest = LANES - 3 * tiles
        if rest:
            parts.append(jnp.zeros((rest, LANES), F32))
        turned = jnp.transpose(jnp.concatenate(parts, axis=0))[:, : 3 * tiles].astype(BF16)
        second.append(jnp.dot(turned, spread[...], preferred_element_type=F32))
    pushed = []
    for p in range(pair_count):
        gaps = [
            jnp.broadcast_to(first[p : p + 1, c * LANES : (c + 1) * LANES], (LANES, LANES))
            - second[c][:, p * LANES : (p + 1) * LANES]
            for c in range(3)
        ]
        dist = gaps[0] * gaps[0] + gaps[1] * gaps[1] + gaps[2] * gaps[2]
        weight = jnp.exp(dist * (-1.0 / REACH))
        pushed.append(
            jnp.concatenate(
                [jnp.sum(weight * gaps[c], axis=0, keepdims=True) for c in range(3)], axis=1
            )
        )
    total = PENALTY * dot_thirds(select[0, :tiles, :pair_count], jnp.concatenate(pushed, axis=0))
    for c in range(3):
        pushes[:, c, :] = total[:, c * LANES : (c + 1) * LANES]


def advance(internal, contact, ext, inv_mass, vel, disp, rows):
    for c in range(3):
        span = slice(c * rows, (c + 1) * rows)
        accel = inv_mass[...] * (ext[span, :] - internal[c] + contact[c])
        vel_c = vel[span, :] + DT * accel
        yield c, vel_c, disp[span, :] + DT * vel_c


def components(array):
    rows = array.shape[0] // 3
    return [array[c * rows : (c + 1) * rows, :] for c in range(3)]


def first_update_kernel(starting, *refs):
    refs = list(refs)
    own = refs[0]
    contact, lists, inv_mass, disp, vel, ext = refs[5:11]
    new_vel, new_disp, *sends = refs[11:]
    rows = disp.shape[0] // 3
    backs = returned_sums(in_place(refs[1:5], BESIDE), lists, rows)
    internal = [mine + more for mine, more in zip(components(own), backs)]
    if starting:
        *sends, ext_rows = sends
        spread_rows(vel, new_vel, 3)
        spread_rows(ext, ext_rows, 3)
        vel, ext = new_vel, ext_rows
    sums = components(contact)
    steps = advance(internal, sums, ext, inv_mass, vel, disp, rows)
    for c, vel_c, disp_c in steps:
        span = slice(c * rows, (c + 1) * rows)
        new_vel[span, :] = vel_c
        new_disp[span, :] = disp_c
    gather_halo(new_disp, rows, lists, sends)


def update_kernel(case, *refs):
    own = refs[0]
    lists, ext, inv_mass, vel, disp, contact = refs[5:11]
    rows = disp.shape[0] // 3
    sums = returned_sums(in_place(refs[1:5], ALONE), lists, rows)
    internal = [mine + more for mine, more in zip(components(own), sums)]
    steps = advance(internal, components(contact), ext, inv_mass, vel, disp, rows)
    if case == "final":
        new_vel, new_disp = refs[11:]
        for c, vel_c, disp_c in steps:
            for h in range(rows):
                new_vel[c : c + 1, h * LANES : (h + 1) * LANES] = vel_c[h : h + 1, :]
                new_disp[c : c + 1, h * LANES : (h + 1) * LANES] = disp_c[h : h + 1, :]
        return
    if case == "last":
        coords, inverse, new_vel, new_disp, outgoing = refs[11:]
    else:
        new_vel, new_disp, *sends = refs[11:]
    for c, vel_c, disp_c in steps:
        new_vel[c * rows : (c + 1) * rows, :] = vel_c
        new_disp[c * rows : (c + 1) * rows, :] = disp_c
    if case == "last":

        def position_row(c, h):
            mine = coords[c : c + 1, h * LANES : (h + 1) * LANES]
            return mine + new_disp[c * rows + h : c * rows + h + 1, :]

        gather_slots(position_row, rows, inverse, outgoing)
    else:
        gather_halo(new_disp, rows, lists, sends)


def vmem(count):
    return [pl.BlockSpec(memory_space=pltpu.VMEM)] * count


def shape(*dims):
    return jax.ShapeDtypeStruct(dims, F32)


def call(kernel, inputs, outputs, name, smem=(), far=(), scratch=(), vmem_bytes=VMEM_BYTES):
    specs = [
        pl.BlockSpec(
            memory_space=pltpu.SMEM if i in smem else pl.ANY if i in far else pltpu.VMEM
        )
        for i in range(len(inputs))
    ]
    return pl.pallas_call(
        kernel,
        out_shape=tuple(outputs),
        in_specs=specs,
        out_specs=tuple(vmem(len(outputs))),
        scratch_shapes=list(scratch),
        compiler_params=pltpu.CompilerParams(vmem_limit_bytes=vmem_bytes),
        name=name,
    )(*inputs)


def partners():
    px, py = lax.axis_size("px"), lax.axis_size("py")
    number = lambda i, j: i * py + j
    swaps = [[] for _ in range(4)]
    for i in range(px):
        for j in range(py):
            me = number(i, j)
            swaps[0].append((me, number(i ^ 1, j)))
            other = i - 1 if i % 2 == 0 else i + 1
            swaps[1].append((me, number(other, j) if 0 <= other < px else number(i, j ^ 1)))
            swaps[2].append((me, number(i, j ^ 1)))
            other = j - 1 if j % 2 == 0 else j + 1
            swaps[3].append((me, number(i, other % py)))
    return swaps


def exchange(blocks, order):
    swaps = partners()
    return [lax.ppermute(blocks[n], ("px", "py"), swaps[n]) for n in order]


def swap(slots, devices, capacity):
    axes = ("px", "py")
    if capacity == LANES:
        return lax.all_to_all(slots, axes, 0, 0, tiled=True)
    ratio = LANES // capacity
    parts = jnp.transpose(slots.reshape(-1, 3, ratio, capacity), (0, 2, 1, 3)).reshape(
        devices, 3, capacity
    )
    moved = lax.all_to_all(parts, axes, 0, 0, tiled=True)
    return jnp.transpose(moved.reshape(-1, ratio, 3, capacity), (0, 2, 1, 3)).reshape(
        -1, 3, LANES
    )


def body(
    coords,
    displacement,
    velocity,
    inv_mass,
    ext_force,
    thickness,
    stiffness,
    elem_nodes,
    block_class,
    halo_lists,
    contact_nodes,
    contact_bucket,
    tile_pairs,
):
    rows = coords.shape[1] // LANES
    quarter = halo_lists.shape[1] // LANES
    elem_rows = elem_nodes.shape[1] // LANES
    devices = lax.axis_size("px") * lax.axis_size("py")
    capacity = 2 * contact_nodes.shape[0] // devices
    slot_rows = devices * capacity // LANES
    inv_mass = inv_mass.reshape(rows, LANES)
    thickness = thickness.reshape(elem_rows, LANES)
    nodal = shape(3 * rows, LANES)
    sent = [shape(3 * quarter, LANES)] * 4
    slots = shape(slot_rows, 3, LANES)

    counts = (lax.axis_size("px"), lax.axis_size("py"))
    corner_values = shape(12 * elem_rows, LANES)

    sources = [
        coords,
        displacement,
        contact_bucket.reshape(-1, LANES),
        contact_nodes.reshape(-1, LANES),
    ]
    inverse, outgoing = call(
        functools.partial(slots_kernel, devices, capacity),
        sources,
        [jax.ShapeDtypeStruct((slot_rows, LANES), I32), slots],
        "slots",
        far=range(4),
        scratch=[pltpu.VMEM(source.shape, source.dtype) for source in sources]
        + [pltpu.SemaphoreType.DMA((4,))],
        vmem_bytes=WHOLE_VMEM,
    )
    disp, lists, nodes, splat, *sends = call(
        functools.partial(prepare_kernel, counts),
        [displacement, halo_lists, elem_nodes, stiffness, inverse],
        [
            nodal,
            jax.ShapeDtypeStruct((4 * quarter, LANES), I32),
            jax.ShapeDtypeStruct((4 * elem_rows, LANES), I32),
            shape(144, LANES),
        ]
        + sent,
        "prepare",
        far=(4,),
    )
    pair_count = tile_pairs.shape[1]
    select, spread, slow = call(
        masks_kernel,
        [tile_pairs, block_class.reshape(1, -1), lists],
        [
            shape(2, LANES, LANES),
            jax.ShapeDtypeStruct((3 * slot_rows, pair_count * LANES), BF16),
            jax.ShapeDtypeStruct((elem_rows, LANES), I32),
        ],
        "masks",
        far=(2,),
    )
    vel = velocity
    for step_no in range(STEPS):
        for sub_no in range(SUBS):
            first = sub_no == 0
            last = sub_no == SUBS - 1
            final = last and step_no == STEPS - 1
            if first:
                arrived = swap(outgoing, devices, capacity)
                if step_no:
                    sends = call(sends_kernel, [disp, lists, outgoing], sent, "sends", far=(2,))
            recvs = exchange(sends, BESIDE if first else ALONE)
            (found,) = call(own_kernel, [disp, nodes], [corner_values], "own_corners")
            field = [found, *recvs, nodes, thickness, splat]
            if first:
                (held,) = call(
                    functools.partial(force_kernel, rows), field, [corner_values], "forces"
                )
                (pushes,) = call(
                    functools.partial(contact_kernel, pair_count),
                    [select, spread, arrived, held],
                    [slots],
                    "contact",
                    far=(3,),
                )
                returned = swap(pushes, devices, capacity)
                outs = call(
                    functools.partial(after_kernel, functools.partial(halo_sum_kernel, rows), 2),
                    [held, nodes, pushes],
                    sent,
                    "halo_sum",
                    far=(2,),
                )
                forces = held
            else:
                (forces,) = call(
                    functools.partial(later_force_kernel, rows),
                    field + [held, slow],
                    [corner_values],
                    "forces_later",
                )
                outs = call(
                    functools.partial(halo_sum_kernel, rows), [forces, nodes], sent, "halo_sum"
                )
            backs = exchange(outs, BESIDE if first else ALONE)
            (own,) = call(own_sum_kernel, [forces, nodes, outs[2]], [nodal], "own_sum", far=(2,))
            if first:
                (contact,) = call(
                    contact_sum_kernel, [returned, inverse], [nodal], "contact_sum"
                )
                inputs = [own, *backs, contact, lists, inv_mass, disp, vel]
                outputs = [nodal] * 2 + sent
                if step_no == 0:
                    inputs.append(ext_force)
                    outputs.append(nodal)
                else:
                    inputs.append(ext)
                vel, disp, *sends = call(
                    functools.partial(first_update_kernel, step_no == 0),
                    inputs,
                    outputs,
                    "first_update",
                )
                if step_no == 0:
                    *sends, ext = sends
                continue
            inputs = [own, *backs, lists, ext, inv_mass, vel, disp, contact]
            if final:
                vel, disp = call(
                    functools.partial(update_kernel, "final"),
                    inputs,
                    [shape(3, rows * LANES)] * 2,
                    "final_update",
                )
            elif last:
                vel, disp, outgoing = call(
                    functools.partial(update_kernel, "last"),
                    inputs + [coords, inverse],
                    [nodal] * 2 + [slots],
                    "last_update",
                )
            else:
                vel, disp, *sends = call(
                    functools.partial(update_kernel, "inner"),
                    inputs,
                    [nodal] * 2 + sent,
                    "update",
                )
    return (disp, vel)


def solution(mesh):
    placed = (
        P(None, ("px", "py")),
        P(None, ("px", "py")),
        P(None, ("px", "py")),
        P(("px", "py")),
        P(None, ("px", "py")),
        P(("px", "py")),
        P(),
        P(None, ("px", "py")),
        P(("px", "py")),
        P(None, ("px", "py")),
        P(("px", "py")),
        P(("px", "py"), None),
        P(None, ("px", "py")),
    )
    return jax.shard_map(
        body,
        mesh=mesh,
        in_specs=placed,
        out_specs=(P(None, ("px", "py")), P(None, ("px", "py"))),
        check_vma=False,
    )
```
